32 devices in a mesh: dp: 8 (over y, x, core), tensor: 4 (over z).
Axes of the slice: x: 2, y: 2, z: 4, core: 2. Of those that a mesh axis runs over, the one named last changes fastest.
Arguments:
- layer_in: bfloat16 [8192, 2048], P(('dp', 'tensor')), may hold values from -6 to 6
- cotangent: bfloat16 [8192, 2048], P(('dp', 'tensor')), may hold values from -6 to 6
- doc_ids: int32 [8192], P('dp'), may hold values from 0 to 3, as said below
- positions: int32 [8192], P('dp'), may hold values from 0 to 511, as said below
- attn_gain: float32 [2048], replicated, may hold values from 0.5 to 1.5
- w_query: bfloat16 [2048, 2048], P(None, 'tensor'), may hold values from -0.125 to 0.125
- w_key: bfloat16 [2048, 2048], P(None, 'tensor'), may hold values from -0.125 to 0.125
- w_value: bfloat16 [2048, 2048], P(None, 'tensor'), may hold values from -0.125 to 0.125
- w_out: bfloat16 [2048, 2048], P('tensor'), may hold values from -3 to 3
- ffn_gain: float32 [2048], replicated, may hold values from 0.5 to 1.5
- w_gate: bfloat16 [2048, 8192], P(None, 'tensor'), may hold values from -0.125 to 0.125
- w_up: bfloat16 [2048, 8192], P(None, 'tensor'), may hold values from -0.125 to 0.125
- w_down: bfloat16 [8192, 2048], P('tensor'), may hold values from -0.0625 to 0.0625
Outputs:
- layer_out: bfloat16 [8192, 2048], P(('dp', 'tensor'))
- in_grad: bfloat16 [8192, 2048], P(('dp', 'tensor'))
- attn_gain_grad: float32 [2048], replicated
- query_grad: float32 [2048, 2048], P(None, 'tensor')
- key_grad: float32 [2048, 2048], P(None, 'tensor')
- value_grad: float32 [2048, 2048], P(None, 'tensor')
- out_grad: float32 [2048, 2048], P('tensor')
- ffn_gain_grad: float32 [2048], replicated
- gate_grad: float32 [2048, 8192], P(None, 'tensor')
- up_grad: float32 [2048, 8192], P(None, 'tensor')
- down_grad: float32 [8192, 2048], P('tensor')
The draws below stay inside these ranges and needn't reach their ends.
Inputs may be any that keep to these rules, and one draw needn't show every extreme that they name: `doc_ids`: within each sequence of 1024 tokens the ids never fall, start at 0 and end at 3: 4 contiguous documents of ragged lengths, one of which holds exactly 512 tokens. `positions`: each token's offset from the first token of its document.
All inputs are finite; a program needn't handle non-finite values.
Results may differ from the reference program's by a relative error of at most 0.018.
Values may be sent and summed in bfloat16 or wider, within the bound.
No kernel may reach another device: no remote copies, remote signals or barrier semaphores. Data moves between devices by JAX's collectives and lax.ppermute only.
A program may use at most 320 MiB of HBM per device.

```python
import math
import jax
import jax.numpy as jnp
from jax import lax

D = 2048
HEADS = 16
HD = 128
FF = 8192
SEQ = 1024
DOCS = 4
TOKENS = 8192


def doc_layout(key):
    seq_count = TOKENS // SEQ
    seq_keys = jax.random.split(jax.random.fold_in(key, 7), seq_count)
    half = SEQ // 2

    def layout_one(one_key):
        cut_key, long_key = jax.random.split(one_key)
        shuffled = jax.random.permutation(cut_key, half - 1).astype(jnp.int32)
        cuts = jnp.sort(shuffled[:DOCS - 2] + 1).astype(jnp.int32)
        small_starts = jnp.concatenate([jnp.zeros((1,), jnp.int32), cuts])
        long_index = jax.random.randint(long_key, (), 0, DOCS).astype(jnp.int32)
        rank = jnp.arange(DOCS - 1, dtype=jnp.int32)
        moved = small_starts + jnp.where(rank >= long_index, half, 0).astype(jnp.int32)
        padded = jnp.concatenate([small_starts, jnp.full((1,), half, jnp.int32)])
        long_start = jnp.sum(jnp.where(jnp.arange(DOCS, dtype=jnp.int32) == long_index, padded, 0)).astype(jnp.int32)
        starts = jnp.concatenate([moved, long_start[None]])
        places = jnp.arange(SEQ, dtype=jnp.int32)
        begun = starts[None, :] <= places[:, None]
        numbers = (jnp.sum(begun.astype(jnp.int32), axis=1) - 1).astype(jnp.int32)
        latest = jnp.max(jnp.where(begun, starts[None, :], 0), axis=1).astype(jnp.int32)
        return (numbers, (places - latest).astype(jnp.int32))
    numbers, offsets = jax.vmap(layout_one)(seq_keys)
    return (numbers.reshape(-1), offsets.reshape(-1))


def draw_doc_ids(key, part):
    return doc_layout(key)[0]


def draw_positions(key, part):
    return doc_layout(key)[1]


def levels(stream_key, dims, cuts, low, high):
    factor_of, own = 1.0, jax.random.fold_in(stream_key, 6)
    for axis_at, blocks in cuts:
        heights = jnp.exp(jax.random.uniform(jax.random.fold_in(own, axis_at), (blocks,), jnp.float32, low / len(cuts), high / len(cuts)))
        factor_of = factor_of * jnp.repeat(heights, dims[axis_at] // blocks).reshape([-1 if axis == axis_at else 1 for axis in range(len(dims))])
    return factor_of


def bell_draw(own_key, shape, deviation, most, cuts=(), held_as=jnp.bfloat16):
    values = jax.random.normal(own_key, shape, jnp.float32) * deviation
    if len(cuts) > 0:
        values = levels(own_key, shape, cuts, -0.22, 0.18) * values
    return jnp.clip(values, min=-most, max=most).astype(held_as)


def setup_inputs(seed: int = 0) -> dict:
    splits = jax.random.split(jax.random.key(seed), 14)
    return {
        "layer_in": bell_draw(splits[0], (TOKENS, D), 1.0, 6.0, ((0, 32),)),
        "cotangent": bell_draw(splits[1], (TOKENS, D), 1.0, 6.0, ((0, 32),)),
        "doc_ids": draw_doc_ids(jax.random.fold_in(splits[13], 71), 0),
        "positions": draw_positions(jax.random.fold_in(splits[13], 71), 0),
        "attn_gain": jnp.clip(1.0 + 0.1 * jax.random.normal(splits[4], (D,), jnp.float32), 0.5, 1.5),
        "w_query": bell_draw(splits[5], (D, D), D ** -0.5, 0.125, ((1, 4),)),
        "w_key": bell_draw(splits[6], (D, D), D ** -0.5, 0.125, ((1, 4),)),
        "w_value": bell_draw(splits[7], (D, D), D ** -0.5, 0.125, ((1, 4),)),
        "w_out": bell_draw(splits[8], (D, D), 4 ** -0.5, 3.0, ((0, 4),)),
        "ffn_gain": jnp.clip(1.0 + 0.1 * jax.random.normal(splits[9], (D,), jnp.float32), 0.5, 1.5),
        "w_gate": bell_draw(splits[10], (D, FF), D ** -0.5, 0.125, ((1, 4),)),
        "w_up": bell_draw(splits[11], (D, FF), D ** -0.5, 0.125, ((1, 4),)),
        "w_down": bell_draw(splits[12], (FF, D), FF ** -0.5, 0.0625, ((0, 4),)),
    }


EPS = 1e-05
ROPE_BASE = 500000.0
HIGH = lax.Precision.HIGHEST

@jax.custom_vjp
def low(v):
    return lax.optimization_barrier(v.astype(jnp.bfloat16)).astype(jnp.float32)

@jax.custom_vjp
def low_back(v):
    return v

def low_keep(v):
    return (low(v), None)

def low_pass(kept, grad):
    return (grad,)

def back_keep(v):
    return (v, None)

def back_low(kept, grad):
    return (low(grad),)
low.defvjp(low_keep, low_pass)
low_back.defvjp(back_keep, back_low)

def rms_scale(values, gain):
    return values * lax.rsqrt(lax.optimization_barrier(jnp.mean(values * values, axis=-1, keepdims=True)) + EPS) * gain

def rope_turn(values, positions):
    half = HD // 2
    freqs = ROPE_BASE ** (-(jnp.arange(half).astype(jnp.float32) * 2.0) / HD)
    angles = positions.astype(jnp.float32)[:, None] * freqs[None, :]
    cosine = jnp.cos(angles)[:, None, :]
    sine = jnp.sin(angles)[:, None, :]
    heads = values.reshape(values.shape[0], -1, HD)
    lower = heads[..., :half]
    upper = heads[..., half:]
    turned = jnp.concatenate([lower * cosine - upper * sine, upper * cosine + lower * sine], axis=-1)
    return turned.reshape(values.shape)

def attend_one(pieces):
    query_s, key_s, value_s, ids_s = pieces
    heads_q = query_s.reshape(SEQ, HEADS, HD)
    heads_k = key_s.reshape(SEQ, HEADS, HD)
    heads_v = value_s.reshape(SEQ, HEADS, HD)
    scores = jnp.einsum('qhd,khd->hqk', heads_q, heads_k, precision=HIGH) / math.sqrt(HD) - math.log(SEQ)
    scores = low_back(scores)
    places = jnp.arange(SEQ)
    allowed = (ids_s[:, None] == ids_s[None, :]) & (places[:, None] >= places[None, :])
    probs = low(jnp.where(allowed[None], jax.nn.sigmoid(scores), 0.0))
    mixed = jnp.einsum('hqk,khd->qhd', probs, heads_v, precision=HIGH).reshape(SEQ, HEADS * HD)
    return low(low_back(mixed))

def forward(layer_f, doc_ids, positions, attn_gain, w_query, w_key, w_value, w_out, ffn_gain, w_gate, w_up, w_down):
    normed = low(rms_scale(layer_f, attn_gain))
    query_pre = low_back(jnp.dot(normed, w_query, precision=HIGH))
    key_pre = low_back(jnp.dot(normed, w_key, precision=HIGH))
    value = low(low_back(jnp.dot(normed, w_value, precision=HIGH)))
    query = low(rope_turn(query_pre, positions))
    key_rot = low(rope_turn(key_pre, positions))
    seq_count = layer_f.shape[0] // SEQ
    mixed = lax.map(jax.checkpoint(attend_one), (query.reshape(seq_count, SEQ, D), key_rot.reshape(seq_count, SEQ, D), value.reshape(seq_count, SEQ, D), doc_ids.reshape(seq_count, SEQ)))
    mixed = mixed.reshape(seq_count * SEQ, D)
    attn_branch = low_back(jnp.dot(mixed, w_out, precision=HIGH))
    resid = layer_f + attn_branch
    normed2 = low(rms_scale(resid, ffn_gain))
    gate = low_back(jnp.dot(normed2, w_gate, precision=HIGH))
    up_proj = low_back(jnp.dot(normed2, w_up, precision=HIGH))
    inner = low(jax.nn.silu(gate) * up_proj)
    return resid + jnp.dot(inner, w_down, precision=HIGH)

def reference(layer_in, cotangent, doc_ids, positions, attn_gain, w_query, w_key, w_value, w_out, ffn_gain, w_gate, w_up, w_down):
    weights = (attn_gain.astype(jnp.float32), w_query.astype(jnp.float32), w_key.astype(jnp.float32), w_value.astype(jnp.float32), w_out.astype(jnp.float32), ffn_gain.astype(jnp.float32), w_gate.astype(jnp.float32), w_up.astype(jnp.float32), w_down.astype(jnp.float32))
    layer_f = layer_in.astype(jnp.float32)

    def wrapped(layer_v, *params):
        return forward(layer_v, doc_ids, positions, *params)
    result, pullback = jax.vjp(wrapped, layer_f, *weights)
    grads = pullback(cotangent.astype(jnp.float32))
    return (result.astype(jnp.bfloat16), grads[0].astype(jnp.bfloat16), grads[1], grads[2], grads[3], grads[4], grads[5], grads[6], grads[7], grads[8], grads[9])
```

```python
import functools
import math

import jax
import jax.numpy as jnp
from jax import lax
from jax.experimental import pallas as pl
from jax.experimental.pallas import tpu as pltpu
from jax.sharding import PartitionSpec as P

HD = 128
EPS = 1e-05
ROPE_BASE = 500000.0
BF = jnp.bfloat16
F32 = jnp.float32
MIB = 1 << 20


def dot(left, right):
    return lax.dot_general(left, right, (((1,), (0,)), ((), ())), preferred_element_type=F32)


def dot_nt(left, right):
    return lax.dot_general(left, right, (((1,), (1,)), ((), ())), preferred_element_type=F32)


def dot_tn(left, right):
    return lax.dot_general(left, right, (((0,), (0,)), ((), ())), preferred_element_type=F32)


def sigmoid(v):
    return 1.0 / (1.0 + jnp.exp(-v))


def rms_scale(values, gain):
    return values * lax.rsqrt(jnp.mean(values * values, axis=-1, keepdims=True) + EPS) * gain


def call(body, *, name, grid, scalars, in_specs, out_specs, out_shape, scratch=(), aliases=None,
         flops=0, nbytes=0, trans=0, vmem=40):
    return pl.pallas_call(
        body,
        grid_spec=pltpu.PrefetchScalarGridSpec(
            num_scalar_prefetch=scalars,
            grid=grid,
            in_specs=in_specs,
            out_specs=out_specs,
            scratch_shapes=list(scratch),
        ),
        out_shape=out_shape,
        input_output_aliases=aliases or {},
        compiler_params=pltpu.CompilerParams(vmem_limit_bytes=vmem * MIB),
        cost_estimate=pl.CostEstimate(flops=flops, bytes_accessed=nbytes, transcendentals=trans),
        name=name,
    )


ANY = pl.BlockSpec(memory_space=pl.ANY)


def xor_pairs(size, mask):
    return [(i, i ^ mask) for i in range(size)]


def tie_body(*refs):
    pass


def tie(values, others):
    return call(
        tie_body,
        name="tie",
        grid=(1,),
        scalars=0,
        in_specs=[ANY] * (len(values) + len(others)),
        out_specs=[ANY] * len(values),
        out_shape=[jax.ShapeDtypeStruct(v.shape, v.dtype) for v in values],
        aliases={i: i for i in range(len(values))},
        vmem=1,
    )(*values, *others)


def after(value, *others):
    return tie([value], others)[0]


class LineGather:
    def __init__(self, own, size, place):
        self.size, self.place = size, place
        self.ups, self.downs = [own], [own]

    def step(self, *others):
        k, size = len(self.ups), self.size
        if others:
            self.ups[-1], self.downs[-1] = tie([self.ups[-1], self.downs[-1]], others)
        up, down = self.ups[-1], self.downs[-1]
        self.ups.append(lax.ppermute(up, "tensor", [(i, i + 1) for i in range(k - 1, size - 1)]))
        self.downs.append(lax.ppermute(down, "tensor", [(i + 1, i) for i in range(0, size - k)]))

    def slot(self, j):
        groups = {}
        for at in range(self.size):
            groups.setdefault((at ^ j) - at, []).append(at)
        value = None
        for off, places in groups.items():
            arr = self.downs[off] if off >= 0 else self.ups[-off]
            if value is None:
                value = arr
            else:
                here = functools.reduce(jnp.logical_or, [self.place == at for at in places])
                value = jnp.where(here, arr, value)
        return value


def exchange(pieces, size):
    return [pieces[0]] + [
        lax.ppermute(pieces[j], "tensor", xor_pairs(size, j)) for j in range(1, size)
    ]


def rows_at(values, block, rows):
    return lax.dynamic_slice_in_dim(values, block * rows, rows, axis=0)


def cols_at(values, block, cols):
    return lax.dynamic_slice_in_dim(values, block * cols, cols, axis=1)


def join_body(places, *refs):
    pieces, out = refs[:-1], refs[-1]
    step = pl.program_id(0) * pl.num_programs(1) + pl.program_id(1)
    for k, piece in enumerate(pieces):

        @pl.when(step == k)
        def _():
            out[...] = piece[...]


def finish_body(core, mine, other, *outs):
    at = 0
    for source, turn in ((mine, 0), (other, 1)):

        @pl.when(pl.program_id(0) == turn)
        def _():
            at = 0
            for out in outs:
                width = out.shape[1]
                out[...] = source[:, at : at + width].astype(F32)
                at += width


class Reducer:
    def __init__(self, count):
        self.count = count
        self.bits = count.bit_length() - 1
        self.index = lax.axis_index("dp")
        self.core = self.bit(0)

    def bit(self, b):
        return (self.index >> b) & 1

    def split(self, left):
        half = left.shape[1] // 2
        return (cols_at(left, 1 - self.core, half), cols_at(left, self.core, half))

    def swap(self, value, b):
        return lax.ppermute(value, "dp", xor_pairs(self.count, 1 << b))

    def give(self, halves, right):
        return self.swap(dot_tn(halves[0], right).astype(BF), 0)

    def keep(self, halves, right, got):
        return (dot_tn(halves[1], right) + got.astype(F32)).astype(BF)

    def open(self, chip):
        cols = chip.shape[1]
        halves = [lax.slice_in_dim(chip, at * cols // 2, (at + 1) * cols // 2, axis=1) for at in (0, 1)]
        orders = [list(range(1, self.bits)), list(range(self.bits - 1, 0, -1))]
        return [[[half], order, order, jnp.int32(0)] for half, order in zip(halves, orders)]

    def add(self, state):
        out = []
        for (part,), order, left, place in state:
            half, mine = part.shape[0] // 2, self.bit(left[0])
            got = self.swap(rows_at(part, 1 - mine, half), left[0])
            part = (rows_at(part, mine, half).astype(F32) + got.astype(F32)).astype(BF)
            out.append([[part], order, left[1:], place * 2 + mine])
        return out

    def spread(self, state):
        out = []
        for held, order, left, place in state:
            step = order[len(order) - 1 - (len(held).bit_length() - 1)]
            out.append([held + [self.swap(p, step) for p in held], order, left, place])
        return out

    def wait(self, state, *others):
        flat = [p for held, *_ in state for p in held]
        got = list(tie(flat, others))
        return [[[got.pop(0) for _ in held], order, left, place] for held, order, left, place in state]

    def pieces(self, state):
        return [p for held, *_ in state for p in held]

    def close(self, state, widths):
        pieces = self.pieces(state)
        places = [place for *_, place in state]
        brows, bcols = pieces[0].shape
        blocks = len(pieces) // 2
        rows, cols = brows * blocks, bcols * 2
        half = call(
            join_body,
            name="join",
            grid=(2, blocks),
            scalars=1,
            in_specs=[pl.BlockSpec((brows, bcols), lambda h, k, s: (0, 0))] * len(pieces),
            out_specs=pl.BlockSpec((brows, bcols), lambda h, k, s: (k ^ s[h], h)),
            out_shape=jax.ShapeDtypeStruct((rows, cols), BF),
            nbytes=rows * cols * 4,
            vmem=24,
        )(jnp.stack(places), *pieces)
        other = self.swap(half, 0)
        crows = min(256, rows)
        nblk = rows // crows
        return call(
            finish_body,
            name="finish",
            grid=(2, nblk),
            scalars=1,
            in_specs=[
                pl.BlockSpec((crows, cols), lambda g, b, s: (jnp.where(g == 0, b, nblk - 1), 0)),
                pl.BlockSpec((crows, cols), lambda g, b, s: (jnp.where(g == 0, 0, b), 0)),
            ],
            out_specs=[
                pl.BlockSpec((crows, w), lambda g, b, s: ((g ^ s[0]) * nblk + b, 0)) for w in widths
            ],
            out_shape=[jax.ShapeDtypeStruct((2 * rows, w), F32) for w in widths],
            nbytes=rows * cols * 12,
            vmem=24,
        )(self.core.reshape(1), half, other)


def gain_total(part, dp, tensor):
    value = part.reshape(-1, 128)
    for name, size in (("dp", dp), ("tensor", tensor)):
        step = 1
        while step < size:
            value = value + lax.ppermute(value, name, xor_pairs(size, step))
            step *= 2
    return value.reshape(-1)


def qkv_body(*refs):
    chunk, rows, wq, wk, wv, cos, sin = refs[:7]
    q_out, k_out, v_out, rows_out = refs[-4:]
    x = rows[...]
    cosine, sine = cos[...], sin[...]

    def turned(pre):
        out = []
        for h in range(pre.shape[1] // HD):
            one = pre[:, h * HD : (h + 1) * HD]
            out.append(one * cosine + pltpu.roll(one, HD // 2, 1) * sine)
        return jnp.concatenate(out, axis=1)

    q_out[...] = turned(dot(x, wq[...])).astype(BF)
    k_out[...] = turned(dot(x, wk[...])).astype(BF)
    v_out[...] = dot(x, wv[...]).astype(BF)
    rows_out[...] = x


def qkv_slot(chunk, rows, w_query, w_key, w_value, cos, sin, held, count):
    t, d = rows.shape
    width = w_query.shape[1]
    bn = min(256, width)
    wspec = pl.BlockSpec((d, bn), lambda i, s: (0, i))
    tspec = pl.BlockSpec((t, HD), lambda i, s: (s[0], 0))
    return call(
        qkv_body,
        name="qkv",
        grid=(width // bn,),
        scalars=1,
        in_specs=[pl.BlockSpec((t, d), lambda i, s: (0, 0)), wspec, wspec, wspec, tspec, tspec]
        + [ANY] * len(held),
        out_specs=[pl.BlockSpec((t, bn), lambda i, s: (s[0], i))] * 3
        + [pl.BlockSpec((t, d), lambda i, s: (s[0], 0))],
        out_shape=[jax.ShapeDtypeStruct((count * t, width), BF)] * 3
        + [jax.ShapeDtypeStruct((count * t, d), BF)],
        aliases={7 + i: i for i in range(len(held))},
        flops=6 * t * d * width,
        nbytes=2 * (3 * d * width + 2 * t * d + 3 * t * width),
        vmem=32,
    )(chunk, rows, w_query, w_key, w_value, cos, sin, *held)


def attend_consts(seq_len):
    to_log2 = math.log2(math.e)
    return (to_log2 / math.sqrt(HD), math.log2(seq_len))


def attend_body(docs, q_ref, k_ref, v_ref, ids_col, ids_row, mix, acc, *, block):
    seq_len = q_ref.shape[0]
    scale, shift = attend_consts(seq_len)
    causal = lax.broadcasted_iota(jnp.int32, (block, block), 0) >= lax.broadcasted_iota(
        jnp.int32, (block, block), 1
    )

    def term(i, j):
        q = q_ref[i * block : (i + 1) * block, :]
        k = k_ref[j * block : (j + 1) * block, :]
        sig = 1.0 / (1.0 + jnp.exp2(shift - dot_nt(q, k) * scale))
        same = ids_col[i * block : (i + 1) * block, :] == ids_row[:, j * block : (j + 1) * block]
        allowed = same & causal if i == j else same
        probs = jnp.where(allowed, sig, 0.0).astype(BF)
        return dot(probs, v_ref[j * block : (j + 1) * block, :])

    for i in range(seq_len // block):
        acc[...] = term(i, i)
        for j in range(i):

            @pl.when(docs[(j + 1) * block - 1] == docs[i * block])
            def _():
                acc[...] += term(i, j)

        mix[i * block : (i + 1) * block, :] = acc[...].astype(BF)


def attend(docs, q, k, v):
    seq_len, width = q.shape
    block = 256
    head = pl.BlockSpec((seq_len, HD), lambda h, s: (0, h))
    return call(
        functools.partial(attend_body, block=block),
        name="attend",
        grid=(width // HD,),
        scalars=1,
        in_specs=[
            head,
            head,
            head,
            pl.BlockSpec((seq_len, 1), lambda h, s: (0, 0)),
            pl.BlockSpec((1, seq_len), lambda h, s: (0, 0)),
        ],
        out_specs=head,
        out_shape=jax.ShapeDtypeStruct((seq_len, width), BF),
        scratch=[pltpu.VMEM((block, HD), F32)],
        flops=3 * seq_len * seq_len * width,
        nbytes=8 * seq_len * width,
        trans=seq_len * seq_len * width // HD,
        vmem=24,
    )(docs, q, k, v, docs.reshape(-1, 1), docs.reshape(1, -1))


def attend_back_body(*refs, block, count):
    docs, chunks, q_ref, k_ref, v_ref = refs[:5]
    grads = refs[5 : 5 + count]
    ids_col, ids_row, cos, sin, out, dmix, dq, dk, dv = refs[5 + count :]
    seq_len = q_ref.shape[0]
    t = seq_len // count
    scale, shift = attend_consts(seq_len)
    for c in range(count):
        dmix[pl.ds(pl.multiple_of(chunks[c] * t, t), t), :] = grads[c][...]
    causal = lax.broadcasted_iota(jnp.int32, (block, block), 0) <= lax.broadcasted_iota(
        jnp.int32, (block, block), 1
    )

    def at(i):
        return slice(i * block, (i + 1) * block)

    def term(i, j):
        q, k, v, d = q_ref[at(i), :], k_ref[at(j), :], v_ref[at(j), :], dmix[at(i), :]
        sig = 1.0 / (1.0 + jnp.exp2(shift - dot_nt(k, q) * scale))
        same = ids_col[at(j), :] == ids_row[:, at(i)]
        allowed = same & causal if i == j else same
        probs = jnp.where(allowed, sig, 0.0)
        d_scores = (dot_nt(v, d) * probs * (1.0 - probs)).astype(BF)
        return dot_tn(d_scores, k), dot(d_scores, q), dot(probs.astype(BF), d)

    for i in range(seq_len // block):
        dq[at(i), :], dk[at(i), :], dv[at(i), :] = term(i, i)
    for i in range(seq_len // block):
        for j in range(i):

            @pl.when(docs[(j + 1) * block - 1] == docs[i * block])
            def _():
                a, b, c = term(i, j)
                dq[at(i), :] += a
                dk[at(j), :] += b
                dv[at(j), :] += c

    cosine, sine = cos[...], sin[...]

    def turned_back(v):
        v = v * (1.0 / math.sqrt(HD))
        return (v * cosine - pltpu.roll(v, HD // 2, 1) * sine).astype(BF)

    width = out.shape[1] // 3
    at_head = pl.program_id(0) * HD
    for part, value in enumerate((turned_back(dq[...]), turned_back(dk[...]), dv[...].astype(BF))):
        out[:, pl.ds(pl.multiple_of(at_head + part * width, HD), HD)] = value


def attend_back(docs, chunks, q, k, v, grads, cos, sin):
    seq_len, width = q.shape
    block, count = 256, len(grads)
    head = pl.BlockSpec((seq_len, HD), lambda h, s, c: (0, h))
    whole = lambda r, c: pl.BlockSpec((r, c), lambda h, s, e: (0, 0))
    return call(
        functools.partial(attend_back_body, block=block, count=count),
        name="attend_back",
        grid=(width // HD,),
        scalars=2,
        in_specs=[head, head, head]
        + [pl.BlockSpec((seq_len // count, HD), lambda h, s, c: (0, h))] * count
        + [whole(seq_len, 1), whole(1, seq_len), whole(seq_len, HD), whole(seq_len, HD)],
        out_specs=whole(seq_len, 3 * width),
        out_shape=jax.ShapeDtypeStruct((seq_len, 3 * width), BF),
        scratch=[pltpu.VMEM((seq_len, HD), BF)] + [pltpu.VMEM((seq_len, HD), F32)] * 3,
        flops=7 * seq_len * seq_len * width,
        nbytes=14 * seq_len * width,
        trans=seq_len * seq_len * width // HD,
        vmem=40,
    )(docs, chunks, q, k, v, *grads, docs.reshape(-1, 1), docs.reshape(1, -1), cos, sin)


def project_body(*refs, count):
    chunks = refs[0]
    mixes = refs[1 : 1 + count]
    w_ref, x_ref, gain, resid, normed, acc = refs[1 + count :]
    for c in range(count):

        @pl.when(pl.program_id(0) == c)
        def _():
            term = dot(mixes[c][...], w_ref[...])
            acc[...] = term if c == 0 else acc[...] + term

    @pl.when(pl.program_id(0) == count - 1)
    def _():
        total = x_ref[...].astype(F32) + acc[...]
        resid[...] = total
        normed[...] = rms_scale(total, gain[...]).astype(BF)


def project(chunks, mixes, w_out, x, gain):
    t, d = x.shape
    count = len(mixes)
    width = mixes[0].shape[1]
    whole = lambda r, c: pl.BlockSpec((r, c), lambda i, s: (0, 0))
    return call(
        functools.partial(project_body, count=count),
        name="project",
        grid=(count,),
        scalars=1,
        in_specs=[whole(t, width)] * count
        + [pl.BlockSpec((width, d), lambda i, s: (s[i], 0)), whole(t, d), whole(1, d)],
        out_specs=[whole(t, d)] * 2,
        out_shape=[jax.ShapeDtypeStruct((t, d), F32), jax.ShapeDtypeStruct((t, d), BF)],
        scratch=[pltpu.VMEM((t, d), F32)],
        flops=2 * t * d * d,
        nbytes=2 * d * d + 10 * t * d,
        vmem=32,
    )(chunks, *mixes, w_out, x, gain.reshape(1, -1))


def ffn_body(*refs):
    chunk, rows, cot, wg, wu, wd = refs[:6]
    inner, d_gate, d_up, rows_out, d_rows, down, token, acc_d, acc_o = refs[-9:]
    step, last = pl.program_id(0), pl.num_programs(0) - 1
    x = rows[...]
    gate = dot(x, wg[...])
    up = dot(x, wu[...])
    sig = sigmoid(gate)
    silu = gate * sig
    inner_b = (silu * up).astype(BF)
    inner[...] = inner_b
    d_inner = dot_nt(cot[...], wd[...])
    dg = (d_inner * up * (sig * (1.0 + gate * (1.0 - sig)))).astype(BF)
    du = (d_inner * silu).astype(BF)
    d_gate[...] = dg
    d_up[...] = du
    term_o = dot(inner_b, wd[...])
    term_d = dot_nt(dg, wg[...]) + dot_nt(du, wu[...])

    @pl.when(step == 0)
    def _():
        acc_o[...] = term_o
        acc_d[...] = term_d
        rows_out[...] = x

    @pl.when(step > 0)
    def _():
        acc_o[...] += term_o
        acc_d[...] += term_d

    @pl.when(step == last)
    def _():
        d_rows[...] = acc_d[...].astype(BF)
        down[...] = acc_o[...].astype(BF)
        token[...] = jnp.zeros_like(token)


def ffn_slot(chunk, rows, cot, w_gate, w_up, w_down, held, count):
    t, d = rows.shape
    hidden = w_gate.shape[1]
    bh = min(512, hidden)
    wcol = pl.BlockSpec((d, bh), lambda i, s: (0, i))
    part = pl.BlockSpec((t, bh), lambda i, s: (s[0], i))
    line = pl.BlockSpec((t, d), lambda i, s: (s[0], 0))
    return call(
        ffn_body,
        name="ffn",
        grid=(hidden // bh,),
        scalars=1,
        in_specs=[
            pl.BlockSpec((t, d), lambda i, s: (0, 0)),
            line,
            wcol,
            wcol,
            pl.BlockSpec((bh, d), lambda i, s: (i, 0)),
        ]
        + [ANY] * len(held),
        out_specs=[part] * 3 + [line] * 3 + [pl.BlockSpec((8, 128), lambda i, s: (0, 0))],
        out_shape=[jax.ShapeDtypeStruct((count * t, hidden), BF)] * 3
        + [jax.ShapeDtypeStruct((count * t, d), BF)] * 3
        + [jax.ShapeDtypeStruct((8, 128), F32)],
        scratch=[pltpu.VMEM((t, d), F32)] * 2,
        aliases={6 + i: i for i in range(len(held))},
        flops=14 * t * d * hidden,
        nbytes=2 * (3 * d * hidden + 5 * t * d + 3 * t * hidden),
        trans=2 * t * hidden,
        vmem=44,
    )(chunk, rows, cot, w_gate, w_up, w_down, *held)


def local(
    layer_in,
    cotangent,
    doc_ids,
    positions,
    attn_gain,
    w_query,
    w_key,
    w_value,
    w_out,
    ffn_gain,
    w_gate,
    w_up,
    w_down,
    *,
    dp,
    tensor,
):
    t, d = layer_in.shape
    width = w_query.shape[1]
    place = lax.axis_index("tensor")
    chunks = jnp.stack([place ^ j for j in range(tensor)]).astype(jnp.int32)
    chunk = [chunks[j : j + 1] for j in range(tensor)]
    reducer = Reducer(dp)

    share = w_out.shape[0] // dp
    w_out_all = lax.all_gather(
        rows_at(w_out, reducer.index, share), ("tensor", "dp"), axis=0, tiled=True
    )
    cot_all = lax.all_gather(cotangent, "tensor", axis=0, tiled=True)

    half = HD // 2
    freqs = ROPE_BASE ** (-(jnp.arange(half).astype(F32) * 2.0) / HD)
    angles = positions.astype(F32)[:, None] * freqs[None, :]
    cosine, sine = jnp.cos(angles), jnp.sin(angles)
    cos = jnp.concatenate([cosine, cosine], axis=1)
    sin = jnp.concatenate([-sine, sine], axis=1)

    own_in = layer_in.astype(F32)
    line = LineGather(rms_scale(own_in, attn_gain).astype(BF), tensor, place)
    held = []
    for j in range(tensor):
        if j + 1 < tensor:
            line.step()
        held = qkv_slot(chunk[j], line.slot(j), w_query, w_key, w_value, cos, sin, held, tensor)
    query, key, value, normed = held

    mixed = attend(doc_ids, query, key, value)
    mixes = exchange([rows_at(mixed, place ^ j, t) for j in range(tensor)], tensor)
    resid, normed2_own = project(chunks, mixes, w_out_all, layer_in, ffn_gain)

    line = LineGather(normed2_own, tensor, place)
    line.step()
    held, token = [], None
    for j in range(tensor):
        if 0 < j < tensor - 1:
            line.step(token)
        *held, token = ffn_slot(chunk[j], line.slot(j), cot_all, w_gate, w_up, w_down, held, tensor)
    inner, d_gate, d_up, normed2, d_normed2_part, down_part = held

    d_normed2 = lax.psum_scatter(d_normed2_part, "tensor", scatter_dimension=0, tiled=True)

    inner_halves = reducer.split(inner)
    normed2_halves = reducer.split(normed2)
    down_got = reducer.give(inner_halves, cot_all)
    gate_got = reducer.give(normed2_halves, d_gate)
    down_red = reducer.open(reducer.keep(inner_halves, cot_all, down_got))
    up_got = reducer.give(normed2_halves, d_up)
    gate_red = reducer.open(reducer.keep(normed2_halves, d_gate, gate_got))
    up_red = reducer.open(reducer.keep(normed2_halves, d_up, up_got))
    turns = range(1, reducer.bits)
    for _ in turns:
        down_red = reducer.add(down_red)
    gate_red = reducer.add(gate_red)
    d_normed2 = after(
        d_normed2, *reducer.pieces(down_red), *reducer.pieces(gate_red), *reducer.pieces(up_red)
    )
    down_part = after(down_part, *reducer.pieces(up_red))
    down_sum = lax.psum_scatter(down_part, "tensor", scatter_dimension=0, tiled=True)
    layer_out = (resid + down_sum.astype(F32)).astype(BF)

    norm_out, norm_pull = jax.vjp(rms_scale, resid, ffn_gain)
    d_resid_part, ffn_gain_part = norm_pull(d_normed2.astype(F32))
    d_resid = cotangent.astype(F32) + d_resid_part
    d_resid_low = d_resid.astype(BF)
    d_mix_own = dot_nt(d_resid_low, w_out_all).astype(BF)
    d_mixes = exchange([cols_at(d_mix_own, place ^ j, width) for j in range(tensor)], tensor)

    up_red = reducer.add(up_red)
    for _ in turns[1:]:
        gate_red = reducer.add(gate_red)
    down_red = reducer.spread(down_red)
    d_mixes = tie(
        d_mixes, [p for red in (up_red, gate_red, down_red) for p in reducer.pieces(red)]
    )
    d_qkv = attend_back(doc_ids, chunks, query, key, value, d_mixes, cos, sin)

    line = LineGather(after(d_resid_low, d_mixes[-1]), tensor, place)
    line.step()
    w_qkv = jnp.concatenate([w_query, w_key, w_value], axis=1)
    d_normed = lax.psum_scatter(
        dot_nt(d_qkv, w_qkv).astype(BF), "tensor", scatter_dimension=0, tiled=True
    )
    normed_halves = reducer.split(normed)
    qkv_got = reducer.give(normed_halves, d_qkv)
    qkv_red = reducer.open(reducer.keep(normed_halves, d_qkv, qkv_got))
    for _ in turns[1:]:
        up_red = reducer.add(up_red)
    for _ in turns[1:]:
        down_red = reducer.spread(down_red)
    gate_red = reducer.spread(gate_red)
    for _ in range(2, tensor):
        line.step()
    (down_grad,) = reducer.close(down_red, [d])
    qkv_red = reducer.add(qkv_red)
    hidden = w_gate.shape[1]
    for _ in turns[1:]:
        gate_red = reducer.spread(gate_red)
    up_red = reducer.spread(up_red)
    (gate_grad,) = reducer.close(gate_red, [hidden])

    d_resid_all = jnp.zeros((t * tensor, d), BF)
    for j in range(tensor):
        d_resid_all = lax.dynamic_update_slice_in_dim(d_resid_all, line.slot(j), (place ^ j) * t, axis=0)
    mixed_halves = reducer.split(mixed)
    out_got = reducer.give(mixed_halves, d_resid_all)
    out_red = reducer.open(reducer.keep(mixed_halves, d_resid_all, out_got))
    for _ in turns[1:]:
        qkv_red = reducer.add(qkv_red)
    for _ in turns[1:]:
        up_red = reducer.spread(up_red)
    for _ in turns:
        out_red = reducer.add(out_red)
    d_normed = after(d_normed, down_grad, gate_grad, *reducer.pieces(out_red), *reducer.pieces(up_red))
    (up_grad,) = reducer.close(up_red, [hidden])
    for _ in turns:
        qkv_red = reducer.spread(qkv_red)
        out_red = reducer.spread(out_red)
    query_grad, key_grad, value_grad = reducer.close(qkv_red, [width] * 3)
    (out_grad,) = reducer.close(out_red, [d])

    norm_first, first_pull = jax.vjp(rms_scale, own_in, attn_gain)
    d_in_part, attn_gain_part = first_pull(d_normed.astype(F32))
    in_grad = (d_resid + d_in_part).astype(BF)
    attn_gain_grad = gain_total(attn_gain_part, dp, tensor)
    ffn_gain_grad = gain_total(ffn_gain_part, dp, tensor)
    return (
        layer_out,
        in_grad,
        attn_gain_grad,
        query_grad,
        key_grad,
        value_grad,
        out_grad,
        ffn_gain_grad,
        gate_grad,
        up_grad,
        down_grad,
    )


def solution(mesh):
    rows, cols, lines = P(("dp", "tensor"), None), P(None, "tensor"), P("tensor", None)
    return jax.shard_map(
        functools.partial(local, dp=mesh.shape["dp"], tensor=mesh.shape["tensor"]),
        mesh=mesh,
        in_specs=(
            rows, rows, P("dp"), P("dp"), P(), cols, cols, cols, lines, P(), cols, cols, lines
        ),
        out_specs=(rows, rows, P(), cols, cols, cols, lines, P(), cols, cols, lines),
        check_vma=False,
    )
```

```python
import functools
import math

import jax
import jax.numpy as jnp
from jax import lax
from jax.experimental import pallas as pl
from jax.experimental.pallas import tpu as pltpu
from jax.sharding import PartitionSpec as P

HD = 128
EPS = 1e-05
ROPE_BASE = 500000.0
BF = jnp.bfloat16
F32 = jnp.float32
VMEM = 56 << 20
COST = {
    "give": 8, "keep": 10, "fold": 4, "spread": 4, "join": 4.5, "finish": 11, "middle": 9.5, "attend": 11,
    "attend_back": 17, "back_project": 11, "qkv": 5.6, "project": 8.6, "ffn": 22, "last": 5, "tie": 0.5,
}


def dot(left, right):
    return lax.dot_general(left, right, (((1,), (0,)), ((), ())), preferred_element_type=F32)


def dot_nt(left, right):
    return lax.dot_general(left, right, (((1,), (1,)), ((), ())), preferred_element_type=F32)


def dot_tn(left, right):
    return lax.dot_general(left, right, (((0,), (0,)), ((), ())), preferred_element_type=F32)


def sigmoid(v):
    return 1.0 / (1.0 + jnp.exp(-v))


def rms_scale(values, gain):
    return values * lax.rsqrt(jnp.mean(values * values, axis=-1, keepdims=True) + EPS) * gain


ANY = pl.BlockSpec(memory_space=pl.ANY)
TOKEN = jax.ShapeDtypeStruct((8, 128), F32)


def call(body, *, name, grid, scalars, in_specs, out_specs, out_shape, scratch=(), aliases=None):
    def run(order, *operands):
        tokens = order.take()
        ahead = scalars + len(in_specs)

        def whole(*refs):
            outs = refs[ahead + len(tokens) :]
            body(*refs[:ahead], *outs[: len(out_shape)], *outs[len(out_shape) + 1 :])
            outs[len(out_shape)][...] = jnp.zeros((8, 128), F32)

        *values, token = pl.pallas_call(
            whole,
            grid_spec=pltpu.PrefetchScalarGridSpec(
                num_scalar_prefetch=scalars,
                grid=grid,
                in_specs=list(in_specs) + [ANY] * len(tokens),
                out_specs=list(out_specs) + [pl.BlockSpec((8, 128), lambda *_: (0, 0))],
                scratch_shapes=list(scratch),
            ),
            out_shape=list(out_shape) + [TOKEN],
            input_output_aliases=aliases or {},
            compiler_params=pltpu.CompilerParams(vmem_limit_bytes=VMEM),
            cost_estimate=pl.CostEstimate(flops=int(COST[name] * 1e+09), bytes_accessed=int(COST[name] * 1e6), transcendentals=0),
            name=name,
        )(*operands, *tokens)
        order.give(token)
        return values

    return run


class Order:
    def __init__(self):
        self.tokens = []

    def take(self):
        return self.tokens

    def give(self, token):
        self.tokens = [token]

    def after(self, *values):
        return call(
            lambda *refs: None,
            name="tie",
            grid=(1,),
            scalars=0,
            in_specs=[ANY] * len(values),
            out_specs=[ANY] * len(values),
            out_shape=[jax.ShapeDtypeStruct(v.shape, v.dtype) for v in values],
            aliases={i: i for i in range(len(values))},
            )(self, *values)


def xor_pairs(size, mask):
    return [(i, i ^ mask) for i in range(size)]


class LineGather:
    def __init__(self, own, size, place):
        self.size, self.place = size, place
        self.ups, self.downs = [own], [own]

    def step(self, order=None):
        k, size = len(self.ups), self.size
        if order is not None:
            if k == 1:
                self.ups = self.downs = order.after(self.ups[0])
                self.downs = list(self.downs)
            else:
                self.ups[-1], self.downs[-1] = order.after(self.ups[-1], self.downs[-1])
        up, down = self.ups[-1], self.downs[-1]
        self.ups.append(lax.ppermute(up, "tensor", [(i, i + 1) for i in range(k - 1, size - 1)]))
        self.downs.append(lax.ppermute(down, "tensor", [(i + 1, i) for i in range(0, size - k)]))

    def hold(self, order):
        self.ups[-1], self.downs[-1] = order.after(self.ups[-1], self.downs[-1])

    def slot(self, j):
        groups = {}
        for at in range(self.size):
            groups.setdefault((at ^ j) - at, []).append(at)
        value = None
        for off, places in groups.items():
            arr = self.downs[off] if off >= 0 else self.ups[-off]
            if value is None:
                value = arr
            else:
                here = functools.reduce(jnp.logical_or, [self.place == at for at in places])
                value = jnp.where(here, arr, value)
        return value


def exchange(values):
    return lax.all_to_all(values, "tensor", 0, 0, tiled=True)


def rows_at(values, block, rows):
    return lax.dynamic_slice_in_dim(values, block * rows, rows, axis=0)


def cols_at(values, block, cols):
    return lax.dynamic_slice_in_dim(values, block * cols, cols, axis=1)


def give_body(places, *refs, two, last):
    out = refs[-1]
    if not two:
        out[...] = dot(refs[0][...], refs[1][...]).astype(BF)
        return

    @pl.when(pl.program_id(0) < last)
    def _():
        out[...] = dot(refs[0][...], refs[1][...]).astype(BF)

    @pl.when(pl.program_id(0) == last)
    def _():
        out[...] = second(refs[2:4], None).astype(BF)


def second(refs, rows):
    left, right = refs
    total, t = None, left.shape[2]
    for k in range(left.shape[0]):
        part = left[k] if rows is None else left[k, rows, :]
        term = dot(part, right[k * t : (k + 1) * t, :])
        total = term if total is None else total + term
    return total


def keep_body(places, *refs, two, last, lanes, chunks):
    ins = 4 if two else 2
    got, outs = refs[ins], refs[ins + 1 :]
    step = pl.program_id(0)
    rows = outs[0].shape[0]
    for lane in range(lanes):
        for rel in (1, 0):
            at = pl.multiple_of((places[1 + lane] ^ rel) * rows, rows)
            place = pl.ds(at, rows)
            out = outs[2 * lane + rel]
            inside = (step >= lane * chunks) & (step < (lane + 1) * chunks)

            @pl.when((inside & (step < last)) if two else inside)
            def _():
                total = dot(refs[0][place, :], refs[1][...])
                out[...] = (total + got[place, :].astype(F32)).astype(BF)

            if two and lane == lanes - 1:

                @pl.when(step == last)
                def _():
                    total = second(refs[2:4], place)
                    out[...] = (total + got[place, :].astype(F32)).astype(BF)


def fold_body(places, *refs):
    ins, outs = refs[:4], refs[4:]
    for h in (0, 1):
        total = (ins[2 * h][...].astype(F32) + ins[2 * h + 1][...].astype(F32)).astype(BF)
        if len(outs) == 2:
            outs[h][...] = total
        else:
            for rel in (0, 1):

                @pl.when(pl.program_id(0) == rel)
                def _():
                    outs[2 * h + rel][...] = total


def spread_body(places, *refs):
    ins, outs = refs[:4], refs[4:]
    for k in (0, 1):

        @pl.when(pl.program_id(0) == k)
        def _():
            for h in (0, 1):
                outs[h][...] = ins[2 * h + k][...]


def join_body(places, *refs):
    pieces, out = refs[:-1], refs[-1]
    step = pl.program_id(0) * 2 + pl.program_id(1)
    for k, piece in enumerate(pieces):

        @pl.when(step == k)
        def _():
            out[...] = piece[...]


def finish_body(core, mine, other, *outs, turned):
    for source, turn in ((mine, 0), (other, 1)):

        @pl.when(pl.program_id(0) == turn)
        def _():
            at = 0
            for k, out in enumerate(outs):
                flip = turned and k == len(outs) - 1
                width = out.shape[0] if flip else out.shape[1]
                value = source[:, at : at + width].astype(F32)
                out[...] = value.T if flip else value
                at += width


class Product:
    def __init__(self, left, right, widths, firsts, pair=()):
        self.left, self.right, self.widths, self.firsts, self.pair = left, right, widths, firsts, pair
        self.rows = left.shape[0] // 2
        self.cols = right.shape[1] + (pair[1].shape[1] if pair else 0)
        self.bn = min(512, widths[-1])


class Gradients:
    def __init__(self, products, count):
        self.count = count
        self.bits = count.bit_length() - 1
        self.index = lax.axis_index("dp")
        self.orders = [list(range(1, self.bits)), list(range(self.bits - 1, 0, -1))]
        self.step = 0
        self.kept, self.gots = [], []
        per = 2 // len(products)
        self.products = [
            Product(*p[:3], [o[0] for o in self.orders[i * per : (i + 1) * per]], p[3:])
            for i, p in enumerate(products)
        ]

    def bit(self, b):
        return (self.index >> b) & 1

    def scalars(self, *values):
        return jnp.stack([jnp.asarray(v, jnp.int32) for v in values])

    def swap(self, value, b):
        return lax.ppermute(value, "dp", xor_pairs(self.count, 1 << b))

    def operands(self, p, core):
        tokens, last = p.right.shape[0], p.right.shape[1] // p.bn
        specs = [
            pl.BlockSpec((p.rows, tokens), lambda n, s: (s[0], 0)),
            pl.BlockSpec((tokens, p.bn), lambda n, s: (0, jnp.minimum(n, last - 1))),
        ]
        if p.pair:
            count, _, t = p.pair[0].shape
            specs += [
                pl.BlockSpec((count, p.rows, t), lambda n, s: (0, s[0], 0)),
                pl.BlockSpec((tokens, p.bn), lambda n, s: (0, 0)),
            ]
        return specs, [p.left, p.right, *p.pair], dict(two=bool(p.pair), last=last)

    def give(self, order, at=0):
        p = self.products[at]
        specs, values, facts = self.operands(p, 1 - self.bit(0))
        (out,) = call(
            functools.partial(give_body, **facts),
            name="give",
            grid=(p.cols // p.bn,),
            scalars=1,
            in_specs=specs,
            out_specs=[pl.BlockSpec((p.rows, p.bn), lambda n, s: (0, n))],
            out_shape=[jax.ShapeDtypeStruct((p.rows, p.cols), BF)],
        )(order, self.scalars(1 - self.bit(0)), *values)
        p.got = self.swap(out, 0)

    def keep(self, order, at=0):
        p = self.products[at]
        lanes = len(p.firsts)
        rows, cols = p.rows // 2, p.cols // lanes
        chunks = cols // p.bn
        specs, values, facts = self.operands(p, self.bit(0))

        def out_spec(lane):
            return pl.BlockSpec(
                (rows, p.bn), lambda n, s: (0, jnp.clip(n - lane * chunks, 0, chunks - 1))
            )

        outs = call(
            functools.partial(keep_body, lanes=lanes, chunks=chunks, **facts),
            name="keep",
            grid=(lanes * chunks,),
            scalars=1,
            in_specs=specs + [pl.BlockSpec((p.rows, p.bn), lambda n, s: (0, n))],
            out_specs=[out_spec(k // 2) for k in range(2 * lanes)],
            out_shape=[jax.ShapeDtypeStruct((rows, cols), BF)] * (2 * lanes),
        )(order, self.scalars(self.bit(0), *[self.bit(b) for b in p.firsts]), *values, p.got)
        for h in range(lanes):
            self.kept.append(outs[2 * h])
            self.gots.append(self.swap(outs[2 * h + 1], p.firsts[h]))

    def fold(self, order):
        rows, cols = self.kept[0].shape
        self.step += 1
        more = self.step < self.bits - 1
        nexts = [self.bit(o[self.step]) for o in self.orders] if more else [0, 0]
        orows = rows // 2 if more else rows
        spec = lambda h: pl.BlockSpec((orows, cols), lambda r, s: (s[h] ^ r, 0))
        outs = call(
            fold_body,
            name="fold",
            grid=(2 if more else 1,),
            scalars=1,
            in_specs=[spec(0), spec(0), spec(1), spec(1)],
            out_specs=[pl.BlockSpec((orows, cols), lambda r, s: (0, 0))] * (4 if more else 2),
            out_shape=[jax.ShapeDtypeStruct((orows, cols), BF)] * (4 if more else 2),
        )(order, self.scalars(*nexts), self.kept[0], self.gots[0], self.kept[1], self.gots[1])
        self.kept = outs[:: 2 if more else 1]
        if more:
            self.gots = [self.swap(outs[1 + 2 * h], self.orders[h][self.step]) for h in (0, 1)]
        else:
            self.ask()

    def ask(self):
        self.step -= 1
        self.gots = [self.swap(k, o[self.step]) for k, o in zip(self.kept, self.orders)]

    def spread(self, order):
        rows, cols = self.kept[0].shape
        spec = pl.BlockSpec((rows, cols), lambda k, s: (0, 0))
        self.kept = call(
            spread_body,
            name="spread",
            grid=(2,),
            scalars=1,
            in_specs=[spec] * 4,
            out_specs=[
                pl.BlockSpec((rows, cols), lambda k, s: (k ^ s[0], 0)),
                pl.BlockSpec((rows, cols), lambda k, s: (k ^ s[1], 0)),
            ],
            out_shape=[jax.ShapeDtypeStruct((2 * rows, cols), BF)] * 2,
        )(
            order,
            self.scalars(*[self.bit(o[self.step]) for o in self.orders]),
            self.kept[0],
            self.gots[0],
            self.kept[1],
            self.gots[1],
        )
        self.ask()

    def join(self, order):
        brows, bcols = self.kept[0].shape
        lane = 0
        for p in self.products:
            lanes = range(lane, lane + len(p.firsts))
            lane += len(p.firsts)
            (p.half,) = call(
                join_body,
                name="join",
                grid=(len(lanes), 2),
                scalars=1,
                in_specs=[pl.BlockSpec((brows, bcols), lambda h, k, s: (0, 0))] * (2 * len(lanes)),
                out_specs=[pl.BlockSpec((brows, bcols), lambda h, k, s: (k ^ s[h], h))],
                out_shape=[jax.ShapeDtypeStruct((p.rows, p.cols), BF)],
            )(
                order,
                self.scalars(*[self.bit(self.orders[l][self.step]) for l in lanes]),
                *[v for l in lanes for v in (self.kept[l], self.gots[l])],
            )
            p.other = self.swap(p.half, 0)

    def finish(self, order, at=0):
        p = self.products[at]
        rows, cols = p.half.shape
        crows = min(256, rows)
        nblk = rows // crows
        turned = bool(p.pair)
        specs = [
            pl.BlockSpec((crows, w), lambda g, b, s: ((g ^ s[0]) * nblk + b, 0)) for w in p.widths
        ]
        shapes = [jax.ShapeDtypeStruct((2 * rows, w), F32) for w in p.widths]
        if turned:
            w = p.widths[-1]
            specs[-1] = pl.BlockSpec((w, crows), lambda g, b, s: (0, (g ^ s[0]) * nblk + b))
            shapes[-1] = jax.ShapeDtypeStruct((w, 2 * rows), F32)
        return call(
            functools.partial(finish_body, turned=turned),
            name="finish",
            grid=(2, nblk),
            scalars=1,
            in_specs=[
                pl.BlockSpec((crows, cols), lambda g, b, s: (jnp.where(g == 0, b, nblk - 1), 0)),
                pl.BlockSpec((crows, cols), lambda g, b, s: (jnp.where(g == 0, 0, b), 0)),
            ],
            out_specs=specs,
            out_shape=shapes,
        )(order, self.scalars(self.bit(0)), p.half, p.other)


class GainTotals:
    def __init__(self, parts, dp, tensor):
        self.size = parts[0].size
        self.value = jnp.concatenate([p.reshape(-1, 128) for p in parts], axis=0)
        self.left = []
        for name, size in (("tensor", tensor), ("dp", dp)):
            step = 1
            while step < size:
                masks = [step, 2 * step, 3 * step] if 2 * step < size else [step]
                self.left.append((name, size, masks))
                step *= 1 + len(masks)
        self.next()

    def next(self):
        name, size, masks = self.left.pop(0)
        self.got = [lax.ppermute(self.value, name, xor_pairs(size, m)) for m in masks]

    def step(self, order):
        self.value, *got = order.after(self.value, *self.got)
        self.value = self.value + got[0]
        if len(got) == 3:
            self.value = self.value + (got[1] + got[2])
        if self.left:
            self.next()

    def split(self, order):
        while self.left:
            self.step(order)
        self.step(order)
        value = self.value.reshape(-1)
        return [value[k : k + self.size] for k in range(0, value.size, self.size)]


def qkv_body(*refs):
    chunk, rows, wq, wk, wv, cos, sin = refs[:7]
    q_out, k_out, v_out, rows_out = refs[-4:]
    x = rows[...]
    cosine, sine = cos[...], sin[...]

    def turned(pre):
        out = []
        for h in range(pre.shape[1] // HD):
            one = pre[:, h * HD : (h + 1) * HD]
            out.append(one * cosine + pltpu.roll(one, HD // 2, 1) * sine)
        return jnp.concatenate(out, axis=1)

    q_out[...] = turned(dot(x, wq[...])).astype(BF)
    k_out[...] = turned(dot(x, wk[...])).astype(BF)
    v_out[...] = dot(x, wv[...]).astype(BF)
    part = rows_out.shape[0]
    rows_out[...] = rows[:, pl.ds(pl.multiple_of(pl.program_id(0) * part, part), part)].T


def qkv_slot(order, chunk, rows, w_query, w_key, w_value, cos, sin, held, count):
    t, d = rows.shape
    width = w_query.shape[1]
    bn = min(256, width)
    wspec = pl.BlockSpec((d, bn), lambda i, s: (0, i))
    tspec = pl.BlockSpec((t, HD), lambda i, s: (s[0], 0))
    return call(
        qkv_body,
        name="qkv",
        grid=(width // bn,),
        scalars=1,
        in_specs=[pl.BlockSpec((t, d), lambda i, s: (0, 0)), wspec, wspec, wspec, tspec, tspec]
        + [ANY] * len(held),
        out_specs=[pl.BlockSpec((t, bn), lambda i, s: (s[0], i))] * 3
        + [pl.BlockSpec((d // (width // bn), t), lambda i, s: (i, s[0]))],
        out_shape=[jax.ShapeDtypeStruct((count * t, width), BF)] * 3
        + [jax.ShapeDtypeStruct((d, count * t), BF)],
        aliases={7 + i: i for i in range(len(held))},
    )(order, chunk, rows, w_query, w_key, w_value, cos, sin, *held)


def attend_consts(seq_len):
    to_log2 = math.log2(math.e)
    return (to_log2 / math.sqrt(HD), math.log2(seq_len))


def attend_body(docs, q_ref, k_ref, v_ref, ids_col, ids_row, mix, acc, *, block):
    seq_len = q_ref.shape[0]
    scale, shift = attend_consts(seq_len)
    causal = lax.broadcasted_iota(jnp.int32, (block, block), 0) >= lax.broadcasted_iota(
        jnp.int32, (block, block), 1
    )

    def term(i, j):
        q = q_ref[i * block : (i + 1) * block, :]
        k = k_ref[j * block : (j + 1) * block, :]
        sig = 1.0 / (1.0 + jnp.exp2(shift - dot_nt(q, k) * scale))
        same = ids_col[i * block : (i + 1) * block, :] == ids_row[:, j * block : (j + 1) * block]
        allowed = same & causal if i == j else same
        probs = jnp.where(allowed, sig, 0.0).astype(BF)
        return dot(probs, v_ref[j * block : (j + 1) * block, :])

    for i in range(seq_len // block):
        acc[...] = term(i, i)
        for j in range(i):

            @pl.when(docs[(j + 1) * block - 1] == docs[i * block])
            def _():
                acc[...] += term(i, j)

        mix[i * block : (i + 1) * block, :] = acc[...].astype(BF)


def attend(order, docs, q, k, v):
    seq_len, width = q.shape
    block = 256
    head = pl.BlockSpec((seq_len, HD), lambda h, s: (0, h))
    return call(
        functools.partial(attend_body, block=block),
        name="attend",
        grid=(width // HD,),
        scalars=1,
        in_specs=[
            head,
            head,
            head,
            pl.BlockSpec((seq_len, 1), lambda h, s: (0, 0)),
            pl.BlockSpec((1, seq_len), lambda h, s: (0, 0)),
        ],
        out_specs=[head],
        out_shape=[jax.ShapeDtypeStruct((seq_len, width), BF)],
        scratch=[pltpu.VMEM((block, HD), F32)],
    )(order, docs, q, k, v, docs.reshape(-1, 1), docs.reshape(1, -1))


def attend_back_body(
    docs, q_ref, k_ref, v_ref, dmix, ids_col, ids_row, cos, sin, out, dq, dk, dv, *, block
):
    seq_len = q_ref.shape[0]
    scale, shift = attend_consts(seq_len)
    causal = lax.broadcasted_iota(jnp.int32, (block, block), 0) <= lax.broadcasted_iota(
        jnp.int32, (block, block), 1
    )

    def at(i):
        return slice(i * block, (i + 1) * block)

    def term(i, j):
        q, k, v, d = q_ref[at(i), :], k_ref[at(j), :], v_ref[at(j), :], dmix[at(i), :]
        sig = 1.0 / (1.0 + jnp.exp2(shift - dot_nt(k, q) * scale))
        same = ids_col[at(j), :] == ids_row[:, at(i)]
        allowed = same & causal if i == j else same
        probs = jnp.where(allowed, sig, 0.0)
        d_scores = (dot_nt(v, d) * probs * (1.0 - probs)).astype(BF)
        return dot_tn(d_scores, k), dot(d_scores, q), dot(probs.astype(BF), d)

    for i in range(seq_len // block):
        dq[at(i), :], dk[at(i), :], dv[at(i), :] = term(i, i)
    for i in range(seq_len // block):
        for j in range(i):

            @pl.when(docs[(j + 1) * block - 1] == docs[i * block])
            def _():
                a, b, c = term(i, j)
                dq[at(i), :] += a
                dk[at(j), :] += b
                dv[at(j), :] += c

    cosine, sine = cos[...], sin[...]

    def turned_back(v):
        v = v * (1.0 / math.sqrt(HD))
        return (v * cosine - pltpu.roll(v, HD // 2, 1) * sine).astype(BF)

    width = out.shape[1] // 3
    at_head = pl.program_id(0) * HD
    for part, value in enumerate((turned_back(dq[...]), turned_back(dk[...]), dv[...].astype(BF))):
        out[:, pl.ds(pl.multiple_of(at_head + part * width, HD), HD)] = value


def attend_back(order, docs, q, k, v, d_mix, cos, sin):
    seq_len, width = q.shape
    head = pl.BlockSpec((seq_len, HD), lambda h, s: (0, h))
    whole = lambda r, c: pl.BlockSpec((r, c), lambda h, s: (0, 0))
    return call(
        functools.partial(attend_back_body, block=256),
        name="attend_back",
        grid=(width // HD,),
        scalars=1,
        in_specs=[head] * 4
        + [whole(seq_len, 1), whole(1, seq_len), whole(seq_len, HD), whole(seq_len, HD)],
        out_specs=[whole(seq_len, 3 * width)],
        out_shape=[jax.ShapeDtypeStruct((seq_len, 3 * width), BF)],
        scratch=[pltpu.VMEM((seq_len, HD), F32)] * 3,
    )(order, docs, q, k, v, d_mix, docs.reshape(-1, 1), docs.reshape(1, -1), cos, sin)


def project_body(mix, w_ref, x_ref, gain, resid, normed, acc):
    parts, _, cols = w_ref.shape
    step = pl.program_id(0)

    @pl.when(step == 0)
    def _():
        acc[...] = x_ref[...].astype(F32)

    for p in range(parts):
        acc[:, p * cols : (p + 1) * cols] += dot(mix[...], w_ref[p])

    @pl.when(step == pl.num_programs(0) - 1)
    def _():
        resid[...] = acc[...]
        normed[...] = rms_scale(acc[...], gain[...]).astype(BF)


def project(order, mix, w_out, x, gain):
    t, d = x.shape
    width = mix.shape[1]
    parts, _, cols = w_out.shape
    whole = lambda r, c: pl.BlockSpec((r, c), lambda i: (0, 0))
    return call(
        project_body,
        name="project",
        grid=(mix.shape[0] // t,),
        scalars=0,
        in_specs=[
            pl.BlockSpec((t, width), lambda i: (i, 0)),
            pl.BlockSpec((parts, width, cols), lambda i: (0, i, 0)),
            whole(t, d),
            whole(1, d),
        ],
        out_specs=[whole(t, d)] * 2,
        out_shape=[jax.ShapeDtypeStruct((t, d), F32), jax.ShapeDtypeStruct((t, d), BF)],
        scratch=[pltpu.VMEM((t, d), F32)],
    )(order, mix, w_out, x, gain.reshape(1, -1))


def norm_back(d_normed, rows, gain):
    r = lax.rsqrt(jnp.mean(rows * rows, axis=-1, keepdims=True) + EPS)
    u = rows * r
    scaled = d_normed * gain
    d_rows = r * (scaled - u * jnp.mean(scaled * u, axis=-1, keepdims=True))
    return d_rows, jnp.sum(d_normed * u, axis=0, keepdims=True)


def middle_body(d_ref, resid, cot, gain, w_ref, out, d_resid, low_t, part, low):
    parts, _, cols = w_ref.shape

    @pl.when(pl.program_id(0) == 0)
    def _():
        d_rows, part[...] = norm_back(d_ref[...].astype(F32), resid[...], gain[...])
        total = cot[...].astype(F32) + d_rows
        d_resid[...] = total
        low[...] = total.astype(BF)
        low_t[...] = low[...].T

    total = None
    for p in range(parts):
        term = dot_nt(low[:, p * cols : (p + 1) * cols], w_ref[p])
        total = term if total is None else total + term
    out[...] = total.astype(BF)


def middle(order, d_normed2, resid, cot, gain, w_out, width):
    t, d = resid.shape
    parts, rows, cols = w_out.shape
    count = rows // width
    whole = lambda r, c: pl.BlockSpec((r, c), lambda i: (0, 0))
    return call(
        middle_body,
        name="middle",
        grid=(count,),
        scalars=0,
        in_specs=[whole(t, d)] * 3
        + [whole(1, d), pl.BlockSpec((parts, width, cols), lambda i: (0, i, 0))],
        out_specs=[
            pl.BlockSpec((t, width), lambda i: (i, 0)),
            whole(t, d),
            whole(d, t),
            whole(1, d),
        ],
        out_shape=[
            jax.ShapeDtypeStruct((count * t, width), BF),
            jax.ShapeDtypeStruct((t, d), F32),
            jax.ShapeDtypeStruct((d, t), BF),
            jax.ShapeDtypeStruct((1, d), F32),
        ],
        scratch=[pltpu.VMEM((t, d), BF)],
    )(order, d_normed2, resid, cot, gain.reshape(1, -1), w_out)


def last_body(d_ref, x_ref, d_resid, gain, out, part):
    d_rows, part[...] = norm_back(d_ref[...].astype(F32), x_ref[...].astype(F32), gain[...])
    out[...] = (d_resid[...] + d_rows).astype(BF)


def last(order, d_normed, x, d_resid, gain):
    t, d = x.shape
    whole = lambda r, c: pl.BlockSpec((r, c), lambda i: (0, 0))
    return call(
        last_body,
        name="last",
        grid=(1,),
        scalars=0,
        in_specs=[whole(t, d)] * 3 + [whole(1, d)],
        out_specs=[whole(t, d), whole(1, d)],
        out_shape=[jax.ShapeDtypeStruct((t, d), BF), jax.ShapeDtypeStruct((1, d), F32)],
    )(order, d_normed, x, d_resid, gain.reshape(1, -1))


def back_project_body(d_ref, wq, wk, wv, out):
    total = None
    width = wq.shape[1]
    for k, w in enumerate((wq, wk, wv)):
        term = dot_nt(d_ref[:, k * width : (k + 1) * width], w[...])
        total = term if total is None else total + term
    out[...] = total.astype(BF)


def back_project(order, d_qkv, w_query, w_key, w_value):
    seq_len, wide = d_qkv.shape
    d, width = w_query.shape
    bn = 512
    wspec = pl.BlockSpec((bn, width), lambda i: (i, 0))
    return call(
        back_project_body,
        name="back_project",
        grid=(d // bn,),
        scalars=0,
        in_specs=[pl.BlockSpec((seq_len, wide), lambda i: (0, 0)), wspec, wspec, wspec],
        out_specs=[pl.BlockSpec((seq_len, bn), lambda i: (0, i))],
        out_shape=[jax.ShapeDtypeStruct((seq_len, d), BF)],
    )(order, d_qkv, w_query, w_key, w_value)[0]


def ffn_body(*refs):
    chunk, rows, cot, wg, wu, wd = refs[:6]
    inner, d_gate, d_up, rows_out, cot_out, d_rows, down, acc_d, acc_o = refs[-9:]
    step, last = pl.program_id(0), pl.num_programs(0) - 1
    x = rows[...]
    gate = dot(x, wg[...])
    up = dot(x, wu[...])
    sig = sigmoid(gate)
    silu = gate * sig
    inner_b = (silu * up).astype(BF)
    inner[...] = inner_b.T
    part = rows_out.shape[0]
    rows_out[...] = rows[:, pl.ds(pl.multiple_of(step * part, part), part)].T
    d_inner = dot_nt(cot[...], wd[...])
    dg = (d_inner * up * (sig * (1.0 + gate * (1.0 - sig)))).astype(BF)
    du = (d_inner * silu).astype(BF)
    d_gate[...] = dg
    d_up[...] = du
    term_o = dot(inner_b, wd[...])
    term_d = dot_nt(dg, wg[...]) + dot_nt(du, wu[...])

    @pl.when(step == 0)
    def _():
        acc_o[...] = term_o
        acc_d[...] = term_d
        cot_out[...] = cot[...]

    @pl.when(step > 0)
    def _():
        acc_o[...] += term_o
        acc_d[...] += term_d

    @pl.when(step == last)
    def _():
        d_rows[...] = acc_d[...].astype(BF)
        down[...] = acc_o[...].astype(BF)


def ffn_slot(order, chunk, rows, cot, w_gate, w_up, w_down, held, count):
    t, d = rows.shape
    hidden = w_gate.shape[1]
    bh = min(512, hidden)
    steps = hidden // bh
    wcol = pl.BlockSpec((d, bh), lambda i, s: (0, i))
    part = pl.BlockSpec((t, bh), lambda i, s: (s[0], i))
    line = pl.BlockSpec((t, d), lambda i, s: (s[0], 0))
    return call(
        ffn_body,
        name="ffn",
        grid=(hidden // bh,),
        scalars=1,
        in_specs=[
            pl.BlockSpec((t, d), lambda i, s: (0, 0)),
            pl.BlockSpec((t, d), lambda i, s: (0, 0)),
            wcol,
            wcol,
            pl.BlockSpec((bh, d), lambda i, s: (i, 0)),
        ]
        + [ANY] * len(held),
        out_specs=[pl.BlockSpec((bh, t), lambda i, s: (i, s[0])), part, part]
        + [pl.BlockSpec((d // steps, t), lambda i, s: (i, s[0])), line, line, line],
        out_shape=[jax.ShapeDtypeStruct((hidden, count * t), BF)]
        + [jax.ShapeDtypeStruct((count * t, hidden), BF)] * 2
        + [jax.ShapeDtypeStruct((d, count * t), BF)]
        + [jax.ShapeDtypeStruct((count * t, d), BF)] * 3,
        scratch=[pltpu.VMEM((t, d), F32)] * 2,
        aliases={6 + i: i for i in range(len(held))},
    )(order, chunk, rows, cot, w_gate, w_up, w_down, *held)


def local(
    layer_in,
    cotangent,
    doc_ids,
    positions,
    attn_gain,
    w_query,
    w_key,
    w_value,
    w_out,
    ffn_gain,
    w_gate,
    w_up,
    w_down,
    *,
    dp,
    tensor,
):
    t, d = layer_in.shape
    width = w_query.shape[1]
    hidden = w_gate.shape[1]
    place = lax.axis_index("tensor")
    chunks = jnp.stack([place ^ j for j in range(tensor)]).astype(jnp.int32)
    chunk = [chunks[j : j + 1] for j in range(tensor)]
    order = Order()

    share = w_out.shape[1] // dp
    w_cols = lax.all_gather(
        cols_at(w_out, lax.axis_index("dp"), share), "tensor", axis=0, tiled=True
    )
    half = HD // 2
    freqs = ROPE_BASE ** (-(jnp.arange(half).astype(F32) * 2.0) / HD)
    angles = positions.astype(F32)[:, None] * freqs[None, :]
    cosine, sine = jnp.cos(angles), jnp.sin(angles)
    cos = jnp.concatenate([cosine, cosine], axis=1)
    sin = jnp.concatenate([-sine, sine], axis=1)

    normed_own = rms_scale(layer_in.astype(F32), attn_gain).astype(BF)
    line = LineGather(normed_own, tensor, place)
    line.step()
    held = []
    for j in range(tensor):
        if 0 < j < tensor - 1:
            line.step(order)
        if j == tensor - 1:
            cots = LineGather(cotangent, tensor, place)
            cots.step(order)
        held = qkv_slot(order, chunk[j], line.slot(j), w_query, w_key, w_value, cos, sin, held, tensor)
        if j == 1:
            (w_cols,) = order.after(w_cols)
            w_out_all = lax.all_gather(w_cols, "dp", axis=0)
    query, key, value, normed_t = held
    (mixed,) = attend(order, doc_ids, query, key, value)
    mix = exchange(mixed)
    cots.step(order)
    resid, normed2_own = project(order, mix, w_out_all, layer_in, ffn_gain)

    weights = (w_gate, w_up, w_down)
    line = LineGather(normed2_own, tensor, place)
    line.step()
    held = ffn_slot(order, chunk[0], line.slot(0), cotangent, *weights, [], tensor)
    for j in range(1, tensor):
        if j < tensor - 1:
            line.step(order)
            if len(cots.ups) < tensor:
                cots.step(order)
        else:
            cots.hold(order)
            line.hold(order)
        held = ffn_slot(order, chunk[j], line.slot(j), cots.slot(j), *weights, held, tensor)
    inner_t, d_gate, d_up, normed2_t, cot_all, d_normed2_part, down_part = held
    d_normed2 = lax.psum_scatter(d_normed2_part, "tensor", scatter_dimension=0, tiled=True)

    first = Gradients([(inner_t, cot_all, [d])], dp)
    wide = Gradients([(normed2_t, d_gate, [hidden]), (normed2_t, d_up, [hidden])], dp)
    more = range(first.bits - 2)

    first.give(order)
    wide.give(order, 0)
    wide.give(order, 1)
    first.keep(order)
    wide.keep(order, 0)
    wide.keep(order, 1)
    first.fold(order)
    for _ in more:
        first.fold(order)
    d_mix, d_resid, d_resid_t, ffn_gain_part = middle(
        order, d_normed2, resid, cotangent, ffn_gain, w_out_all, width
    )
    d_mix = exchange(d_mix)
    d_resid_all = lax.all_gather(d_resid_t, "tensor", axis=0)
    for _ in more:
        first.spread(order)
    wide.fold(order)
    (d_qkv,) = attend_back(order, doc_ids, query, key, value, d_mix, cos, sin)
    downs = exchange(order.after(down_part)[0]).reshape(tensor, t, d)
    d_normed = lax.psum_scatter(
        back_project(order, d_qkv, w_query, w_key, w_value),
        "tensor",
        scatter_dimension=0,
        tiled=True,
    )
    first.join(order)
    for _ in more:
        wide.fold(order)
    for _ in more:
        wide.spread(order)
    attn = Gradients([(normed_t, d_qkv, [width] * 4, d_resid_all, mixed)], dp)
    attn.give(order)
    attn.keep(order)
    wide.join(order)
    (down_grad,) = first.finish(order)
    attn.fold(order)
    (gate_grad,) = wide.finish(order, 0)
    for _ in more:
        attn.fold(order)
    in_grad, attn_gain_part = last(order, d_normed, layer_in, d_resid, attn_gain)
    totals = GainTotals([attn_gain_part, ffn_gain_part], dp, tensor)
    (up_grad,) = wide.finish(order, 1)
    totals.step(order)
    for _ in more:
        attn.spread(order)
    attn_gain_grad, ffn_gain_grad = totals.split(order)
    attn.join(order)
    query_grad, key_grad, value_grad, out_grad = attn.finish(order)
    layer_out = (resid + jnp.sum(downs.astype(F32), axis=0)).astype(BF)
    return (
        layer_out,
        in_grad,
        attn_gain_grad,
        query_grad,
        key_grad,
        value_grad,
        out_grad,
        ffn_gain_grad,
        gate_grad,
        up_grad,
        down_grad,
    )


def solution(mesh):
    rows, cols, lines = P(("dp", "tensor"), None), P(None, "tensor"), P("tensor", None)
    return jax.shard_map(
        functools.partial(local, dp=mesh.shape["dp"], tensor=mesh.shape["tensor"]),
        mesh=mesh,
        in_specs=(
            rows, rows, P("dp"), P("dp"), P(), cols, cols, cols, lines, P(), cols, cols, lines
        ),
        out_specs=(rows, rows, P(), cols, cols, cols, lines, P(), cols, cols, lines),
        check_vma=False,
    )
```

```python
import functools
import math

import jax
import jax.numpy as jnp
from jax import lax
from jax.experimental import pallas as pl
from jax.experimental.pallas import tpu as pltpu
from jax.sharding import PartitionSpec as P

HD = 128
EPS = 1e-05
ROPE_BASE = 500000.0
BF = jnp.bfloat16
F32 = jnp.float32
VMEM = 56 << 20
COST = {
    "give": 8, "give_second": 2.5, "keep": 10, "fold": 4, "spread": 4, "join": 4.5, "finish": 11, "middle": 9.5, "attend": 11,
    "attend_back": 17, "back_project": 11, "qkv": 5.6, "project": 8.6, "ffn": 22, "last": 5, "tie": 0.5,
}


def dot(left, right):
    return lax.dot_general(left, right, (((1,), (0,)), ((), ())), preferred_element_type=F32)


def dot_nt(left, right):
    return lax.dot_general(left, right, (((1,), (1,)), ((), ())), preferred_element_type=F32)


def dot_tn(left, right):
    return lax.dot_general(left, right, (((0,), (0,)), ((), ())), preferred_element_type=F32)


def sigmoid(v):
    return 1.0 / (1.0 + jnp.exp(-v))


def rms_scale(values, gain):
    return values * lax.rsqrt(jnp.mean(values * values, axis=-1, keepdims=True) + EPS) * gain


ANY = pl.BlockSpec(memory_space=pl.ANY)
TOKEN = jax.ShapeDtypeStruct((8, 128), F32)


def call(body, *, name, grid, scalars, in_specs, out_specs, out_shape, scratch=(), aliases=None):
    def run(order, *operands):
        tokens = order.take()
        ahead = scalars + len(in_specs)

        def whole(*refs):
            outs = refs[ahead + len(tokens) :]
            body(*refs[:ahead], *outs[: len(out_shape)], *outs[len(out_shape) + 1 :])
            outs[len(out_shape)][...] = jnp.zeros((8, 128), F32)

        *values, token = pl.pallas_call(
            whole,
            grid_spec=pltpu.PrefetchScalarGridSpec(
                num_scalar_prefetch=scalars,
                grid=grid,
                in_specs=list(in_specs) + [ANY] * len(tokens),
                out_specs=list(out_specs) + [pl.BlockSpec((8, 128), lambda *_: (0, 0))],
                scratch_shapes=list(scratch),
            ),
            out_shape=list(out_shape) + [TOKEN],
            input_output_aliases=aliases or {},
            compiler_params=pltpu.CompilerParams(vmem_limit_bytes=VMEM),
            cost_estimate=pl.CostEstimate(flops=int(COST[name] * order.worth * 1e9), bytes_accessed=int(COST[name] * 1e6), transcendentals=0),
            name=name,
        )(*operands, *tokens)
        order.give(token)
        return values

    return run


class Order:
    def __init__(self):
        self.tokens, self.worth = [], 1.3

    def take(self):
        return self.tokens

    def give(self, token):
        self.tokens = [token]

    def after(self, *values):
        return call(
            lambda *refs: None,
            name="tie",
            grid=(1,),
            scalars=0,
            in_specs=[ANY] * len(values),
            out_specs=[ANY] * len(values),
            out_shape=[jax.ShapeDtypeStruct(v.shape, v.dtype) for v in values],
            aliases={i: i for i in range(len(values))},
            )(self, *values)


def xor_pairs(size, mask):
    return [(i, i ^ mask) for i in range(size)]


class LineGather:
    def __init__(self, own, size, place):
        self.size, self.place = size, place
        self.ups, self.downs = [own], [own]

    def step(self, order=None):
        k, size = len(self.ups), self.size
        if order is not None:
            if k == 1:
                self.ups = self.downs = order.after(self.ups[0])
                self.downs = list(self.downs)
            else:
                self.ups[-1], self.downs[-1] = order.after(self.ups[-1], self.downs[-1])
        up, down = self.ups[-1], self.downs[-1]
        self.ups.append(lax.ppermute(up, "tensor", [(i, i + 1) for i in range(k - 1, size - 1)]))
        self.downs.append(lax.ppermute(down, "tensor", [(i + 1, i) for i in range(0, size - k)]))

    def hold(self, order):
        self.ups[-1], self.downs[-1] = order.after(self.ups[-1], self.downs[-1])

    def slot(self, j):
        groups = {}
        for at in range(self.size):
            groups.setdefault((at ^ j) - at, []).append(at)
        value = None
        for off, places in groups.items():
            arr = self.downs[off] if off >= 0 else self.ups[-off]
            if value is None:
                value = arr
            else:
                here = functools.reduce(jnp.logical_or, [self.place == at for at in places])
                value = jnp.where(here, arr, value)
        return value


def exchange(values):
    return lax.all_to_all(values, "tensor", 0, 0, tiled=True)


def rows_at(values, block, rows):
    return lax.dynamic_slice_in_dim(values, block * rows, rows, axis=0)


def cols_at(values, block, cols):
    return lax.dynamic_slice_in_dim(values, block * cols, cols, axis=1)


def give_body(places, left, right, out):
    out[...] = dot(left[...], right[...]).astype(BF)


def give_second_body(places, left, right, out):
    out[...] = second((left, right), None).astype(BF)


def second(refs, rows):
    left, right = refs
    total, t = None, left.shape[2]
    for k in range(left.shape[0]):
        part = left[k] if rows is None else left[k, rows, :]
        term = dot(part, right[k * t : (k + 1) * t, :])
        total = term if total is None else total + term
    return total


def keep_body(places, *refs, two, last, lanes, chunks):
    ins = 4 if two else 2
    gots, outs = refs[ins : ins + (2 if two else 1)], refs[ins + (2 if two else 1) :]
    step = pl.program_id(0)
    rows = outs[0].shape[0]
    for lane in range(lanes):
        for rel in (1, 0):
            at = pl.multiple_of((places[1 + lane] ^ rel) * rows, rows)
            place = pl.ds(at, rows)
            out = outs[2 * lane + rel]
            inside = (step >= lane * chunks) & (step < (lane + 1) * chunks)

            @pl.when((inside & (step < last)) if two else inside)
            def _():
                total = dot(refs[0][place, :], refs[1][...])
                out[...] = (total + gots[0][place, :].astype(F32)).astype(BF)

            if two and lane == lanes - 1:

                @pl.when(step == last)
                def _():
                    total = second(refs[2:4], place)
                    out[...] = (total + gots[1][place, :].astype(F32)).astype(BF)


def fold_body(places, *refs):
    ins, outs = refs[:4], refs[4:]
    for h in (0, 1):
        total = (ins[2 * h][...].astype(F32) + ins[2 * h + 1][...].astype(F32)).astype(BF)
        if len(outs) == 2:
            outs[h][...] = total
        else:
            for rel in (0, 1):

                @pl.when(pl.program_id(0) == rel)
                def _():
                    outs[2 * h + rel][...] = total


def spread_body(places, *refs):
    ins, outs = refs[:4], refs[4:]
    for k in (0, 1):

        @pl.when(pl.program_id(0) == k)
        def _():
            for h in (0, 1):
                outs[h][...] = ins[2 * h + k][...]


def join_body(places, *refs):
    pieces, out = refs[:-1], refs[-1]
    step = pl.program_id(0) * 2 + pl.program_id(1)
    for k, piece in enumerate(pieces):

        @pl.when(step == k)
        def _():
            out[...] = piece[...]


def finish_body(core, mine, other, *outs, turned):
    for source, turn in ((mine, 0), (other, 1)):

        @pl.when(pl.program_id(0) == turn)
        def _():
            at = 0
            for k, out in enumerate(outs):
                flip = turned and k == len(outs) - 1
                width = out.shape[0] if flip else out.shape[1]
                value = source[:, at : at + width].astype(F32)
                out[...] = value.T if flip else value
                at += width


class Product:
    def __init__(self, left, right, widths, firsts, pair=()):
        self.left, self.right, self.widths, self.firsts, self.pair = left, right, widths, firsts, pair
        self.rows = left.shape[0] // 2
        self.cols = right.shape[1] + (pair[1].shape[1] if pair else 0)
        self.bn = min(512, widths[-1])
        self.gots = []


class Gradients:
    def __init__(self, products, count):
        self.count = count
        self.bits = count.bit_length() - 1
        self.index = lax.axis_index("dp")
        self.orders = [list(range(1, self.bits)), list(range(self.bits - 1, 0, -1))]
        self.step = 0
        self.kept, self.gots = [], []
        per = 2 // len(products)
        self.products = [
            Product(*p[:3], [o[0] for o in self.orders[i * per : (i + 1) * per]], p[3:])
            for i, p in enumerate(products)
        ]

    def bit(self, b):
        return (self.index >> b) & 1

    def scalars(self, *values):
        return jnp.stack([jnp.asarray(v, jnp.int32) for v in values])

    def swap(self, value, b):
        return lax.ppermute(value, "dp", xor_pairs(self.count, 1 << b))

    def operands(self, p, core):
        tokens, last = p.right.shape[0], p.right.shape[1] // p.bn
        specs = [
            pl.BlockSpec((p.rows, tokens), lambda n, s: (s[0], 0)),
            pl.BlockSpec((tokens, p.bn), lambda n, s: (0, jnp.minimum(n, last - 1))),
        ]
        if p.pair:
            count, _, t = p.pair[0].shape
            specs += [
                pl.BlockSpec((count, p.rows, t), lambda n, s: (0, s[0], 0)),
                pl.BlockSpec((tokens, p.bn), lambda n, s: (0, 0)),
            ]
        return specs, [p.left, p.right, *p.pair], dict(two=bool(p.pair), last=last)

    def give(self, order, at=0, second=False):
        p = self.products[at]
        specs, values, facts = self.operands(p, 1 - self.bit(0))
        some = slice(2, 4) if second else slice(0, 2)
        cols = values[some][1].shape[1]
        (out,) = call(
            give_second_body if second else give_body,
            name="give_second" if second else "give",
            grid=(cols // p.bn,),
            scalars=1,
            in_specs=specs[some],
            out_specs=[pl.BlockSpec((p.rows, p.bn), lambda n, s: (0, n))],
            out_shape=[jax.ShapeDtypeStruct((p.rows, cols), BF)],
        )(order, self.scalars(1 - self.bit(0)), *values[some])
        p.gots.append(self.swap(out, 0))

    def keep(self, order, at=0):
        p = self.products[at]
        lanes = len(p.firsts)
        rows, cols = p.rows // 2, p.cols // lanes
        chunks = cols // p.bn
        specs, values, facts = self.operands(p, self.bit(0))

        def out_spec(lane):
            return pl.BlockSpec(
                (rows, p.bn), lambda n, s: (0, jnp.clip(n - lane * chunks, 0, chunks - 1))
            )

        outs = call(
            functools.partial(keep_body, lanes=lanes, chunks=chunks, **facts),
            name="keep",
            grid=(lanes * chunks,),
            scalars=1,
            in_specs=specs
            + [
                pl.BlockSpec((p.rows, p.bn), lambda n, s: (0, jnp.minimum(n, facts["last"] - 1))),
                pl.BlockSpec((p.rows, p.bn), lambda n, s: (0, 0)),
            ][: len(p.gots)],
            out_specs=[out_spec(k // 2) for k in range(2 * lanes)],
            out_shape=[jax.ShapeDtypeStruct((rows, cols), BF)] * (2 * lanes),
        )(order, self.scalars(self.bit(0), *[self.bit(b) for b in p.firsts]), *values, *p.gots)
        for h in range(lanes):
            self.kept.append(outs[2 * h])
            self.gots.append(self.swap(outs[2 * h + 1], p.firsts[h]))

    def fold(self, order):
        rows, cols = self.kept[0].shape
        self.step += 1
        more = self.step < self.bits - 1
        nexts = [self.bit(o[self.step]) for o in self.orders] if more else [0, 0]
        orows = rows // 2 if more else rows
        spec = lambda h: pl.BlockSpec((orows, cols), lambda r, s: (s[h] ^ r, 0))
        outs = call(
            fold_body,
            name="fold",
            grid=(2 if more else 1,),
            scalars=1,
            in_specs=[spec(0), spec(0), spec(1), spec(1)],
            out_specs=[pl.BlockSpec((orows, cols), lambda r, s: (0, 0))] * (4 if more else 2),
            out_shape=[jax.ShapeDtypeStruct((orows, cols), BF)] * (4 if more else 2),
        )(order, self.scalars(*nexts), self.kept[0], self.gots[0], self.kept[1], self.gots[1])
        self.kept = outs[:: 2 if more else 1]
        if more:
            self.gots = [self.swap(outs[1 + 2 * h], self.orders[h][self.step]) for h in (0, 1)]
        else:
            self.ask()

    def hold(self, order):
        self.gots = order.after(*self.gots)

    def ask(self):
        self.step -= 1
        self.gots = [self.swap(k, o[self.step]) for k, o in zip(self.kept, self.orders)]

    def spread(self, order):
        rows, cols = self.kept[0].shape
        spec = pl.BlockSpec((rows, cols), lambda k, s: (0, 0))
        self.kept = call(
            spread_body,
            name="spread",
            grid=(2,),
            scalars=1,
            in_specs=[spec] * 4,
            out_specs=[
                pl.BlockSpec((rows, cols), lambda k, s: (k ^ s[0], 0)),
                pl.BlockSpec((rows, cols), lambda k, s: (k ^ s[1], 0)),
            ],
            out_shape=[jax.ShapeDtypeStruct((2 * rows, cols), BF)] * 2,
        )(
            order,
            self.scalars(*[self.bit(o[self.step]) for o in self.orders]),
            self.kept[0],
            self.gots[0],
            self.kept[1],
            self.gots[1],
        )
        self.ask()

    def join(self, order):
        brows, bcols = self.kept[0].shape
        lane = 0
        for p in self.products:
            lanes = range(lane, lane + len(p.firsts))
            lane += len(p.firsts)
            (p.half,) = call(
                join_body,
                name="join",
                grid=(len(lanes), 2),
                scalars=1,
                in_specs=[pl.BlockSpec((brows, bcols), lambda h, k, s: (0, 0))] * (2 * len(lanes)),
                out_specs=[pl.BlockSpec((brows, bcols), lambda h, k, s: (k ^ s[h], h))],
                out_shape=[jax.ShapeDtypeStruct((p.rows, p.cols), BF)],
            )(
                order,
                self.scalars(*[self.bit(self.orders[l][self.step]) for l in lanes]),
                *[v for l in lanes for v in (self.kept[l], self.gots[l])],
            )
            p.other = self.swap(p.half, 0)

    def finish(self, order, at=0):
        p = self.products[at]
        rows, cols = p.half.shape
        crows = min(256, rows)
        nblk = rows // crows
        turned = bool(p.pair)
        specs = [
            pl.BlockSpec((crows, w), lambda g, b, s: ((g ^ s[0]) * nblk + b, 0)) for w in p.widths
        ]
        shapes = [jax.ShapeDtypeStruct((2 * rows, w), F32) for w in p.widths]
        if turned:
            w = p.widths[-1]
            specs[-1] = pl.BlockSpec((w, crows), lambda g, b, s: (0, (g ^ s[0]) * nblk + b))
            shapes[-1] = jax.ShapeDtypeStruct((w, 2 * rows), F32)
        return call(
            functools.partial(finish_body, turned=turned),
            name="finish",
            grid=(2, nblk),
            scalars=1,
            in_specs=[
                pl.BlockSpec((crows, cols), lambda g, b, s: (jnp.where(g == 0, b, nblk - 1), 0)),
                pl.BlockSpec((crows, cols), lambda g, b, s: (jnp.where(g == 0, 0, b), 0)),
            ],
            out_specs=specs,
            out_shape=shapes,
        )(order, self.scalars(self.bit(0)), p.half, p.other)


class GainTotals:
    def __init__(self, parts, dp, tensor):
        self.size = parts[0].size
        self.value = jnp.concatenate([p.reshape(-1, 128) for p in parts], axis=0)
        self.left = [
            (name, size, [1 << k])
            for name, size in (("tensor", tensor), ("dp", dp))
            for k in range(size.bit_length() - 1)
        ]
        self.next()

    def next(self):
        name, size, masks = self.left.pop(0)
        self.got = [lax.ppermute(self.value, name, xor_pairs(size, m)) for m in masks]

    def step(self, order):
        self.value, *got = order.after(self.value, *self.got)
        self.value = self.value + got[0]
        if self.left:
            self.next()

    def split(self, order):
        while self.left:
            self.step(order)
        self.step(order)
        value = self.value.reshape(-1)
        return [value[k : k + self.size] for k in range(0, value.size, self.size)]


def qkv_body(*refs):
    chunk, rows, wq, wk, wv, cos, sin = refs[:7]
    q_out, k_out, v_out, rows_out = refs[-4:]
    x = rows[...]
    cosine, sine = cos[...], sin[...]

    def turned(pre):
        out = []
        for h in range(pre.shape[1] // HD):
            one = pre[:, h * HD : (h + 1) * HD]
            out.append(one * cosine + pltpu.roll(one, HD // 2, 1) * sine)
        return jnp.concatenate(out, axis=1)

    q_out[...] = turned(dot(x, wq[...])).astype(BF)
    k_out[...] = turned(dot(x, wk[...])).astype(BF)
    v_out[...] = dot(x, wv[...]).astype(BF)
    part = rows_out.shape[0]
    rows_out[...] = rows[:, pl.ds(pl.multiple_of(pl.program_id(0) * part, part), part)].T


def qkv_slot(order, chunk, rows, w_query, w_key, w_value, cos, sin, held, count):
    t, d = rows.shape
    width = w_query.shape[1]
    bn = min(256, width)
    wspec = pl.BlockSpec((d, bn), lambda i, s: (0, i))
    tspec = pl.BlockSpec((t, HD), lambda i, s: (s[0], 0))
    return call(
        qkv_body,
        name="qkv",
        grid=(width // bn,),
        scalars=1,
        in_specs=[pl.BlockSpec((t, d), lambda i, s: (0, 0)), wspec, wspec, wspec, tspec, tspec]
        + [ANY] * len(held),
        out_specs=[pl.BlockSpec((t, bn), lambda i, s: (s[0], i))] * 3
        + [pl.BlockSpec((d // (width // bn), t), lambda i, s: (i, s[0]))],
        out_shape=[jax.ShapeDtypeStruct((count * t, width), BF)] * 3
        + [jax.ShapeDtypeStruct((d, count * t), BF)],
        aliases={7 + i: i for i in range(len(held))},
    )(order, chunk, rows, w_query, w_key, w_value, cos, sin, *held)


def attend_consts(seq_len):
    to_log2 = math.log2(math.e)
    return (to_log2 / math.sqrt(HD), math.log2(seq_len))


def attend_body(docs, q_ref, k_ref, v_ref, ids_col, ids_row, mix, acc, *, block):
    seq_len = q_ref.shape[0]
    scale, shift = attend_consts(seq_len)
    causal = lax.broadcasted_iota(jnp.int32, (block, block), 0) >= lax.broadcasted_iota(
        jnp.int32, (block, block), 1
    )

    def term(i, j):
        q = q_ref[i * block : (i + 1) * block, :]
        k = k_ref[j * block : (j + 1) * block, :]
        sig = 1.0 / (1.0 + jnp.exp2(shift - dot_nt(q, k) * scale))
        same = ids_col[i * block : (i + 1) * block, :] == ids_row[:, j * block : (j + 1) * block]
        allowed = same & causal if i == j else same
        probs = jnp.where(allowed, sig, 0.0).astype(BF)
        return dot(probs, v_ref[j * block : (j + 1) * block, :])

    for i in range(seq_len // block):
        acc[...] = term(i, i)
        for j in range(i):

            @pl.when(docs[(j + 1) * block - 1] == docs[i * block])
            def _():
                acc[...] += term(i, j)

        mix[i * block : (i + 1) * block, :] = acc[...].astype(BF)


def attend(order, docs, q, k, v):
    seq_len, width = q.shape
    block = 256
    head = pl.BlockSpec((seq_len, HD), lambda h, s: (0, h))
    return call(
        functools.partial(attend_body, block=block),
        name="attend",
        grid=(width // HD,),
        scalars=1,
        in_specs=[
            head,
            head,
            head,
            pl.BlockSpec((seq_len, 1), lambda h, s: (0, 0)),
            pl.BlockSpec((1, seq_len), lambda h, s: (0, 0)),
        ],
        out_specs=[head],
        out_shape=[jax.ShapeDtypeStruct((seq_len, width), BF)],
        scratch=[pltpu.VMEM((block, HD), F32)],
    )(order, docs, q, k, v, docs.reshape(-1, 1), docs.reshape(1, -1))


def attend_back_body(
    docs, q_ref, k_ref, v_ref, dmix, ids_col, ids_row, cos, sin, out, dq, dk, dv, *, block
):
    seq_len = q_ref.shape[0]
    scale, shift = attend_consts(seq_len)
    causal = lax.broadcasted_iota(jnp.int32, (block, block), 0) <= lax.broadcasted_iota(
        jnp.int32, (block, block), 1
    )

    def at(i):
        return slice(i * block, (i + 1) * block)

    def term(i, j):
        q, k, v, d = q_ref[at(i), :], k_ref[at(j), :], v_ref[at(j), :], dmix[at(i), :]
        sig = 1.0 / (1.0 + jnp.exp2(shift - dot_nt(k, q) * scale))
        same = ids_col[at(j), :] == ids_row[:, at(i)]
        allowed = same & causal if i == j else same
        probs = jnp.where(allowed, sig, 0.0)
        d_scores = (dot_nt(v, d) * probs * (1.0 - probs)).astype(BF)
        return dot_tn(d_scores, k), dot(d_scores, q), dot(probs.astype(BF), d)

    for i in range(seq_len // block):
        dq[at(i), :], dk[at(i), :], dv[at(i), :] = term(i, i)
    for i in range(seq_len // block):
        for j in range(i):

            @pl.when(docs[(j + 1) * block - 1] == docs[i * block])
            def _():
                a, b, c = term(i, j)
                dq[at(i), :] += a
                dk[at(j), :] += b
                dv[at(j), :] += c

    cosine, sine = cos[...], sin[...]

    def turned_back(v):
        v = v * (1.0 / math.sqrt(HD))
        return (v * cosine - pltpu.roll(v, HD // 2, 1) * sine).astype(BF)

    width = out.shape[1] // 3
    at_head = pl.program_id(0) * HD
    for part, value in enumerate((turned_back(dq[...]), turned_back(dk[...]), dv[...].astype(BF))):
        out[:, pl.ds(pl.multiple_of(at_head + part * width, HD), HD)] = value


def attend_back(order, docs, q, k, v, d_mix, cos, sin):
    seq_len, width = q.shape
    head = pl.BlockSpec((seq_len, HD), lambda h, s: (0, h))
    whole = lambda r, c: pl.BlockSpec((r, c), lambda h, s: (0, 0))
    return call(
        functools.partial(attend_back_body, block=256),
        name="attend_back",
        grid=(width // HD,),
        scalars=1,
        in_specs=[head] * 4
        + [whole(seq_len, 1), whole(1, seq_len), whole(seq_len, HD), whole(seq_len, HD)],
        out_specs=[whole(seq_len, 3 * width)],
        out_shape=[jax.ShapeDtypeStruct((seq_len, 3 * width), BF)],
        scratch=[pltpu.VMEM((seq_len, HD), F32)] * 3,
    )(order, docs, q, k, v, d_mix, docs.reshape(-1, 1), docs.reshape(1, -1), cos, sin)


def project_body(mix, w_ref, x_ref, gain, resid, normed, acc):
    parts, _, cols = w_ref.shape
    step = pl.program_id(0)

    @pl.when(step == 0)
    def _():
        acc[...] = x_ref[...].astype(F32)

    for p in range(parts):
        acc[:, p * cols : (p + 1) * cols] += dot(mix[...], w_ref[p])

    @pl.when(step == pl.num_programs(0) - 1)
    def _():
        resid[...] = acc[...]
        normed[...] = rms_scale(acc[...], gain[...]).astype(BF)


def project(order, mix, w_out, x, gain):
    t, d = x.shape
    width = mix.shape[1]
    parts, _, cols = w_out.shape
    whole = lambda r, c: pl.BlockSpec((r, c), lambda i: (0, 0))
    return call(
        project_body,
        name="project",
        grid=(mix.shape[0] // t,),
        scalars=0,
        in_specs=[
            pl.BlockSpec((t, width), lambda i: (i, 0)),
            pl.BlockSpec((parts, width, cols), lambda i: (0, i, 0)),
            whole(t, d),
            whole(1, d),
        ],
        out_specs=[whole(t, d)] * 2,
        out_shape=[jax.ShapeDtypeStruct((t, d), F32), jax.ShapeDtypeStruct((t, d), BF)],
        scratch=[pltpu.VMEM((t, d), F32)],
    )(order, mix, w_out, x, gain.reshape(1, -1))


def norm_back(d_normed, rows, gain):
    r = lax.rsqrt(jnp.mean(rows * rows, axis=-1, keepdims=True) + EPS)
    u = rows * r
    scaled = d_normed * gain
    d_rows = r * (scaled - u * jnp.mean(scaled * u, axis=-1, keepdims=True))
    return d_rows, jnp.sum(d_normed * u, axis=0, keepdims=True)


def middle_body(d_ref, resid, cot, gain, w_ref, out, d_resid, low_t, part, low):
    parts, _, cols = w_ref.shape

    @pl.when(pl.program_id(0) == 0)
    def _():
        d_rows, part[...] = norm_back(d_ref[...].astype(F32), resid[...], gain[...])
        total = cot[...].astype(F32) + d_rows
        d_resid[...] = total
        low[...] = total.astype(BF)
        low_t[...] = low[...].T

    total = None
    for p in range(parts):
        term = dot_nt(low[:, p * cols : (p + 1) * cols], w_ref[p])
        total = term if total is None else total + term
    out[...] = total.astype(BF)


def middle(order, d_normed2, resid, cot, gain, w_out, width):
    t, d = resid.shape
    parts, rows, cols = w_out.shape
    count = rows // width
    whole = lambda r, c: pl.BlockSpec((r, c), lambda i: (0, 0))
    return call(
        middle_body,
        name="middle",
        grid=(count,),
        scalars=0,
        in_specs=[whole(t, d)] * 3
        + [whole(1, d), pl.BlockSpec((parts, width, cols), lambda i: (0, i, 0))],
        out_specs=[
            pl.BlockSpec((t, width), lambda i: (i, 0)),
            whole(t, d),
            whole(d, t),
            whole(1, d),
        ],
        out_shape=[
            jax.ShapeDtypeStruct((count * t, width), BF),
            jax.ShapeDtypeStruct((t, d), F32),
            jax.ShapeDtypeStruct((d, t), BF),
            jax.ShapeDtypeStruct((1, d), F32),
        ],
        scratch=[pltpu.VMEM((t, d), BF)],
    )(order, d_normed2, resid, cot, gain.reshape(1, -1), w_out)


def last_body(d_ref, x_ref, d_resid, gain, out, part):
    d_rows, part[...] = norm_back(d_ref[...].astype(F32), x_ref[...].astype(F32), gain[...])
    out[...] = (d_resid[...] + d_rows).astype(BF)


def last(order, d_normed, x, d_resid, gain):
    t, d = x.shape
    whole = lambda r, c: pl.BlockSpec((r, c), lambda i: (0, 0))
    return call(
        last_body,
        name="last",
        grid=(1,),
        scalars=0,
        in_specs=[whole(t, d)] * 3 + [whole(1, d)],
        out_specs=[whole(t, d), whole(1, d)],
        out_shape=[jax.ShapeDtypeStruct((t, d), BF), jax.ShapeDtypeStruct((1, d), F32)],
    )(order, d_normed, x, d_resid, gain.reshape(1, -1))


def back_project_body(d_ref, wq, wk, wv, out):
    total = None
    width = wq.shape[1]
    for k, w in enumerate((wq, wk, wv)):
        term = dot_nt(d_ref[:, k * width : (k + 1) * width], w[...])
        total = term if total is None else total + term
    out[...] = total.astype(BF)


def back_project(order, d_qkv, w_query, w_key, w_value):
    seq_len, wide = d_qkv.shape
    d, width = w_query.shape
    bn = 512
    wspec = pl.BlockSpec((bn, width), lambda i: (i, 0))
    return call(
        back_project_body,
        name="back_project",
        grid=(d // bn,),
        scalars=0,
        in_specs=[pl.BlockSpec((seq_len, wide), lambda i: (0, 0)), wspec, wspec, wspec],
        out_specs=[pl.BlockSpec((seq_len, bn), lambda i: (0, i))],
        out_shape=[jax.ShapeDtypeStruct((seq_len, d), BF)],
    )(order, d_qkv, w_query, w_key, w_value)[0]


def ffn_body(*refs):
    chunk, rows, cot, wg, wu, wd = refs[:6]
    inner, d_gate, d_up, rows_out, cot_out, d_rows, down, acc_d, acc_o = refs[-9:]
    step, last = pl.program_id(0), pl.num_programs(0) - 1
    x = rows[...]
    gate = dot(x, wg[...])
    up = dot(x, wu[...])
    sig = sigmoid(gate)
    silu = gate * sig
    inner_b = (silu * up).astype(BF)
    inner[...] = inner_b.T
    part = rows_out.shape[0]
    rows_out[...] = rows[:, pl.ds(pl.multiple_of(step * part, part), part)].T
    d_inner = dot_nt(cot[...], wd[...])
    dg = (d_inner * up * (sig * (1.0 + gate * (1.0 - sig)))).astype(BF)
    du = (d_inner * silu).astype(BF)
    d_gate[...] = dg
    d_up[...] = du
    term_o = dot(inner_b, wd[...])
    term_d = dot_nt(dg, wg[...]) + dot_nt(du, wu[...])

    @pl.when(step == 0)
    def _():
        acc_o[...] = term_o
        acc_d[...] = term_d
        cot_out[...] = cot[...]

    @pl.when(step > 0)
    def _():
        acc_o[...] += term_o
        acc_d[...] += term_d

    @pl.when(step == last)
    def _():
        d_rows[...] = acc_d[...].astype(BF)
        down[...] = acc_o[...].astype(BF)


def ffn_slot(order, chunk, rows, cot, w_gate, w_up, w_down, held, count):
    t, d = rows.shape
    hidden = w_gate.shape[1]
    bh = min(512, hidden)
    steps = hidden // bh
    wcol = pl.BlockSpec((d, bh), lambda i, s: (0, i))
    part = pl.BlockSpec((t, bh), lambda i, s: (s[0], i))
    line = pl.BlockSpec((t, d), lambda i, s: (s[0], 0))
    return call(
        ffn_body,
        name="ffn",
        grid=(hidden // bh,),
        scalars=1,
        in_specs=[
            pl.BlockSpec((t, d), lambda i, s: (0, 0)),
            pl.BlockSpec((t, d), lambda i, s: (0, 0)),
            wcol,
            wcol,
            pl.BlockSpec((bh, d), lambda i, s: (i, 0)),
        ]
        + [ANY] * len(held),
        out_specs=[pl.BlockSpec((bh, t), lambda i, s: (i, s[0])), part, part]
        + [pl.BlockSpec((d // steps, t), lambda i, s: (i, s[0])), line, line, line],
        out_shape=[jax.ShapeDtypeStruct((hidden, count * t), BF)]
        + [jax.ShapeDtypeStruct((count * t, hidden), BF)] * 2
        + [jax.ShapeDtypeStruct((d, count * t), BF)]
        + [jax.ShapeDtypeStruct((count * t, d), BF)] * 3,
        scratch=[pltpu.VMEM((t, d), F32)] * 2,
        aliases={6 + i: i for i in range(len(held))},
    )(order, chunk, rows, cot, w_gate, w_up, w_down, *held)


def local(
    layer_in,
    cotangent,
    doc_ids,
    positions,
    attn_gain,
    w_query,
    w_key,
    w_value,
    w_out,
    ffn_gain,
    w_gate,
    w_up,
    w_down,
    *,
    dp,
    tensor,
):
    t, d = layer_in.shape
    width = w_query.shape[1]
    hidden = w_gate.shape[1]
    place = lax.axis_index("tensor")
    chunks = jnp.stack([place ^ j for j in range(tensor)]).astype(jnp.int32)
    chunk = [chunks[j : j + 1] for j in range(tensor)]
    order = Order()

    share = w_out.shape[1] // dp
    w_cols = lax.all_gather(
        cols_at(w_out, lax.axis_index("dp"), share), "tensor", axis=0, tiled=True
    )
    half = HD // 2
    freqs = ROPE_BASE ** (-(jnp.arange(half).astype(F32) * 2.0) / HD)
    angles = positions.astype(F32)[:, None] * freqs[None, :]
    cosine, sine = jnp.cos(angles), jnp.sin(angles)
    cos = jnp.concatenate([cosine, cosine], axis=1)
    sin = jnp.concatenate([-sine, sine], axis=1)

    normed_own = rms_scale(layer_in.astype(F32), attn_gain).astype(BF)
    line = LineGather(normed_own, tensor, place)
    line.step()
    held = []
    for j in range(tensor):
        if 0 < j < tensor - 1:
            line.step(order)
        if j == tensor - 1:
            cots = LineGather(cotangent, tensor, place)
            cots.step(order)
        held = qkv_slot(order, chunk[j], line.slot(j), w_query, w_key, w_value, cos, sin, held, tensor)
        if j == 1:
            (w_cols,) = order.after(w_cols)
            w_out_all = lax.all_gather(w_cols, "dp", axis=0)
    query, key, value, normed_t = held
    (mixed,) = attend(order, doc_ids, query, key, value)
    mix = exchange(mixed)
    cots.step(order)
    resid, normed2_own = project(order, mix, w_out_all, layer_in, ffn_gain)

    weights = (w_gate, w_up, w_down)
    line = LineGather(normed2_own, tensor, place)
    line.step()
    held = ffn_slot(order, chunk[0], line.slot(0), cotangent, *weights, [], tensor)
    for j in range(1, tensor):
        if j < tensor - 1:
            line.step(order)
            if len(cots.ups) < tensor:
                cots.step(order)
        else:
            cots.hold(order)
            line.hold(order)
        held = ffn_slot(order, chunk[j], line.slot(j), cots.slot(j), *weights, held, tensor)
    inner_t, d_gate, d_up, normed2_t, cot_all, d_normed2_part, down_part = held
    d_normed2 = lax.psum_scatter(d_normed2_part, "tensor", scatter_dimension=0, tiled=True)

    first = Gradients([(inner_t, cot_all, [d])], dp)
    wide = Gradients([(normed2_t, d_gate, [hidden]), (normed2_t, d_up, [hidden])], dp)
    more = range(first.bits - 2)

    first.give(order)
    wide.give(order, 0)
    wide.give(order, 1)
    first.keep(order)
    wide.keep(order, 0)
    wide.keep(order, 1)
    first.fold(order)
    for _ in more:
        first.fold(order)
    d_mix, d_resid, d_resid_t, ffn_gain_part = middle(
        order, d_normed2, resid, cotangent, ffn_gain, w_out_all, width
    )
    d_mix = exchange(d_mix)
    d_resid_all = lax.all_gather(d_resid_t, "tensor", axis=0)
    for _ in more:
        first.spread(order)
    wide.fold(order)
    (d_qkv,) = attend_back(order, doc_ids, query, key, value, d_mix, cos, sin)
    attn = Gradients([(normed_t, d_qkv, [width] * 4, d_resid_all, mixed)], dp)
    attn.give(order)
    d_normed = lax.psum_scatter(
        back_project(order, d_qkv, w_query, w_key, w_value),
        "tensor",
        scatter_dimension=0,
        tiled=True,
    )
    first.join(order)
    for _ in more:
        wide.fold(order)
    attn.give(order, second=True)
    attn.keep(order)
    wide.hold(order)
    usual, order.worth = order.worth, 10
    attn.fold(order)
    order.worth = usual
    for _ in more:
        wide.spread(order)
    (down_grad,) = first.finish(order)
    in_grad, attn_gain_part = last(order, d_normed, layer_in, d_resid, attn_gain)
    totals = GainTotals([attn_gain_part, ffn_gain_part], dp, tensor)
    totals.step(order)
    totals.step(order)
    down_sum = lax.psum_scatter(
        order.after(down_part)[0], "tensor", scatter_dimension=0, tiled=True
    )
    totals.step(order)
    attn.hold(order)
    order.worth = 0.3
    wide.hold(order)
    wide.join(order)
    for _ in more:
        attn.fold(order)
    totals.step(order)
    (gate_grad,) = wide.finish(order, 0)
    for _ in more:
        attn.spread(order)
    (up_grad,) = wide.finish(order, 1)
    attn_gain_grad, ffn_gain_grad = totals.split(order)
    attn.join(order)
    query_grad, key_grad, value_grad, out_grad = attn.finish(order)
    layer_out = (resid + down_sum.astype(F32)).astype(BF)
    return (
        layer_out,
        in_grad,
        attn_gain_grad,
        query_grad,
        key_grad,
        value_grad,
        out_grad,
        ffn_gain_grad,
        gate_grad,
        up_grad,
        down_grad,
    )


def solution(mesh):
    rows, cols, lines = P(("dp", "tensor"), None), P(None, "tensor"), P("tensor", None)
    return jax.shard_map(
        functools.partial(local, dp=mesh.shape["dp"], tensor=mesh.shape["tensor"]),
        mesh=mesh,
        in_specs=(
            rows, rows, P("dp"), P("dp"), P(), cols, cols, cols, lines, P(), cols, cols, lines
        ),
        out_specs=(rows, rows, P(), cols, cols, cols, lines, P(), cols, cols, lines),
        check_vma=False,
    )
```

```python
import functools
import math

import jax
import jax.numpy as jnp
from jax import lax
from jax.experimental import pallas as pl
from jax.experimental.pallas import tpu as pltpu
from jax.sharding import PartitionSpec as P

HD = 128
EPS = 1e-05
ROPE_BASE = 500000.0
BF = jnp.bfloat16
F32 = jnp.float32
VMEM = 56 << 20
COST = {
    "give": 8, "give_second": 2.5, "keep": 10, "fold": 4, "spread": 4, "join": 4.5, "finish": 5.5, "middle": 9.5, "attend": 11,
    "attend_back": 17, "back_project": 11, "qkv": 5.6, "project": 8.6, "ffn": 22, "last": 5, "tie": 0.5,
}


def dot(left, right):
    return lax.dot_general(left, right, (((1,), (0,)), ((), ())), preferred_element_type=F32)


def dot_nt(left, right):
    return lax.dot_general(left, right, (((1,), (1,)), ((), ())), preferred_element_type=F32)


def dot_tn(left, right):
    return lax.dot_general(left, right, (((0,), (0,)), ((), ())), preferred_element_type=F32)


def sigmoid(v):
    return 1.0 / (1.0 + jnp.exp(-v))


def rms_scale(values, gain):
    return values * lax.rsqrt(jnp.mean(values * values, axis=-1, keepdims=True) + EPS) * gain


ANY = pl.BlockSpec(memory_space=pl.ANY)
TOKEN = jax.ShapeDtypeStruct((8, 128), F32)


def call(body, *, name, grid, scalars, in_specs, out_specs, out_shape, scratch=(), aliases=None):
    def run(order, *operands):
        tokens = order.take()
        ahead = scalars + len(in_specs)

        def whole(*refs):
            outs = refs[ahead + len(tokens) :]
            body(*refs[:ahead], *outs[: len(out_shape)], *outs[len(out_shape) + 1 :])
            outs[len(out_shape)][...] = jnp.zeros((8, 128), F32)

        *values, token = pl.pallas_call(
            whole,
            grid_spec=pltpu.PrefetchScalarGridSpec(
                num_scalar_prefetch=scalars,
                grid=grid,
                in_specs=list(in_specs) + [ANY] * len(tokens),
                out_specs=list(out_specs) + [pl.BlockSpec((8, 128), lambda *_: (0, 0))],
                scratch_shapes=list(scratch),
            ),
            out_shape=list(out_shape) + [TOKEN],
            input_output_aliases=aliases or {},
            compiler_params=pltpu.CompilerParams(vmem_limit_bytes=VMEM),
            cost_estimate=pl.CostEstimate(flops=int(COST[name] * order.worth * 1e9), bytes_accessed=int(COST[name] * 1e6), transcendentals=0),
            name=name,
        )(*operands, *tokens)
        order.give(token)
        return values

    return run


class Order:
    def __init__(self):
        self.tokens, self.worth = [], 1.3

    def take(self):
        return self.tokens

    def give(self, token):
        self.tokens = [token]

    def after(self, *values):
        return call(
            lambda *refs: None,
            name="tie",
            grid=(1,),
            scalars=0,
            in_specs=[ANY] * len(values),
            out_specs=[ANY] * len(values),
            out_shape=[jax.ShapeDtypeStruct(v.shape, v.dtype) for v in values],
            aliases={i: i for i in range(len(values))},
            )(self, *values)


def xor_pairs(size, mask):
    return [(i, i ^ mask) for i in range(size)]


class LineGather:
    def __init__(self, own, size, place):
        self.size, self.place = size, place
        self.ups, self.downs = [own], [own]

    def step(self, order=None):
        k, size = len(self.ups), self.size
        if order is not None:
            if k == 1:
                self.ups = self.downs = order.after(self.ups[0])
                self.downs = list(self.downs)
            else:
                self.ups[-1], self.downs[-1] = order.after(self.ups[-1], self.downs[-1])
        up, down = self.ups[-1], self.downs[-1]
        self.ups.append(lax.ppermute(up, "tensor", [(i, i + 1) for i in range(k - 1, size - 1)]))
        self.downs.append(lax.ppermute(down, "tensor", [(i + 1, i) for i in range(0, size - k)]))

    def hold(self, order):
        self.ups[-1], self.downs[-1] = order.after(self.ups[-1], self.downs[-1])

    def slot(self, j):
        groups = {}
        for at in range(self.size):
            groups.setdefault((at ^ j) - at, []).append(at)
        value = None
        for off, places in groups.items():
            arr = self.downs[off] if off >= 0 else self.ups[-off]
            if value is None:
                value = arr
            else:
                here = functools.reduce(jnp.logical_or, [self.place == at for at in places])
                value = jnp.where(here, arr, value)
        return value


def exchange(values):
    return lax.all_to_all(values, "tensor", 0, 0, tiled=True)


def rows_at(values, block, rows):
    return lax.dynamic_slice_in_dim(values, block * rows, rows, axis=0)


def cols_at(values, block, cols):
    return lax.dynamic_slice_in_dim(values, block * cols, cols, axis=1)


def give_body(places, left, right, out):
    out[...] = dot(left[...], right[...]).astype(BF)


def give_second_body(places, left, right, out):
    out[...] = second((left, right), None).astype(BF)


def second(refs, rows):
    left, right = refs
    total, t = None, left.shape[2]
    for k in range(left.shape[0]):
        part = left[k] if rows is None else left[k, rows, :]
        term = dot(part, right[k * t : (k + 1) * t, :])
        total = term if total is None else total + term
    return total


def keep_body(places, *refs, two, last, lanes, chunks):
    ins = 4 if two else 2
    gots, outs = refs[ins : ins + (2 if two else 1)], refs[ins + (2 if two else 1) :]
    step = pl.program_id(0)
    rows = outs[0].shape[0]
    for lane in range(lanes):
        for rel in (1, 0):
            at = pl.multiple_of((places[1 + lane] ^ rel) * rows, rows)
            place = pl.ds(at, rows)
            out = outs[2 * lane + rel]
            inside = (step >= lane * chunks) & (step < (lane + 1) * chunks)

            @pl.when((inside & (step < last)) if two else inside)
            def _():
                total = dot(refs[0][place, :], refs[1][...])
                out[...] = (total + gots[0][place, :].astype(F32)).astype(BF)

            if two and lane == lanes - 1:

                @pl.when(step == last)
                def _():
                    total = second(refs[2:4], place)
                    out[...] = (total + gots[1][place, :].astype(F32)).astype(BF)


def fold_body(places, *refs):
    ins, outs = refs[:4], refs[4:]
    for h in (0, 1):
        total = (ins[2 * h][...].astype(F32) + ins[2 * h + 1][...].astype(F32)).astype(BF)
        if len(outs) == 2:
            outs[h][...] = total
        else:
            for rel in (0, 1):

                @pl.when(pl.program_id(0) == rel)
                def _():
                    outs[2 * h + rel][...] = total


def spread_body(places, *refs):
    ins, outs = refs[:4], refs[4:]
    for k in (0, 1):

        @pl.when(pl.program_id(0) == k)
        def _():
            for h in (0, 1):
                outs[h][...] = ins[2 * h + k][...]


def join_body(places, *refs):
    pieces, out = refs[:-1], refs[-1]
    step = pl.program_id(0) * 2 + pl.program_id(1)
    for k, piece in enumerate(pieces):

        @pl.when(step == k)
        def _():
            out[...] = piece[...]


def finish_body(place, source, *refs, turned, count):
    at, outs = 0, refs[-count:]
    for k, out in enumerate(outs):
        flip = turned and k == count - 1
        width = out.shape[0] if flip else out.shape[1]
        value = source[:, at : at + width].astype(F32)
        out[...] = value.T if flip else value
        at += width


class Product:
    def __init__(self, left, right, widths, firsts, pair=()):
        self.left, self.right, self.widths, self.firsts, self.pair = left, right, widths, firsts, pair
        self.rows = left.shape[0] // 2
        self.cols = right.shape[1] + (pair[1].shape[1] if pair else 0)
        self.bn = min(512, widths[-1])
        self.gots = []


class Gradients:
    def __init__(self, products, count):
        self.count = count
        self.bits = count.bit_length() - 1
        self.index = lax.axis_index("dp")
        self.orders = [list(range(1, self.bits)), list(range(self.bits - 1, 0, -1))]
        self.step = 0
        self.kept, self.gots = [], []
        per = 2 // len(products)
        self.products = [
            Product(*p[:3], [o[0] for o in self.orders[i * per : (i + 1) * per]], p[3:])
            for i, p in enumerate(products)
        ]

    def bit(self, b):
        return (self.index >> b) & 1

    def scalars(self, *values):
        return jnp.stack([jnp.asarray(v, jnp.int32) for v in values])

    def swap(self, value, b):
        return lax.ppermute(value, "dp", xor_pairs(self.count, 1 << b))

    def operands(self, p, core):
        tokens, last = p.right.shape[0], p.right.shape[1] // p.bn
        specs = [
            pl.BlockSpec((p.rows, tokens), lambda n, s: (s[0], 0)),
            pl.BlockSpec((tokens, p.bn), lambda n, s: (0, jnp.minimum(n, last - 1))),
        ]
        if p.pair:
            count, _, t = p.pair[0].shape
            specs += [
                pl.BlockSpec((count, p.rows, t), lambda n, s: (0, s[0], 0)),
                pl.BlockSpec((tokens, p.bn), lambda n, s: (0, 0)),
            ]
        return specs, [p.left, p.right, *p.pair], dict(two=bool(p.pair), last=last)

    def give(self, order, at=0, second=False):
        p = self.products[at]
        specs, values, facts = self.operands(p, 1 - self.bit(0))
        some = slice(2, 4) if second else slice(0, 2)
        cols = values[some][1].shape[1]
        (out,) = call(
            give_second_body if second else give_body,
            name="give_second" if second else "give",
            grid=(cols // p.bn,),
            scalars=1,
            in_specs=specs[some],
            out_specs=[pl.BlockSpec((p.rows, p.bn), lambda n, s: (0, n))],
            out_shape=[jax.ShapeDtypeStruct((p.rows, cols), BF)],
        )(order, self.scalars(1 - self.bit(0)), *values[some])
        p.gots.append(self.swap(out, 0))

    def keep(self, order, at=0):
        p = self.products[at]
        lanes = len(p.firsts)
        rows, cols = p.rows // 2, p.cols // lanes
        chunks = cols // p.bn
        specs, values, facts = self.operands(p, self.bit(0))

        def out_spec(lane):
            return pl.BlockSpec(
                (rows, p.bn), lambda n, s: (0, jnp.clip(n - lane * chunks, 0, chunks - 1))
            )

        outs = call(
            functools.partial(keep_body, lanes=lanes, chunks=chunks, **facts),
            name="keep",
            grid=(lanes * chunks,),
            scalars=1,
            in_specs=specs
            + [
                pl.BlockSpec((p.rows, p.bn), lambda n, s: (0, jnp.minimum(n, facts["last"] - 1))),
                pl.BlockSpec((p.rows, p.bn), lambda n, s: (0, 0)),
            ][: len(p.gots)],
            out_specs=[out_spec(k // 2) for k in range(2 * lanes)],
            out_shape=[jax.ShapeDtypeStruct((rows, cols), BF)] * (2 * lanes),
        )(order, self.scalars(self.bit(0), *[self.bit(b) for b in p.firsts]), *values, *p.gots)
        for h in range(lanes):
            self.kept.append(outs[2 * h])
            self.gots.append(self.swap(outs[2 * h + 1], p.firsts[h]))

    def fold(self, order):
        rows, cols = self.kept[0].shape
        self.step += 1
        more = self.step < self.bits - 1
        nexts = [self.bit(o[self.step]) for o in self.orders] if more else [0, 0]
        orows = rows // 2 if more else rows
        spec = lambda h: pl.BlockSpec((orows, cols), lambda r, s: (s[h] ^ r, 0))
        outs = call(
            fold_body,
            name="fold",
            grid=(2 if more else 1,),
            scalars=1,
            in_specs=[spec(0), spec(0), spec(1), spec(1)],
            out_specs=[pl.BlockSpec((orows, cols), lambda r, s: (0, 0))] * (4 if more else 2),
            out_shape=[jax.ShapeDtypeStruct((orows, cols), BF)] * (4 if more else 2),
        )(order, self.scalars(*nexts), self.kept[0], self.gots[0], self.kept[1], self.gots[1])
        self.kept = outs[:: 2 if more else 1]
        if more:
            self.gots = [self.swap(outs[1 + 2 * h], self.orders[h][self.step]) for h in (0, 1)]
        else:
            self.ask()

    def hold(self, order):
        self.gots = order.after(*self.gots)

    def ask(self):
        self.step -= 1
        self.gots = [self.swap(k, o[self.step]) for k, o in zip(self.kept, self.orders)]

    def spread(self, order):
        rows, cols = self.kept[0].shape
        spec = pl.BlockSpec((rows, cols), lambda k, s: (0, 0))
        self.kept = call(
            spread_body,
            name="spread",
            grid=(2,),
            scalars=1,
            in_specs=[spec] * 4,
            out_specs=[
                pl.BlockSpec((rows, cols), lambda k, s: (k ^ s[0], 0)),
                pl.BlockSpec((rows, cols), lambda k, s: (k ^ s[1], 0)),
            ],
            out_shape=[jax.ShapeDtypeStruct((2 * rows, cols), BF)] * 2,
        )(
            order,
            self.scalars(*[self.bit(o[self.step]) for o in self.orders]),
            self.kept[0],
            self.gots[0],
            self.kept[1],
            self.gots[1],
        )
        self.ask()

    def join(self, order):
        brows, bcols = self.kept[0].shape
        lane = 0
        for p in self.products:
            lanes = range(lane, lane + len(p.firsts))
            lane += len(p.firsts)
            (p.half,) = call(
                join_body,
                name="join",
                grid=(len(lanes), 2),
                scalars=1,
                in_specs=[pl.BlockSpec((brows, bcols), lambda h, k, s: (0, 0))] * (2 * len(lanes)),
                out_specs=[pl.BlockSpec((brows, bcols), lambda h, k, s: (k ^ s[h], h))],
                out_shape=[jax.ShapeDtypeStruct((p.rows, p.cols), BF)],
            )(
                order,
                self.scalars(*[self.bit(self.orders[l][self.step]) for l in lanes]),
                *[v for l in lanes for v in (self.kept[l], self.gots[l])],
            )
            p.other = self.swap(p.half, 0)

    def finish(self, order, at=0):
        outs = self.fill(order, at, 0)
        return self.fill(order, at, 1, outs)

    def fill(self, order, at, other, ahead=()):
        p = self.products[at]
        rows, cols = p.half.shape
        crows = min(256, rows)
        nblk = rows // crows
        turned = bool(p.pair)
        specs = [pl.BlockSpec((crows, w), lambda b, s: (s[0] * nblk + b, 0)) for w in p.widths]
        shapes = [jax.ShapeDtypeStruct((2 * rows, w), F32) for w in p.widths]
        if turned:
            w = p.widths[-1]
            specs[-1] = pl.BlockSpec((w, crows), lambda b, s: (0, s[0] * nblk + b))
            shapes[-1] = jax.ShapeDtypeStruct((w, 2 * rows), F32)
        return call(
            functools.partial(finish_body, turned=turned, count=len(specs)),
            name="finish",
            grid=(nblk,),
            scalars=1,
            in_specs=[pl.BlockSpec((crows, cols), lambda b, s: (b, 0))] + [ANY] * len(ahead),
            out_specs=specs,
            out_shape=shapes,
            aliases={2 + k: k for k in range(len(ahead))},
        )(order, self.scalars(self.bit(0) ^ other), p.other if other else p.half, *ahead)


class GainTotals:
    def __init__(self, parts, dp, tensor):
        self.size = parts[0].size
        self.value = jnp.concatenate([p.reshape(-1, 128) for p in parts], axis=0)
        self.left = [
            (name, size, [1 << k])
            for name, size in (("tensor", tensor), ("dp", dp))
            for k in range(size.bit_length() - 1)
        ]
        self.next()

    def next(self):
        name, size, masks = self.left.pop(0)
        self.got = [lax.ppermute(self.value, name, xor_pairs(size, m)) for m in masks]

    def step(self, order):
        self.value, *got = order.after(self.value, *self.got)
        self.value = self.value + got[0]
        if self.left:
            self.next()

    def split(self, order):
        while self.left:
            self.step(order)
        self.step(order)
        value = self.value.reshape(-1)
        return [value[k : k + self.size] for k in range(0, value.size, self.size)]


def qkv_body(*refs):
    chunk, rows, wq, wk, wv, cos, sin = refs[:7]
    q_out, k_out, v_out, rows_out = refs[-4:]
    x = rows[...]
    cosine, sine = cos[...], sin[...]

    def turned(pre):
        out = []
        for h in range(pre.shape[1] // HD):
            one = pre[:, h * HD : (h + 1) * HD]
            out.append(one * cosine + pltpu.roll(one, HD // 2, 1) * sine)
        return jnp.concatenate(out, axis=1)

    q_out[...] = turned(dot(x, wq[...])).astype(BF)
    k_out[...] = turned(dot(x, wk[...])).astype(BF)
    v_out[...] = dot(x, wv[...]).astype(BF)
    part = rows_out.shape[0]
    rows_out[...] = rows[:, pl.ds(pl.multiple_of(pl.program_id(0) * part, part), part)].T


def qkv_slot(order, chunk, rows, w_query, w_key, w_value, cos, sin, held, count):
    t, d = rows.shape
    width = w_query.shape[1]
    bn = min(256, width)
    wspec = pl.BlockSpec((d, bn), lambda i, s: (0, i))
    tspec = pl.BlockSpec((t, HD), lambda i, s: (s[0], 0))
    return call(
        qkv_body,
        name="qkv",
        grid=(width // bn,),
        scalars=1,
        in_specs=[pl.BlockSpec((t, d), lambda i, s: (0, 0)), wspec, wspec, wspec, tspec, tspec]
        + [ANY] * len(held),
        out_specs=[pl.BlockSpec((t, bn), lambda i, s: (s[0], i))] * 3
        + [pl.BlockSpec((d // (width // bn), t), lambda i, s: (i, s[0]))],
        out_shape=[jax.ShapeDtypeStruct((count * t, width), BF)] * 3
        + [jax.ShapeDtypeStruct((d, count * t), BF)],
        aliases={7 + i: i for i in range(len(held))},
    )(order, chunk, rows, w_query, w_key, w_value, cos, sin, *held)


def attend_consts(seq_len):
    to_log2 = math.log2(math.e)
    return (to_log2 / math.sqrt(HD), math.log2(seq_len))


def attend_body(docs, q_ref, k_ref, v_ref, ids_col, ids_row, mix, acc, *, block):
    seq_len = q_ref.shape[0]
    scale, shift = attend_consts(seq_len)
    causal = lax.broadcasted_iota(jnp.int32, (block, block), 0) >= lax.broadcasted_iota(
        jnp.int32, (block, block), 1
    )

    def term(i, j):
        q = q_ref[i * block : (i + 1) * block, :]
        k = k_ref[j * block : (j + 1) * block, :]
        sig = 1.0 / (1.0 + jnp.exp2(shift - dot_nt(q, k) * scale))
        same = ids_col[i * block : (i + 1) * block, :] == ids_row[:, j * block : (j + 1) * block]
        allowed = same & causal if i == j else same
        probs = jnp.where(allowed, sig, 0.0).astype(BF)
        return dot(probs, v_ref[j * block : (j + 1) * block, :])

    for i in range(seq_len // block):
        acc[...] = term(i, i)
        for j in range(i):

            @pl.when(docs[(j + 1) * block - 1] == docs[i * block])
            def _():
                acc[...] += term(i, j)

        mix[i * block : (i + 1) * block, :] = acc[...].astype(BF)


def attend(order, docs, q, k, v):
    seq_len, width = q.shape
    block = 256
    head = pl.BlockSpec((seq_len, HD), lambda h, s: (0, h))
    return call(
        functools.partial(attend_body, block=block),
        name="attend",
        grid=(width // HD,),
        scalars=1,
        in_specs=[
            head,
            head,
            head,
            pl.BlockSpec((seq_len, 1), lambda h, s: (0, 0)),
            pl.BlockSpec((1, seq_len), lambda h, s: (0, 0)),
        ],
        out_specs=[head],
        out_shape=[jax.ShapeDtypeStruct((seq_len, width), BF)],
        scratch=[pltpu.VMEM((block, HD), F32)],
    )(order, docs, q, k, v, docs.reshape(-1, 1), docs.reshape(1, -1))


def attend_back_body(
    docs, q_ref, k_ref, v_ref, dmix, ids_col, ids_row, cos, sin, out, dq, dk, dv, *, block
):
    seq_len = q_ref.shape[0]
    scale, shift = attend_consts(seq_len)
    causal = lax.broadcasted_iota(jnp.int32, (block, block), 0) <= lax.broadcasted_iota(
        jnp.int32, (block, block), 1
    )

    def at(i):
        return slice(i * block, (i + 1) * block)

    def term(i, j):
        q, k, v, d = q_ref[at(i), :], k_ref[at(j), :], v_ref[at(j), :], dmix[at(i), :]
        sig = 1.0 / (1.0 + jnp.exp2(shift - dot_nt(k, q) * scale))
        same = ids_col[at(j), :] == ids_row[:, at(i)]
        allowed = same & causal if i == j else same
        probs = jnp.where(allowed, sig, 0.0)
        d_scores = (dot_nt(v, d) * probs * (1.0 - probs)).astype(BF)
        return dot_tn(d_scores, k), dot(d_scores, q), dot(probs.astype(BF), d)

    for i in range(seq_len // block):
        dq[at(i), :], dk[at(i), :], dv[at(i), :] = term(i, i)
    for i in range(seq_len // block):
        for j in range(i):

            @pl.when(docs[(j + 1) * block - 1] == docs[i * block])
            def _():
                a, b, c = term(i, j)
                dq[at(i), :] += a
                dk[at(j), :] += b
                dv[at(j), :] += c

    cosine, sine = cos[...], sin[...]

    def turned_back(v):
        v = v * (1.0 / math.sqrt(HD))
        return (v * cosine - pltpu.roll(v, HD // 2, 1) * sine).astype(BF)

    width = out.shape[1] // 3
    at_head = pl.program_id(0) * HD
    for part, value in enumerate((turned_back(dq[...]), turned_back(dk[...]), dv[...].astype(BF))):
        out[:, pl.ds(pl.multiple_of(at_head + part * width, HD), HD)] = value


def attend_back(order, docs, q, k, v, d_mix, cos, sin):
    seq_len, width = q.shape
    head = pl.BlockSpec((seq_len, HD), lambda h, s: (0, h))
    whole = lambda r, c: pl.BlockSpec((r, c), lambda h, s: (0, 0))
    return call(
        functools.partial(attend_back_body, block=256),
        name="attend_back",
        grid=(width // HD,),
        scalars=1,
        in_specs=[head] * 4
        + [whole(seq_len, 1), whole(1, seq_len), whole(seq_len, HD), whole(seq_len, HD)],
        out_specs=[whole(seq_len, 3 * width)],
        out_shape=[jax.ShapeDtypeStruct((seq_len, 3 * width), BF)],
        scratch=[pltpu.VMEM((seq_len, HD), F32)] * 3,
    )(order, docs, q, k, v, d_mix, docs.reshape(-1, 1), docs.reshape(1, -1), cos, sin)


def project_body(mix, w_ref, x_ref, gain, resid, normed, acc):
    parts, _, cols = w_ref.shape
    step = pl.program_id(0)

    @pl.when(step == 0)
    def _():
        acc[...] = x_ref[...].astype(F32)

    for p in range(parts):
        acc[:, p * cols : (p + 1) * cols] += dot(mix[...], w_ref[p])

    @pl.when(step == pl.num_programs(0) - 1)
    def _():
        resid[...] = acc[...]
        normed[...] = rms_scale(acc[...], gain[...]).astype(BF)


def project(order, mix, w_out, x, gain):
    t, d = x.shape
    width = mix.shape[1]
    parts, _, cols = w_out.shape
    whole = lambda r, c: pl.BlockSpec((r, c), lambda i: (0, 0))
    return call(
        project_body,
        name="project",
        grid=(mix.shape[0] // t,),
        scalars=0,
        in_specs=[
            pl.BlockSpec((t, width), lambda i: (i, 0)),
            pl.BlockSpec((parts, width, cols), lambda i: (0, i, 0)),
            whole(t, d),
            whole(1, d),
        ],
        out_specs=[whole(t, d)] * 2,
        out_shape=[jax.ShapeDtypeStruct((t, d), F32), jax.ShapeDtypeStruct((t, d), BF)],
        scratch=[pltpu.VMEM((t, d), F32)],
    )(order, mix, w_out, x, gain.reshape(1, -1))


def norm_back(d_normed, rows, gain):
    r = lax.rsqrt(jnp.mean(rows * rows, axis=-1, keepdims=True) + EPS)
    u = rows * r
    scaled = d_normed * gain
    d_rows = r * (scaled - u * jnp.mean(scaled * u, axis=-1, keepdims=True))
    return d_rows, jnp.sum(d_normed * u, axis=0, keepdims=True)


def middle_body(d_ref, resid, cot, gain, w_ref, out, d_resid, low_t, part, low):
    parts, _, cols = w_ref.shape

    @pl.when(pl.program_id(0) == 0)
    def _():
        d_rows, part[...] = norm_back(d_ref[...].astype(F32), resid[...], gain[...])
        total = cot[...].astype(F32) + d_rows
        d_resid[...] = total
        low[...] = total.astype(BF)
        low_t[...] = low[...].T

    total = None
    for p in range(parts):
        term = dot_nt(low[:, p * cols : (p + 1) * cols], w_ref[p])
        total = term if total is None else total + term
    out[...] = total.astype(BF)


def middle(order, d_normed2, resid, cot, gain, w_out, width):
    t, d = resid.shape
    parts, rows, cols = w_out.shape
    count = rows // width
    whole = lambda r, c: pl.BlockSpec((r, c), lambda i: (0, 0))
    return call(
        middle_body,
        name="middle",
        grid=(count,),
        scalars=0,
        in_specs=[whole(t, d)] * 3
        + [whole(1, d), pl.BlockSpec((parts, width, cols), lambda i: (0, i, 0))],
        out_specs=[
            pl.BlockSpec((t, width), lambda i: (i, 0)),
            whole(t, d),
            whole(d, t),
            whole(1, d),
        ],
        out_shape=[
            jax.ShapeDtypeStruct((count * t, width), BF),
            jax.ShapeDtypeStruct((t, d), F32),
            jax.ShapeDtypeStruct((d, t), BF),
            jax.ShapeDtypeStruct((1, d), F32),
        ],
        scratch=[pltpu.VMEM((t, d), BF)],
    )(order, d_normed2, resid, cot, gain.reshape(1, -1), w_out)


def last_body(d_ref, x_ref, d_resid, gain, out, part):
    d_rows, part[...] = norm_back(d_ref[...].astype(F32), x_ref[...].astype(F32), gain[...])
    out[...] = (d_resid[...] + d_rows).astype(BF)


def last(order, d_normed, x, d_resid, gain):
    t, d = x.shape
    whole = lambda r, c: pl.BlockSpec((r, c), lambda i: (0, 0))
    return call(
        last_body,
        name="last",
        grid=(1,),
        scalars=0,
        in_specs=[whole(t, d)] * 3 + [whole(1, d)],
        out_specs=[whole(t, d), whole(1, d)],
        out_shape=[jax.ShapeDtypeStruct((t, d), BF), jax.ShapeDtypeStruct((1, d), F32)],
    )(order, d_normed, x, d_resid, gain.reshape(1, -1))


def back_project_body(d_ref, wq, wk, wv, out):
    total = None
    width = wq.shape[1]
    for k, w in enumerate((wq, wk, wv)):
        term = dot_nt(d_ref[:, k * width : (k + 1) * width], w[...])
        total = term if total is None else total + term
    out[...] = total.astype(BF)


def back_project(order, d_qkv, w_query, w_key, w_value):
    seq_len, wide = d_qkv.shape
    d, width = w_query.shape
    bn = 512
    wspec = pl.BlockSpec((bn, width), lambda i: (i, 0))
    return call(
        back_project_body,
        name="back_project",
        grid=(d // bn,),
        scalars=0,
        in_specs=[pl.BlockSpec((seq_len, wide), lambda i: (0, 0)), wspec, wspec, wspec],
        out_specs=[pl.BlockSpec((seq_len, bn), lambda i: (0, i))],
        out_shape=[jax.ShapeDtypeStruct((seq_len, d), BF)],
    )(order, d_qkv, w_query, w_key, w_value)[0]


def ffn_body(*refs):
    chunk, rows, cot, wg, wu, wd = refs[:6]
    inner, d_gate, d_up, rows_out, cot_out, d_rows, down, acc_d, acc_o = refs[-9:]
    step, last = pl.program_id(0), pl.num_programs(0) - 1
    x = rows[...]
    gate = dot(x, wg[...])
    up = dot(x, wu[...])
    sig = sigmoid(gate)
    silu = gate * sig
    inner_b = (silu * up).astype(BF)
    inner[...] = inner_b.T
    part = rows_out.shape[0]
    rows_out[...] = rows[:, pl.ds(pl.multiple_of(step * part, part), part)].T
    d_inner = dot_nt(cot[...], wd[...])
    dg = (d_inner * up * (sig * (1.0 + gate * (1.0 - sig)))).astype(BF)
    du = (d_inner * silu).astype(BF)
    d_gate[...] = dg
    d_up[...] = du
    term_o = dot(inner_b, wd[...])
    term_d = dot_nt(dg, wg[...]) + dot_nt(du, wu[...])

    @pl.when(step == 0)
    def _():
        acc_o[...] = term_o
        acc_d[...] = term_d
        cot_out[...] = cot[...]

    @pl.when(step > 0)
    def _():
        acc_o[...] += term_o
        acc_d[...] += term_d

    @pl.when(step == last)
    def _():
        d_rows[...] = acc_d[...].astype(BF)
        down[...] = acc_o[...].astype(BF)


def ffn_slot(order, chunk, rows, cot, w_gate, w_up, w_down, held, count):
    t, d = rows.shape
    hidden = w_gate.shape[1]
    bh = min(512, hidden)
    steps = hidden // bh
    wcol = pl.BlockSpec((d, bh), lambda i, s: (0, i))
    part = pl.BlockSpec((t, bh), lambda i, s: (s[0], i))
    line = pl.BlockSpec((t, d), lambda i, s: (s[0], 0))
    return call(
        ffn_body,
        name="ffn",
        grid=(hidden // bh,),
        scalars=1,
        in_specs=[
            pl.BlockSpec((t, d), lambda i, s: (0, 0)),
            pl.BlockSpec((t, d), lambda i, s: (0, 0)),
            wcol,
            wcol,
            pl.BlockSpec((bh, d), lambda i, s: (i, 0)),
        ]
        + [ANY] * len(held),
        out_specs=[pl.BlockSpec((bh, t), lambda i, s: (i, s[0])), part, part]
        + [pl.BlockSpec((d // steps, t), lambda i, s: (i, s[0])), line, line, line],
        out_shape=[jax.ShapeDtypeStruct((hidden, count * t), BF)]
        + [jax.ShapeDtypeStruct((count * t, hidden), BF)] * 2
        + [jax.ShapeDtypeStruct((d, count * t), BF)]
        + [jax.ShapeDtypeStruct((count * t, d), BF)] * 3,
        scratch=[pltpu.VMEM((t, d), F32)] * 2,
        aliases={6 + i: i for i in range(len(held))},
    )(order, chunk, rows, cot, w_gate, w_up, w_down, *held)


def local(
    layer_in,
    cotangent,
    doc_ids,
    positions,
    attn_gain,
    w_query,
    w_key,
    w_value,
    w_out,
    ffn_gain,
    w_gate,
    w_up,
    w_down,
    *,
    dp,
    tensor,
):
    t, d = layer_in.shape
    width = w_query.shape[1]
    hidden = w_gate.shape[1]
    place = lax.axis_index("tensor")
    chunks = jnp.stack([place ^ j for j in range(tensor)]).astype(jnp.int32)
    chunk = [chunks[j : j + 1] for j in range(tensor)]
    order = Order()

    share = w_out.shape[1] // dp
    w_cols = lax.all_gather(
        cols_at(w_out, lax.axis_index("dp"), share), "tensor", axis=0, tiled=True
    )
    half = HD // 2
    freqs = ROPE_BASE ** (-(jnp.arange(half).astype(F32) * 2.0) / HD)
    angles = positions.astype(F32)[:, None] * freqs[None, :]
    cosine, sine = jnp.cos(angles), jnp.sin(angles)
    cos = jnp.concatenate([cosine, cosine], axis=1)
    sin = jnp.concatenate([-sine, sine], axis=1)

    normed_own = rms_scale(layer_in.astype(F32), attn_gain).astype(BF)
    line = LineGather(normed_own, tensor, place)
    line.step()
    held = []
    for j in range(tensor):
        if 0 < j < tensor - 1:
            line.step(order)
        if j == tensor - 1:
            cots = LineGather(cotangent, tensor, place)
            cots.step(order)
        usual, order.worth = order.worth, 20 if j == tensor - 1 else order.worth
        held = qkv_slot(order, chunk[j], line.slot(j), w_query, w_key, w_value, cos, sin, held, tensor)
        order.worth = usual
        if j == min(2, tensor - 1):
            (w_cols,) = order.after(w_cols)
            w_out_all = lax.all_gather(w_cols, "dp", axis=0)
    query, key, value, normed_t = held
    cots.step(order)
    (mixed,) = attend(order, doc_ids, query, key, value)
    mix = exchange(mixed)
    cot_slots = list(order.after(cots.slot(1)))
    cots.step(order)
    cot_slots += order.after(cots.slot(2))
    resid, normed2_own = project(order, mix, w_out_all, layer_in, ffn_gain)

    weights = (w_gate, w_up, w_down)
    line = LineGather(normed2_own, tensor, place)
    line.step()
    held = ffn_slot(order, chunk[0], line.slot(0), cotangent, *weights, [], tensor)
    for j in range(1, tensor):
        if j < tensor - 1:
            line.step(order)
            if len(cots.ups) < tensor:
                cots.step(order)
        else:
            cots.hold(order)
            line.hold(order)
        cot = cot_slots[j - 1] if j < 3 else cots.slot(j)
        held = ffn_slot(order, chunk[j], line.slot(j), cot, *weights, held, tensor)
    inner_t, d_gate, d_up, normed2_t, cot_all, d_normed2_part, down_part = held
    d_normed2 = lax.psum_scatter(d_normed2_part, "tensor", scatter_dimension=0, tiled=True)

    first = Gradients([(inner_t, cot_all, [d])], dp)
    wide = Gradients([(normed2_t, d_gate, [hidden]), (normed2_t, d_up, [hidden])], dp)
    more = range(first.bits - 2)

    first.give(order)
    wide.give(order, 0)
    wide.give(order, 1)
    first.keep(order)
    wide.keep(order, 0)
    wide.keep(order, 1)
    first.fold(order)
    for _ in more:
        first.fold(order)
    d_mix, d_resid, d_resid_t, ffn_gain_part = middle(
        order, d_normed2, resid, cotangent, ffn_gain, w_out_all, width
    )
    d_mix = exchange(d_mix)
    d_resid_all = lax.all_gather(d_resid_t, "tensor", axis=0)
    for _ in more:
        first.spread(order)
    wide.fold(order)
    (d_qkv,) = attend_back(order, doc_ids, query, key, value, d_mix, cos, sin)
    attn = Gradients([(normed_t, d_qkv, [width] * 4, d_resid_all, mixed)], dp)
    attn.give(order)
    d_normed = lax.psum_scatter(
        back_project(order, d_qkv, w_query, w_key, w_value),
        "tensor",
        scatter_dimension=0,
        tiled=True,
    )
    first.join(order)
    for _ in more:
        wide.fold(order)
    attn.give(order, second=True)
    attn.keep(order)
    wide.hold(order)
    usual, order.worth = order.worth, 10
    attn.fold(order)
    order.worth = usual
    for _ in more:
        wide.spread(order)
    for _ in more:
        attn.fold(order)
    down_sum = lax.psum_scatter(
        order.after(down_part)[0], "tensor", scatter_dimension=0, tiled=True
    )
    (down_grad,) = first.finish(order)
    in_grad, attn_gain_part = last(order, d_normed, layer_in, d_resid, attn_gain)
    totals = GainTotals([attn_gain_part, ffn_gain_part], dp, tensor)
    totals.step(order)
    totals.step(order)
    totals.step(order)
    wide.hold(order)
    order.worth = 0.3
    wide.join(order)
    attn.hold(order)
    order.worth = 0.3
    for _ in more:
        attn.spread(order)
    order.worth = 0.3
    (gate_grad,) = wide.finish(order, 0)
    (up_grad,) = wide.finish(order, 1)
    (down_sum,) = order.after(down_sum)
    attn.join(order)
    totals.step(order)
    attn_grads = attn.fill(order, 0, 0)
    attn_gain_grad, ffn_gain_grad = totals.split(order)
    query_grad, key_grad, value_grad, out_grad = attn.fill(order, 0, 1, attn_grads)
    layer_out = (resid + down_sum.astype(F32)).astype(BF)
    return (
        layer_out,
        in_grad,
        attn_gain_grad,
        query_grad,
        key_grad,
        value_grad,
        out_grad,
        ffn_gain_grad,
        gate_grad,
        up_grad,
        down_grad,
    )


def solution(mesh):
    rows, cols, lines = P(("dp", "tensor"), None), P(None, "tensor"), P("tensor", None)
    return jax.shard_map(
        functools.partial(local, dp=mesh.shape["dp"], tensor=mesh.shape["tensor"]),
        mesh=mesh,
        in_specs=(
            rows, rows, P("dp"), P("dp"), P(), cols, cols, cols, lines, P(), cols, cols, lines
        ),
        out_specs=(rows, rows, P(), cols, cols, cols, lines, P(), cols, cols, lines),
        check_vma=False,
    )
```

```python
import functools
import math

import jax
import jax.numpy as jnp
from jax import lax
from jax.experimental import pallas as pl
from jax.experimental.pallas import tpu as pltpu
from jax.sharding import PartitionSpec as P

HD = 128
EPS = 1e-05
ROPE_BASE = 500000.0
BF = jnp.bfloat16
F32 = jnp.float32
VMEM = 56 << 20
COST = {
    "give": 8, "give_second": 2.5, "keep": 10, "fold": 4, "spread": 4, "join": 4.5, "finish": 5.5, "middle": 9.5, "attend": 11,
    "attend_back": 17, "back_project": 11, "qkv": 5.6, "project": 8.6, "ffn": 22, "last": 5, "tie": 0.5,
}


def dot(left, right):
    return lax.dot_general(left, right, (((1,), (0,)), ((), ())), preferred_element_type=F32)


def dot_nt(left, right):
    return lax.dot_general(left, right, (((1,), (1,)), ((), ())), preferred_element_type=F32)


def dot_tn(left, right):
    return lax.dot_general(left, right, (((0,), (0,)), ((), ())), preferred_element_type=F32)


def sigmoid(v):
    return 1.0 / (1.0 + jnp.exp(-v))


def rms_scale(values, gain):
    return values * lax.rsqrt(jnp.mean(values * values, axis=-1, keepdims=True) + EPS) * gain


ANY = pl.BlockSpec(memory_space=pl.ANY)
TOKEN = jax.ShapeDtypeStruct((8, 128), F32)


def call(body, *, name, grid, scalars, in_specs, out_specs, out_shape, scratch=(), aliases=None):
    def run(order, *operands):
        tokens = order.take()
        ahead = scalars + len(in_specs)

        def whole(*refs):
            outs = refs[ahead + len(tokens) :]
            body(*refs[:ahead], *outs[: len(out_shape)], *outs[len(out_shape) + 1 :])
            outs[len(out_shape)][...] = jnp.zeros((8, 128), F32)

        *values, token = pl.pallas_call(
            whole,
            grid_spec=pltpu.PrefetchScalarGridSpec(
                num_scalar_prefetch=scalars,
                grid=grid,
                in_specs=list(in_specs) + [ANY] * len(tokens),
                out_specs=list(out_specs) + [pl.BlockSpec((8, 128), lambda *_: (0, 0))],
                scratch_shapes=list(scratch),
            ),
            out_shape=list(out_shape) + [TOKEN],
            input_output_aliases=aliases or {},
            compiler_params=pltpu.CompilerParams(vmem_limit_bytes=VMEM),
            cost_estimate=pl.CostEstimate(flops=int(COST[name] * order.worth * 1e9), bytes_accessed=int(COST[name] * 1e6), transcendentals=0),
            name=name,
        )(*operands, *tokens)
        order.give(token)
        return values

    return run


class Order:
    def __init__(self):
        self.tokens, self.worth = [], 1.3

    def take(self):
        return self.tokens

    def give(self, token):
        self.tokens = [token]

    def after(self, *values):
        return call(
            lambda *refs: None,
            name="tie",
            grid=(1,),
            scalars=0,
            in_specs=[ANY] * len(values),
            out_specs=[ANY] * len(values),
            out_shape=[jax.ShapeDtypeStruct(v.shape, v.dtype) for v in values],
            aliases={i: i for i in range(len(values))},
            )(self, *values)


def xor_pairs(size, mask):
    return [(i, i ^ mask) for i in range(size)]


class LineGather:
    def __init__(self, own, size, place):
        self.size, self.place = size, place
        self.ups, self.downs = [own], [own]

    def step(self, order=None):
        k, size = len(self.ups), self.size
        if order is not None:
            if k == 1:
                self.ups = self.downs = order.after(self.ups[0])
                self.downs = list(self.downs)
            else:
                self.ups[-1], self.downs[-1] = order.after(self.ups[-1], self.downs[-1])
        up, down = self.ups[-1], self.downs[-1]
        self.ups.append(lax.ppermute(up, "tensor", [(i, i + 1) for i in range(k - 1, size - 1)]))
        self.downs.append(lax.ppermute(down, "tensor", [(i + 1, i) for i in range(0, size - k)]))

    def hold(self, order):
        self.ups[-1], self.downs[-1] = order.after(self.ups[-1], self.downs[-1])

    def slot(self, j):
        groups = {}
        for at in range(self.size):
            groups.setdefault((at ^ j) - at, []).append(at)
        value = None
        for off, places in groups.items():
            arr = self.downs[off] if off >= 0 else self.ups[-off]
            if value is None:
                value = arr
            else:
                here = functools.reduce(jnp.logical_or, [self.place == at for at in places])
                value = jnp.where(here, arr, value)
        return value


def exchange(values):
    return lax.all_to_all(values, "tensor", 0, 0, tiled=True)


def rows_at(values, block, rows):
    return lax.dynamic_slice_in_dim(values, block * rows, rows, axis=0)


def cols_at(values, block, cols):
    return lax.dynamic_slice_in_dim(values, block * cols, cols, axis=1)


def give_body(places, left, right, out):
    out[...] = dot(left[...], right[...]).astype(BF)


def give_second_body(places, left, right, out):
    out[...] = second((left, right), None).astype(BF)


def second(refs, rows):
    left, right = refs
    total, t = None, left.shape[2]
    for k in range(left.shape[0]):
        part = left[k] if rows is None else left[k, rows, :]
        term = dot(part, right[k * t : (k + 1) * t, :])
        total = term if total is None else total + term
    return total


def keep_body(places, *refs, two, last, lanes, chunks):
    ins = 4 if two else 2
    gots, outs = refs[ins : ins + (2 if two else 1)], refs[ins + (2 if two else 1) :]
    step = pl.program_id(0)
    rows = outs[0].shape[0]
    for lane in range(lanes):
        for rel in (1, 0):
            at = pl.multiple_of((places[1 + lane] ^ rel) * rows, rows)
            place = pl.ds(at, rows)
            out = outs[2 * lane + rel]
            inside = (step >= lane * chunks) & (step < (lane + 1) * chunks)

            @pl.when((inside & (step < last)) if two else inside)
            def _():
                total = dot(refs[0][place, :], refs[1][...])
                out[...] = (total + gots[0][place, :].astype(F32)).astype(BF)

            if two and lane == lanes - 1:

                @pl.when(step == last)
                def _():
                    total = second(refs[2:4], place)
                    out[...] = (total + gots[1][place, :].astype(F32)).astype(BF)


def fold_body(places, *refs):
    ins, outs = refs[:4], refs[4:]
    for h in (0, 1):
        total = (ins[2 * h][...].astype(F32) + ins[2 * h + 1][...].astype(F32)).astype(BF)
        if len(outs) == 2:
            outs[h][...] = total
        else:
            for rel in (0, 1):

                @pl.when(pl.program_id(0) == rel)
                def _():
                    outs[2 * h + rel][...] = total


def spread_body(places, *refs):
    ins, outs = refs[:4], refs[4:]
    for k in (0, 1):

        @pl.when(pl.program_id(0) == k)
        def _():
            for h in (0, 1):
                outs[h][...] = ins[2 * h + k][...]


def join_body(places, *refs):
    pieces, out = refs[:-1], refs[-1]
    step = pl.program_id(0) * 2 + pl.program_id(1)
    for k, piece in enumerate(pieces):

        @pl.when(step == k)
        def _():
            out[...] = piece[...]


def finish_body(place, source, *refs, turned, count):
    at, outs = 0, refs[-count:]
    for k, out in enumerate(outs):
        flip = turned and k == count - 1
        width = out.shape[0] if flip else out.shape[1]
        value = source[:, at : at + width].astype(F32)
        out[...] = value.T if flip else value
        at += width


class Product:
    def __init__(self, left, right, widths, firsts, pair=()):
        self.left, self.right, self.widths, self.firsts, self.pair = left, right, widths, firsts, pair
        self.rows = left.shape[0] // 2
        self.cols = right.shape[1] + (pair[1].shape[1] if pair else 0)
        self.bn = min(512, widths[-1])
        self.gots = []


class Gradients:
    def __init__(self, products, count):
        self.count = count
        self.bits = count.bit_length() - 1
        self.index = lax.axis_index("dp")
        self.orders = [list(range(1, self.bits)), list(range(self.bits - 1, 0, -1))]
        self.step = 0
        self.kept, self.gots = [], []
        per = 2 // len(products)
        self.products = [
            Product(*p[:3], [o[0] for o in self.orders[i * per : (i + 1) * per]], p[3:])
            for i, p in enumerate(products)
        ]

    def bit(self, b):
        return (self.index >> b) & 1

    def scalars(self, *values):
        return jnp.stack([jnp.asarray(v, jnp.int32) for v in values])

    def swap(self, value, b):
        return lax.ppermute(value, "dp", xor_pairs(self.count, 1 << b))

    def operands(self, p, core):
        tokens, last = p.right.shape[0], p.right.shape[1] // p.bn
        specs = [
            pl.BlockSpec((p.rows, tokens), lambda n, s: (s[0], 0)),
            pl.BlockSpec((tokens, p.bn), lambda n, s: (0, jnp.minimum(n, last - 1))),
        ]
        if p.pair:
            count, _, t = p.pair[0].shape
            specs += [
                pl.BlockSpec((count, p.rows, t), lambda n, s: (0, s[0], 0)),
                pl.BlockSpec((tokens, p.bn), lambda n, s: (0, 0)),
            ]
        return specs, [p.left, p.right, *p.pair], dict(two=bool(p.pair), last=last)

    def give(self, order, at=0, second=False):
        p = self.products[at]
        specs, values, facts = self.operands(p, 1 - self.bit(0))
        some = slice(2, 4) if second else slice(0, 2)
        cols = values[some][1].shape[1]
        (out,) = call(
            give_second_body if second else give_body,
            name="give_second" if second else "give",
            grid=(cols // p.bn,),
            scalars=1,
            in_specs=specs[some],
            out_specs=[pl.BlockSpec((p.rows, p.bn), lambda n, s: (0, n))],
            out_shape=[jax.ShapeDtypeStruct((p.rows, cols), BF)],
        )(order, self.scalars(1 - self.bit(0)), *values[some])
        p.gots.append(self.swap(out, 0))

    def keep(self, order, at=0):
        p = self.products[at]
        lanes = len(p.firsts)
        rows, cols = p.rows // 2, p.cols // lanes
        chunks = cols // p.bn
        specs, values, facts = self.operands(p, self.bit(0))

        def out_spec(lane):
            return pl.BlockSpec(
                (rows, p.bn), lambda n, s: (0, jnp.clip(n - lane * chunks, 0, chunks - 1))
            )

        outs = call(
            functools.partial(keep_body, lanes=lanes, chunks=chunks, **facts),
            name="keep",
            grid=(lanes * chunks,),
            scalars=1,
            in_specs=specs
            + [
                pl.BlockSpec((p.rows, p.bn), lambda n, s: (0, jnp.minimum(n, facts["last"] - 1))),
                pl.BlockSpec((p.rows, p.bn), lambda n, s: (0, 0)),
            ][: len(p.gots)],
            out_specs=[out_spec(k // 2) for k in range(2 * lanes)],
            out_shape=[jax.ShapeDtypeStruct((rows, cols), BF)] * (2 * lanes),
        )(order, self.scalars(self.bit(0), *[self.bit(b) for b in p.firsts]), *values, *p.gots)
        for h in range(lanes):
            self.kept.append(outs[2 * h])
            self.gots.append(self.swap(outs[2 * h + 1], p.firsts[h]))

    def fold(self, order):
        rows, cols = self.kept[0].shape
        self.step += 1
        more = self.step < self.bits - 1
        nexts = [self.bit(o[self.step]) for o in self.orders] if more else [0, 0]
        orows = rows // 2 if more else rows
        spec = lambda h: pl.BlockSpec((orows, cols), lambda r, s: (s[h] ^ r, 0))
        outs = call(
            fold_body,
            name="fold",
            grid=(2 if more else 1,),
            scalars=1,
            in_specs=[spec(0), spec(0), spec(1), spec(1)],
            out_specs=[pl.BlockSpec((orows, cols), lambda r, s: (0, 0))] * (4 if more else 2),
            out_shape=[jax.ShapeDtypeStruct((orows, cols), BF)] * (4 if more else 2),
        )(order, self.scalars(*nexts), self.kept[0], self.gots[0], self.kept[1], self.gots[1])
        self.kept = outs[:: 2 if more else 1]
        if more:
            self.gots = [self.swap(outs[1 + 2 * h], self.orders[h][self.step]) for h in (0, 1)]
        else:
            self.ask()

    def hold(self, order):
        self.gots = order.after(*self.gots)

    def ask(self):
        self.step -= 1
        self.gots = [self.swap(k, o[self.step]) for k, o in zip(self.kept, self.orders)]

    def spread(self, order):
        rows, cols = self.kept[0].shape
        spec = pl.BlockSpec((rows, cols), lambda k, s: (0, 0))
        self.kept = call(
            spread_body,
            name="spread",
            grid=(2,),
            scalars=1,
            in_specs=[spec] * 4,
            out_specs=[
                pl.BlockSpec((rows, cols), lambda k, s: (k ^ s[0], 0)),
                pl.BlockSpec((rows, cols), lambda k, s: (k ^ s[1], 0)),
            ],
            out_shape=[jax.ShapeDtypeStruct((2 * rows, cols), BF)] * 2,
        )(
            order,
            self.scalars(*[self.bit(o[self.step]) for o in self.orders]),
            self.kept[0],
            self.gots[0],
            self.kept[1],
            self.gots[1],
        )
        self.ask()

    def join(self, order):
        brows, bcols = self.kept[0].shape
        lane = 0
        for p in self.products:
            lanes = range(lane, lane + len(p.firsts))
            lane += len(p.firsts)
            (p.half,) = call(
                join_body,
                name="join",
                grid=(len(lanes), 2),
                scalars=1,
                in_specs=[pl.BlockSpec((brows, bcols), lambda h, k, s: (0, 0))] * (2 * len(lanes)),
                out_specs=[pl.BlockSpec((brows, bcols), lambda h, k, s: (k ^ s[h], h))],
                out_shape=[jax.ShapeDtypeStruct((p.rows, p.cols), BF)],
            )(
                order,
                self.scalars(*[self.bit(self.orders[l][self.step]) for l in lanes]),
                *[v for l in lanes for v in (self.kept[l], self.gots[l])],
            )
            p.other = self.swap(p.half, 0)

    def finish(self, order, at=0):
        outs = self.fill(order, at, 0)
        return self.fill(order, at, 1, outs)

    def fill(self, order, at, other, ahead=()):
        p = self.products[at]
        rows, cols = p.half.shape
        crows = min(256, rows)
        nblk = rows // crows
        turned = bool(p.pair)
        specs = [pl.BlockSpec((crows, w), lambda b, s: (s[0] * nblk + b, 0)) for w in p.widths]
        shapes = [jax.ShapeDtypeStruct((2 * rows, w), F32) for w in p.widths]
        if turned:
            w = p.widths[-1]
            specs[-1] = pl.BlockSpec((w, crows), lambda b, s: (0, s[0] * nblk + b))
            shapes[-1] = jax.ShapeDtypeStruct((w, 2 * rows), F32)
        return call(
            functools.partial(finish_body, turned=turned, count=len(specs)),
            name="finish",
            grid=(nblk,),
            scalars=1,
            in_specs=[pl.BlockSpec((crows, cols), lambda b, s: (b, 0))] + [ANY] * len(ahead),
            out_specs=specs,
            out_shape=shapes,
            aliases={2 + k: k for k in range(len(ahead))},
        )(order, self.scalars(self.bit(0) ^ other), p.other if other else p.half, *ahead)


class GainTotals:
    def __init__(self, parts, dp, tensor):
        self.size = parts[0].size
        self.value = jnp.concatenate([p.reshape(-1, 128) for p in parts], axis=0)
        self.left = [
            (name, size, [1 << k])
            for name, size in (("tensor", tensor), ("dp", dp))
            for k in range(size.bit_length() - 1)
        ]
        self.next()

    def next(self):
        name, size, masks = self.left.pop(0)
        self.got = [lax.ppermute(self.value, name, xor_pairs(size, m)) for m in masks]

    def step(self, order):
        self.value, *got = order.after(self.value, *self.got)
        self.value = self.value + got[0]
        if self.left:
            self.next()

    def split(self, order):
        while self.left:
            self.step(order)
        self.step(order)
        value = self.value.reshape(-1)
        return [value[k : k + self.size] for k in range(0, value.size, self.size)]


def qkv_body(*refs):
    chunk, rows, wq, wk, wv, cos, sin = refs[:7]
    q_out, k_out, v_out, rows_out = refs[-4:]
    x = rows[...]
    cosine, sine = cos[...], sin[...]

    def turned(pre):
        out = []
        for h in range(pre.shape[1] // HD):
            one = pre[:, h * HD : (h + 1) * HD]
            out.append(one * cosine + pltpu.roll(one, HD // 2, 1) * sine)
        return jnp.concatenate(out, axis=1)

    q_out[...] = turned(dot(x, wq[...])).astype(BF)
    k_out[...] = turned(dot(x, wk[...])).astype(BF)
    v_out[...] = dot(x, wv[...]).astype(BF)
    part = rows_out.shape[0]
    rows_out[...] = rows[:, pl.ds(pl.multiple_of(pl.program_id(0) * part, part), part)].T


def qkv_slot(order, chunk, rows, w_query, w_key, w_value, cos, sin, held, count):
    t, d = rows.shape
    width = w_query.shape[1]
    bn = min(256, width)
    wspec = pl.BlockSpec((d, bn), lambda i, s: (0, i))
    tspec = pl.BlockSpec((t, HD), lambda i, s: (s[0], 0))
    return call(
        qkv_body,
        name="qkv",
        grid=(width // bn,),
        scalars=1,
        in_specs=[pl.BlockSpec((t, d), lambda i, s: (0, 0)), wspec, wspec, wspec, tspec, tspec]
        + [ANY] * len(held),
        out_specs=[pl.BlockSpec((t, bn), lambda i, s: (s[0], i))] * 3
        + [pl.BlockSpec((d // (width // bn), t), lambda i, s: (i, s[0]))],
        out_shape=[jax.ShapeDtypeStruct((count * t, width), BF)] * 3
        + [jax.ShapeDtypeStruct((d, count * t), BF)],
        aliases={7 + i: i for i in range(len(held))},
    )(order, chunk, rows, w_query, w_key, w_value, cos, sin, *held)


def attend_consts(seq_len):
    to_log2 = math.log2(math.e)
    return (to_log2 / math.sqrt(HD), math.log2(seq_len))


def attend_body(docs, q_ref, k_ref, v_ref, ids_col, ids_row, mix, acc, *, block):
    seq_len = q_ref.shape[0]
    scale, shift = attend_consts(seq_len)
    causal = lax.broadcasted_iota(jnp.int32, (block, block), 0) >= lax.broadcasted_iota(
        jnp.int32, (block, block), 1
    )

    def term(i, j):
        q = q_ref[i * block : (i + 1) * block, :]
        k = k_ref[j * block : (j + 1) * block, :]
        sig = 1.0 / (1.0 + jnp.exp2(shift - dot_nt(q, k) * scale))
        same = ids_col[i * block : (i + 1) * block, :] == ids_row[:, j * block : (j + 1) * block]
        allowed = same & causal if i == j else same
        probs = jnp.where(allowed, sig, 0.0).astype(BF)
        return dot(probs, v_ref[j * block : (j + 1) * block, :])

    for i in range(seq_len // block):
        acc[...] = term(i, i)
        for j in range(i):

            @pl.when(docs[(j + 1) * block - 1] == docs[i * block])
            def _():
                acc[...] += term(i, j)

        mix[i * block : (i + 1) * block, :] = acc[...].astype(BF)


def attend(order, docs, q, k, v):
    seq_len, width = q.shape
    block = 256
    head = pl.BlockSpec((seq_len, HD), lambda h, s: (0, h))
    return call(
        functools.partial(attend_body, block=block),
        name="attend",
        grid=(width // HD,),
        scalars=1,
        in_specs=[
            head,
            head,
            head,
            pl.BlockSpec((seq_len, 1), lambda h, s: (0, 0)),
            pl.BlockSpec((1, seq_len), lambda h, s: (0, 0)),
        ],
        out_specs=[head],
        out_shape=[jax.ShapeDtypeStruct((seq_len, width), BF)],
        scratch=[pltpu.VMEM((block, HD), F32)],
    )(order, docs, q, k, v, docs.reshape(-1, 1), docs.reshape(1, -1))


def attend_back_body(
    docs, q_ref, k_ref, v_ref, dmix, ids_col, ids_row, cos, sin, out, dq, dk, dv, *, block
):
    seq_len = q_ref.shape[0]
    scale, shift = attend_consts(seq_len)
    causal = lax.broadcasted_iota(jnp.int32, (block, block), 0) <= lax.broadcasted_iota(
        jnp.int32, (block, block), 1
    )

    def at(i):
        return slice(i * block, (i + 1) * block)

    def term(i, j):
        q, k, v, d = q_ref[at(i), :], k_ref[at(j), :], v_ref[at(j), :], dmix[at(i), :]
        sig = 1.0 / (1.0 + jnp.exp2(shift - dot_nt(k, q) * scale))
        same = ids_col[at(j), :] == ids_row[:, at(i)]
        allowed = same & causal if i == j else same
        probs = jnp.where(allowed, sig, 0.0)
        d_scores = (dot_nt(v, d) * probs * (1.0 - probs)).astype(BF)
        return dot_tn(d_scores, k), dot(d_scores, q), dot(probs.astype(BF), d)

    for i in range(seq_len // block):
        dq[at(i), :], dk[at(i), :], dv[at(i), :] = term(i, i)
    for i in range(seq_len // block):
        for j in range(i):

            @pl.when(docs[(j + 1) * block - 1] == docs[i * block])
            def _():
                a, b, c = term(i, j)
                dq[at(i), :] += a
                dk[at(j), :] += b
                dv[at(j), :] += c

    cosine, sine = cos[...], sin[...]

    def turned_back(v):
        v = v * (1.0 / math.sqrt(HD))
        return (v * cosine - pltpu.roll(v, HD // 2, 1) * sine).astype(BF)

    width = out.shape[1] // 3
    at_head = pl.program_id(0) * HD
    for part, value in enumerate((turned_back(dq[...]), turned_back(dk[...]), dv[...].astype(BF))):
        out[:, pl.ds(pl.multiple_of(at_head + part * width, HD), HD)] = value


def attend_back(order, docs, q, k, v, d_mix, cos, sin):
    seq_len, width = q.shape
    head = pl.BlockSpec((seq_len, HD), lambda h, s: (0, h))
    whole = lambda r, c: pl.BlockSpec((r, c), lambda h, s: (0, 0))
    return call(
        functools.partial(attend_back_body, block=256),
        name="attend_back",
        grid=(width // HD,),
        scalars=1,
        in_specs=[head] * 4
        + [whole(seq_len, 1), whole(1, seq_len), whole(seq_len, HD), whole(seq_len, HD)],
        out_specs=[whole(seq_len, 3 * width)],
        out_shape=[jax.ShapeDtypeStruct((seq_len, 3 * width), BF)],
        scratch=[pltpu.VMEM((seq_len, HD), F32)] * 3,
    )(order, docs, q, k, v, d_mix, docs.reshape(-1, 1), docs.reshape(1, -1), cos, sin)


def project_body(mix, w_ref, x_ref, gain, resid, normed, acc):
    parts, _, cols = w_ref.shape
    step = pl.program_id(0)

    @pl.when(step == 0)
    def _():
        acc[...] = x_ref[...].astype(F32)

    for p in range(parts):
        acc[:, p * cols : (p + 1) * cols] += dot(mix[...], w_ref[p])

    @pl.when(step == pl.num_programs(0) - 1)
    def _():
        resid[...] = acc[...]
        normed[...] = rms_scale(acc[...], gain[...]).astype(BF)


def project(order, mix, w_out, x, gain):
    t, d = x.shape
    width = mix.shape[1]
    parts, _, cols = w_out.shape
    whole = lambda r, c: pl.BlockSpec((r, c), lambda i: (0, 0))
    return call(
        project_body,
        name="project",
        grid=(mix.shape[0] // t,),
        scalars=0,
        in_specs=[
            pl.BlockSpec((t, width), lambda i: (i, 0)),
            pl.BlockSpec((parts, width, cols), lambda i: (0, i, 0)),
            whole(t, d),
            whole(1, d),
        ],
        out_specs=[whole(t, d)] * 2,
        out_shape=[jax.ShapeDtypeStruct((t, d), F32), jax.ShapeDtypeStruct((t, d), BF)],
        scratch=[pltpu.VMEM((t, d), F32)],
    )(order, mix, w_out, x, gain.reshape(1, -1))


def norm_back(d_normed, rows, gain):
    r = lax.rsqrt(jnp.mean(rows * rows, axis=-1, keepdims=True) + EPS)
    u = rows * r
    scaled = d_normed * gain
    d_rows = r * (scaled - u * jnp.mean(scaled * u, axis=-1, keepdims=True))
    return d_rows, jnp.sum(d_normed * u, axis=0, keepdims=True)


def middle_body(d_ref, resid, cot, gain, w_ref, out, d_resid, low_t, part, low):
    parts, _, cols = w_ref.shape

    @pl.when(pl.program_id(0) == 0)
    def _():
        d_rows, part[...] = norm_back(d_ref[...].astype(F32), resid[...], gain[...])
        total = cot[...].astype(F32) + d_rows
        d_resid[...] = total
        low[...] = total.astype(BF)
        low_t[...] = low[...].T

    total = None
    for p in range(parts):
        term = dot_nt(low[:, p * cols : (p + 1) * cols], w_ref[p])
        total = term if total is None else total + term
    out[...] = total.astype(BF)


def middle(order, d_normed2, resid, cot, gain, w_out, width):
    t, d = resid.shape
    parts, rows, cols = w_out.shape
    count = rows // width
    whole = lambda r, c: pl.BlockSpec((r, c), lambda i: (0, 0))
    return call(
        middle_body,
        name="middle",
        grid=(count,),
        scalars=0,
        in_specs=[whole(t, d)] * 3
        + [whole(1, d), pl.BlockSpec((parts, width, cols), lambda i: (0, i, 0))],
        out_specs=[
            pl.BlockSpec((t, width), lambda i: (i, 0)),
            whole(t, d),
            whole(d, t),
            whole(1, d),
        ],
        out_shape=[
            jax.ShapeDtypeStruct((count * t, width), BF),
            jax.ShapeDtypeStruct((t, d), F32),
            jax.ShapeDtypeStruct((d, t), BF),
            jax.ShapeDtypeStruct((1, d), F32),
        ],
        scratch=[pltpu.VMEM((t, d), BF)],
    )(order, d_normed2, resid, cot, gain.reshape(1, -1), w_out)


def last_body(d_ref, x_ref, d_resid, gain, out, part):
    d_rows, part[...] = norm_back(d_ref[...].astype(F32), x_ref[...].astype(F32), gain[...])
    out[...] = (d_resid[...] + d_rows).astype(BF)


def last(order, d_normed, x, d_resid, gain):
    t, d = x.shape
    whole = lambda r, c: pl.BlockSpec((r, c), lambda i: (0, 0))
    return call(
        last_body,
        name="last",
        grid=(1,),
        scalars=0,
        in_specs=[whole(t, d)] * 3 + [whole(1, d)],
        out_specs=[whole(t, d), whole(1, d)],
        out_shape=[jax.ShapeDtypeStruct((t, d), BF), jax.ShapeDtypeStruct((1, d), F32)],
    )(order, d_normed, x, d_resid, gain.reshape(1, -1))


def back_project_body(d_ref, wq, wk, wv, out):
    total = None
    width = wq.shape[1]
    for k, w in enumerate((wq, wk, wv)):
        term = dot_nt(d_ref[:, k * width : (k + 1) * width], w[...])
        total = term if total is None else total + term
    out[...] = total.astype(BF)


def back_project(order, d_qkv, w_query, w_key, w_value):
    seq_len, wide = d_qkv.shape
    d, width = w_query.shape
    bn = 512
    wspec = pl.BlockSpec((bn, width), lambda i: (i, 0))
    return call(
        back_project_body,
        name="back_project",
        grid=(d // bn,),
        scalars=0,
        in_specs=[pl.BlockSpec((seq_len, wide), lambda i: (0, 0)), wspec, wspec, wspec],
        out_specs=[pl.BlockSpec((seq_len, bn), lambda i: (0, i))],
        out_shape=[jax.ShapeDtypeStruct((seq_len, d), BF)],
    )(order, d_qkv, w_query, w_key, w_value)[0]


def ffn_body(*refs):
    chunk, rows, cot, wg, wu, wd = refs[:6]
    inner, d_gate, d_up, rows_out, cot_out, d_rows, down, acc_d, acc_o = refs[-9:]
    step, last = pl.program_id(0), pl.num_programs(0) - 1
    x = rows[...]
    gate = dot(x, wg[...])
    up = dot(x, wu[...])
    sig = sigmoid(gate)
    silu = gate * sig
    inner_b = (silu * up).astype(BF)
    inner[...] = inner_b.T
    part = rows_out.shape[0]
    rows_out[...] = rows[:, pl.ds(pl.multiple_of(step * part, part), part)].T
    d_inner = dot_nt(cot[...], wd[...])
    dg = (d_inner * up * (sig * (1.0 + gate * (1.0 - sig)))).astype(BF)
    du = (d_inner * silu).astype(BF)
    d_gate[...] = dg
    d_up[...] = du
    term_o = dot(inner_b, wd[...])
    term_d = dot_nt(dg, wg[...]) + dot_nt(du, wu[...])

    @pl.when(step == 0)
    def _():
        acc_o[...] = term_o
        acc_d[...] = term_d
        cot_out[...] = cot[...]

    @pl.when(step > 0)
    def _():
        acc_o[...] += term_o
        acc_d[...] += term_d

    @pl.when(step == last)
    def _():
        d_rows[...] = acc_d[...].astype(BF)
        down[...] = acc_o[...].astype(BF)


def ffn_slot(order, chunk, rows, cot, w_gate, w_up, w_down, held, count):
    t, d = rows.shape
    hidden = w_gate.shape[1]
    bh = min(512, hidden)
    steps = hidden // bh
    wcol = pl.BlockSpec((d, bh), lambda i, s: (0, i))
    part = pl.BlockSpec((t, bh), lambda i, s: (s[0], i))
    line = pl.BlockSpec((t, d), lambda i, s: (s[0], 0))
    return call(
        ffn_body,
        name="ffn",
        grid=(hidden // bh,),
        scalars=1,
        in_specs=[
            pl.BlockSpec((t, d), lambda i, s: (0, 0)),
            pl.BlockSpec((t, d), lambda i, s: (0, 0)),
            wcol,
            wcol,
            pl.BlockSpec((bh, d), lambda i, s: (i, 0)),
        ]
        + [ANY] * len(held),
        out_specs=[pl.BlockSpec((bh, t), lambda i, s: (i, s[0])), part, part]
        + [pl.BlockSpec((d // steps, t), lambda i, s: (i, s[0])), line, line, line],
        out_shape=[jax.ShapeDtypeStruct((hidden, count * t), BF)]
        + [jax.ShapeDtypeStruct((count * t, hidden), BF)] * 2
        + [jax.ShapeDtypeStruct((d, count * t), BF)]
        + [jax.ShapeDtypeStruct((count * t, d), BF)] * 3,
        scratch=[pltpu.VMEM((t, d), F32)] * 2,
        aliases={6 + i: i for i in range(len(held))},
    )(order, chunk, rows, cot, w_gate, w_up, w_down, *held)


def local(
    layer_in,
    cotangent,
    doc_ids,
    positions,
    attn_gain,
    w_query,
    w_key,
    w_value,
    w_out,
    ffn_gain,
    w_gate,
    w_up,
    w_down,
    *,
    dp,
    tensor,
):
    t, d = layer_in.shape
    width = w_query.shape[1]
    hidden = w_gate.shape[1]
    place = lax.axis_index("tensor")
    chunks = jnp.stack([place ^ j for j in range(tensor)]).astype(jnp.int32)
    chunk = [chunks[j : j + 1] for j in range(tensor)]
    order = Order()

    share = w_out.shape[1] // dp
    w_cols = lax.all_gather(
        cols_at(w_out, lax.axis_index("dp"), share), "tensor", axis=0, tiled=True
    )
    half = HD // 2
    freqs = ROPE_BASE ** (-(jnp.arange(half).astype(F32) * 2.0) / HD)
    angles = positions.astype(F32)[:, None] * freqs[None, :]
    cosine, sine = jnp.cos(angles), jnp.sin(angles)
    cos = jnp.concatenate([cosine, cosine], axis=1)
    sin = jnp.concatenate([-sine, sine], axis=1)

    normed_own = rms_scale(layer_in.astype(F32), attn_gain).astype(BF)
    line = LineGather(normed_own, tensor, place)
    line.step()
    held = []
    for j in range(tensor):
        if 0 < j < tensor - 1:
            line.step(order)
        if j == tensor - 1:
            cots = LineGather(cotangent, tensor, place)
            cots.step(order)
        usual, order.worth = order.worth, 20 if j == tensor - 1 else order.worth
        held = qkv_slot(order, chunk[j], line.slot(j), w_query, w_key, w_value, cos, sin, held, tensor)
        order.worth = usual
        if j == min(2, tensor - 1):
            (w_cols,) = order.after(w_cols)
            w_out_all = lax.all_gather(w_cols, "dp", axis=0)
    query, key, value, normed_t = held
    (mixed,) = attend(order, doc_ids, query, key, value)
    mix = exchange(mixed)
    cots.step(order)
    (cot_first,) = order.after(cots.slot(1))
    resid, normed2_own = project(order, mix, w_out_all, layer_in, ffn_gain)

    weights = (w_gate, w_up, w_down)
    line = LineGather(normed2_own, tensor, place)
    line.step()
    held = ffn_slot(order, chunk[0], line.slot(0), cotangent, *weights, [], tensor)
    for j in range(1, tensor):
        if j < tensor - 1:
            line.step(order)
            if len(cots.ups) < tensor:
                cots.step(order)
        else:
            cots.hold(order)
            line.hold(order)
        cot = cot_first if j == 1 else cots.slot(j)
        held = ffn_slot(order, chunk[j], line.slot(j), cot, *weights, held, tensor)
    inner_t, d_gate, d_up, normed2_t, cot_all, d_normed2_part, down_part = held
    d_normed2 = lax.psum_scatter(d_normed2_part, "tensor", scatter_dimension=0, tiled=True)

    first = Gradients([(inner_t, cot_all, [d])], dp)
    wide = Gradients([(normed2_t, d_gate, [hidden]), (normed2_t, d_up, [hidden])], dp)
    more = range(first.bits - 2)

    first.give(order)
    wide.give(order, 0)
    wide.give(order, 1)
    first.keep(order)
    wide.keep(order, 0)
    wide.keep(order, 1)
    first.fold(order)
    for _ in more:
        first.fold(order)
    d_mix, d_resid, d_resid_t, ffn_gain_part = middle(
        order, d_normed2, resid, cotangent, ffn_gain, w_out_all, width
    )
    d_mix = exchange(d_mix)
    d_resid_all = lax.all_gather(d_resid_t, "tensor", axis=0)
    for _ in more:
        first.spread(order)
    wide.fold(order)
    (d_qkv,) = attend_back(order, doc_ids, query, key, value, d_mix, cos, sin)
    attn = Gradients([(normed_t, d_qkv, [width] * 4, d_resid_all, mixed)], dp)
    attn.give(order)
    d_normed = lax.psum_scatter(
        back_project(order, d_qkv, w_query, w_key, w_value),
        "tensor",
        scatter_dimension=0,
        tiled=True,
    )
    first.join(order)
    for _ in more:
        wide.fold(order)
    attn.give(order, second=True)
    attn.keep(order)
    wide.hold(order)
    usual, order.worth = order.worth, 10
    attn.fold(order)
    order.worth = usual
    down_sum = lax.psum_scatter(
        order.after(down_part)[0], "tensor", scatter_dimension=0, tiled=True
    )
    for _ in more:
        wide.spread(order)
    for _ in more:
        attn.fold(order)
    (down_grad,) = first.finish(order)
    in_grad, attn_gain_part = last(order, d_normed, layer_in, d_resid, attn_gain)
    totals = GainTotals([attn_gain_part, ffn_gain_part], dp, tensor)
    totals.step(order)
    totals.step(order)
    totals.step(order)
    wide.hold(order)
    order.worth = 0.3
    wide.join(order)
    attn.hold(order)
    order.worth = 0.3
    for _ in more:
        attn.spread(order)
    order.worth = 0.3
    order.worth = 5
    gate_grad = wide.fill(order, 0, 0)
    up_grad = wide.fill(order, 1, 0)
    order.worth = 0.02
    (gate_grad,) = wide.fill(order, 0, 1, gate_grad)
    (up_grad,) = wide.fill(order, 1, 1, up_grad)
    (down_sum,) = order.after(down_sum)
    attn.join(order)
    attn_grads = attn.fill(order, 0, 0)
    totals.step(order)
    query_grad, key_grad, value_grad, out_grad = attn.fill(order, 0, 1, attn_grads)
    attn_gain_grad, ffn_gain_grad = totals.split(order)
    layer_out = (resid + down_sum.astype(F32)).astype(BF)
    return (
        layer_out,
        in_grad,
        attn_gain_grad,
        query_grad,
        key_grad,
        value_grad,
        out_grad,
        ffn_gain_grad,
        gate_grad,
        up_grad,
        down_grad,
    )


def solution(mesh):
    rows, cols, lines = P(("dp", "tensor"), None), P(None, "tensor"), P("tensor", None)
    return jax.shard_map(
        functools.partial(local, dp=mesh.shape["dp"], tensor=mesh.shape["tensor"]),
        mesh=mesh,
        in_specs=(
            rows, rows, P("dp"), P("dp"), P(), cols, cols, cols, lines, P(), cols, cols, lines
        ),
        out_specs=(rows, rows, P(), cols, cols, cols, lines, P(), cols, cols, lines),
        check_vma=False,
    )
```

```python
import functools
import math

import jax
import jax.numpy as jnp
from jax import lax
from jax.experimental import pallas as pl
from jax.experimental.pallas import tpu as pltpu
from jax.sharding import PartitionSpec as P

HD = 128
EPS = 1e-05
ROPE_BASE = 500000.0
BF = jnp.bfloat16
F32 = jnp.float32
VMEM = 56 << 20
COST = {
    "give": 8, "give_second": 2.5, "keep": 10, "fold": 4, "spread": 4, "join": 4.5, "finish": 5.5, "middle": 9.5, "attend": 11,
    "attend_back": 17, "back_project": 11, "qkv": 5.6, "project": 8.6, "ffn": 22, "ffn_forward": 9, "ffn_back": 14, "last": 5, "tie": 0.5,
}


def dot(left, right):
    return lax.dot_general(left, right, (((1,), (0,)), ((), ())), preferred_element_type=F32)


def dot_nt(left, right):
    return lax.dot_general(left, right, (((1,), (1,)), ((), ())), preferred_element_type=F32)


def dot_tn(left, right):
    return lax.dot_general(left, right, (((0,), (0,)), ((), ())), preferred_element_type=F32)


def sigmoid(v):
    return 1.0 / (1.0 + jnp.exp(-v))


def rms_scale(values, gain):
    return values * lax.rsqrt(jnp.mean(values * values, axis=-1, keepdims=True) + EPS) * gain


ANY = pl.BlockSpec(memory_space=pl.ANY)
TOKEN = jax.ShapeDtypeStruct((8, 128), F32)


def call(body, *, name, grid, scalars, in_specs, out_specs, out_shape, scratch=(), aliases=None):
    def run(order, *operands):
        tokens = order.take()
        ahead = scalars + len(in_specs)

        def whole(*refs):
            outs = refs[ahead + len(tokens) :]
            body(*refs[:ahead], *outs[: len(out_shape)], *outs[len(out_shape) + 1 :])
            outs[len(out_shape)][...] = jnp.zeros((8, 128), F32)

        *values, token = pl.pallas_call(
            whole,
            grid_spec=pltpu.PrefetchScalarGridSpec(
                num_scalar_prefetch=scalars,
                grid=grid,
                in_specs=list(in_specs) + [ANY] * len(tokens),
                out_specs=list(out_specs) + [pl.BlockSpec((8, 128), lambda *_: (0, 0))],
                scratch_shapes=list(scratch),
            ),
            out_shape=list(out_shape) + [TOKEN],
            input_output_aliases=aliases or {},
            compiler_params=pltpu.CompilerParams(vmem_limit_bytes=VMEM),
            cost_estimate=pl.CostEstimate(flops=int(COST[name] * order.worth * 1e9), bytes_accessed=int(COST[name] * 1e6), transcendentals=0),
            name=name,
        )(*operands, *tokens)
        order.give(token)
        return values

    return run


class Order:
    def __init__(self):
        self.tokens, self.worth = [], 1.3

    def take(self):
        return self.tokens

    def give(self, token):
        self.tokens = [token]

    def after(self, *values):
        return call(
            lambda *refs: None,
            name="tie",
            grid=(1,),
            scalars=0,
            in_specs=[ANY] * len(values),
            out_specs=[ANY] * len(values),
            out_shape=[jax.ShapeDtypeStruct(v.shape, v.dtype) for v in values],
            aliases={i: i for i in range(len(values))},
            )(self, *values)


def xor_pairs(size, mask):
    return [(i, i ^ mask) for i in range(size)]


class LineGather:
    def __init__(self, own, size, place):
        self.size, self.place = size, place
        self.ups, self.downs = [own], [own]

    def step(self, order=None):
        k, size = len(self.ups), self.size
        if order is not None:
            if k == 1:
                self.ups = self.downs = order.after(self.ups[0])
                self.downs = list(self.downs)
            else:
                self.ups[-1], self.downs[-1] = order.after(self.ups[-1], self.downs[-1])
        up, down = self.ups[-1], self.downs[-1]
        self.ups.append(lax.ppermute(up, "tensor", [(i, i + 1) for i in range(k - 1, size - 1)]))
        self.downs.append(lax.ppermute(down, "tensor", [(i + 1, i) for i in range(0, size - k)]))

    def hold(self, order):
        self.ups[-1], self.downs[-1] = order.after(self.ups[-1], self.downs[-1])

    def slot(self, j):
        groups = {}
        for at in range(self.size):
            groups.setdefault((at ^ j) - at, []).append(at)
        value = None
        for off, places in groups.items():
            arr = self.downs[off] if off >= 0 else self.ups[-off]
            if value is None:
                value = arr
            else:
                here = functools.reduce(jnp.logical_or, [self.place == at for at in places])
                value = jnp.where(here, arr, value)
        return value


def exchange(values):
    return lax.all_to_all(values, "tensor", 0, 0, tiled=True)


def rows_at(values, block, rows):
    return lax.dynamic_slice_in_dim(values, block * rows, rows, axis=0)


def cols_at(values, block, cols):
    return lax.dynamic_slice_in_dim(values, block * cols, cols, axis=1)


def give_body(places, left, right, out):
    out[...] = dot(left[...], right[...]).astype(BF)


def give_second_body(places, left, right, out):
    out[...] = second((left, right), None).astype(BF)


def second(refs, rows):
    left, right = refs
    total, t = None, left.shape[2]
    for k in range(left.shape[0]):
        part = left[k] if rows is None else left[k, rows, :]
        term = dot(part, right[k * t : (k + 1) * t, :])
        total = term if total is None else total + term
    return total


def keep_body(places, *refs, two, last, lanes, chunks):
    ins = 4 if two else 2
    gots, outs = refs[ins : ins + (2 if two else 1)], refs[ins + (2 if two else 1) :]
    step = pl.program_id(0)
    rows = outs[0].shape[0]
    for lane in range(lanes):
        for rel in (1, 0):
            at = pl.multiple_of((places[1 + lane] ^ rel) * rows, rows)
            place = pl.ds(at, rows)
            out = outs[2 * lane + rel]
            inside = (step >= lane * chunks) & (step < (lane + 1) * chunks)

            @pl.when((inside & (step < last)) if two else inside)
            def _():
                total = dot(refs[0][place, :], refs[1][...])
                out[...] = (total + gots[0][place, :].astype(F32)).astype(BF)

            if two and lane == lanes - 1:

                @pl.when(step == last)
                def _():
                    total = second(refs[2:4], place)
                    out[...] = (total + gots[1][place, :].astype(F32)).astype(BF)


def fold_body(places, *refs):
    ins, outs = refs[:4], refs[4:]
    for h in (0, 1):
        total = (ins[2 * h][...].astype(F32) + ins[2 * h + 1][...].astype(F32)).astype(BF)
        if len(outs) == 2:
            outs[h][...] = total
        else:
            for rel in (0, 1):

                @pl.when(pl.program_id(0) == rel)
                def _():
                    outs[2 * h + rel][...] = total


def spread_body(places, *refs):
    ins, outs = refs[:4], refs[4:]
    for k in (0, 1):

        @pl.when(pl.program_id(0) == k)
        def _():
            for h in (0, 1):
                outs[h][...] = ins[2 * h + k][...]


def join_body(places, *refs):
    pieces, out = refs[:-1], refs[-1]
    step = pl.program_id(0) * 2 + pl.program_id(1)
    for k, piece in enumerate(pieces):

        @pl.when(step == k)
        def _():
            out[...] = piece[...]


def finish_body(place, source, *refs, turned, count):
    at, outs = 0, refs[-count:]
    for k, out in enumerate(outs):
        flip = turned and k == count - 1
        width = out.shape[0] if flip else out.shape[1]
        value = source[:, at : at + width].astype(F32)
        out[...] = value.T if flip else value
        at += width


class Product:
    def __init__(self, left, right, widths, firsts, pair=()):
        self.left, self.right, self.widths, self.firsts, self.pair = left, right, widths, firsts, pair
        self.rows = left.shape[0] // 2
        self.cols = right.shape[1] + (pair[1].shape[1] if pair else 0)
        self.bn = min(512, widths[-1])
        self.gots = []


class Gradients:
    def __init__(self, products, count):
        self.count = count
        self.bits = count.bit_length() - 1
        self.index = lax.axis_index("dp")
        self.orders = [list(range(1, self.bits)), list(range(self.bits - 1, 0, -1))]
        self.step = 0
        self.kept, self.gots = [], []
        per = 2 // len(products)
        self.products = [
            Product(*p[:3], [o[0] for o in self.orders[i * per : (i + 1) * per]], p[3:])
            for i, p in enumerate(products)
        ]

    def bit(self, b):
        return (self.index >> b) & 1

    def scalars(self, *values):
        return jnp.stack([jnp.asarray(v, jnp.int32) for v in values])

    def swap(self, value, b):
        return lax.ppermute(value, "dp", xor_pairs(self.count, 1 << b))

    def operands(self, p, core):
        tokens, last = p.right.shape[0], p.right.shape[1] // p.bn
        specs = [
            pl.BlockSpec((p.rows, tokens), lambda n, s: (s[0], 0)),
            pl.BlockSpec((tokens, p.bn), lambda n, s: (0, jnp.minimum(n, last - 1))),
        ]
        if p.pair:
            count, _, t = p.pair[0].shape
            specs += [
                pl.BlockSpec((count, p.rows, t), lambda n, s: (0, s[0], 0)),
                pl.BlockSpec((tokens, p.bn), lambda n, s: (0, 0)),
            ]
        return specs, [p.left, p.right, *p.pair], dict(two=bool(p.pair), last=last)

    def give(self, order, at=0, second=False):
        p = self.products[at]
        specs, values, facts = self.operands(p, 1 - self.bit(0))
        some = slice(2, 4) if second else slice(0, 2)
        cols = values[some][1].shape[1]
        (out,) = call(
            give_second_body if second else give_body,
            name="give_second" if second else "give",
            grid=(cols // p.bn,),
            scalars=1,
            in_specs=specs[some],
            out_specs=[pl.BlockSpec((p.rows, p.bn), lambda n, s: (0, n))],
            out_shape=[jax.ShapeDtypeStruct((p.rows, cols), BF)],
        )(order, self.scalars(1 - self.bit(0)), *values[some])
        p.gots.append(self.swap(out, 0))

    def keep(self, order, at=0):
        p = self.products[at]
        lanes = len(p.firsts)
        rows, cols = p.rows // 2, p.cols // lanes
        chunks = cols // p.bn
        specs, values, facts = self.operands(p, self.bit(0))

        def out_spec(lane):
            return pl.BlockSpec(
                (rows, p.bn), lambda n, s: (0, jnp.clip(n - lane * chunks, 0, chunks - 1))
            )

        outs = call(
            functools.partial(keep_body, lanes=lanes, chunks=chunks, **facts),
            name="keep",
            grid=(lanes * chunks,),
            scalars=1,
            in_specs=specs
            + [
                pl.BlockSpec((p.rows, p.bn), lambda n, s: (0, jnp.minimum(n, facts["last"] - 1))),
                pl.BlockSpec((p.rows, p.bn), lambda n, s: (0, 0)),
            ][: len(p.gots)],
            out_specs=[out_spec(k // 2) for k in range(2 * lanes)],
            out_shape=[jax.ShapeDtypeStruct((rows, cols), BF)] * (2 * lanes),
        )(order, self.scalars(self.bit(0), *[self.bit(b) for b in p.firsts]), *values, *p.gots)
        for h in range(lanes):
            self.kept.append(outs[2 * h])
            self.gots.append(self.swap(outs[2 * h + 1], p.firsts[h]))

    def fold(self, order):
        rows, cols = self.kept[0].shape
        self.step += 1
        more = self.step < self.bits - 1
        nexts = [self.bit(o[self.step]) for o in self.orders] if more else [0, 0]
        orows = rows // 2 if more else rows
        spec = lambda h: pl.BlockSpec((orows, cols), lambda r, s: (s[h] ^ r, 0))
        outs = call(
            fold_body,
            name="fold",
            grid=(2 if more else 1,),
            scalars=1,
            in_specs=[spec(0), spec(0), spec(1), spec(1)],
            out_specs=[pl.BlockSpec((orows, cols), lambda r, s: (0, 0))] * (4 if more else 2),
            out_shape=[jax.ShapeDtypeStruct((orows, cols), BF)] * (4 if more else 2),
        )(order, self.scalars(*nexts), self.kept[0], self.gots[0], self.kept[1], self.gots[1])
        self.kept = outs[:: 2 if more else 1]
        if more:
            self.gots = [self.swap(outs[1 + 2 * h], self.orders[h][self.step]) for h in (0, 1)]
        else:
            self.ask()

    def hold(self, order):
        self.gots = order.after(*self.gots)

    def ask(self):
        self.step -= 1
        self.gots = [self.swap(k, o[self.step]) for k, o in zip(self.kept, self.orders)]

    def spread(self, order):
        rows, cols = self.kept[0].shape
        spec = pl.BlockSpec((rows, cols), lambda k, s: (0, 0))
        self.kept = call(
            spread_body,
            name="spread",
            grid=(2,),
            scalars=1,
            in_specs=[spec] * 4,
            out_specs=[
                pl.BlockSpec((rows, cols), lambda k, s: (k ^ s[0], 0)),
                pl.BlockSpec((rows, cols), lambda k, s: (k ^ s[1], 0)),
            ],
            out_shape=[jax.ShapeDtypeStruct((2 * rows, cols), BF)] * 2,
        )(
            order,
            self.scalars(*[self.bit(o[self.step]) for o in self.orders]),
            self.kept[0],
            self.gots[0],
            self.kept[1],
            self.gots[1],
        )
        self.ask()

    def join(self, order):
        brows, bcols = self.kept[0].shape
        lane = 0
        for p in self.products:
            lanes = range(lane, lane + len(p.firsts))
            lane += len(p.firsts)
            (p.half,) = call(
                join_body,
                name="join",
                grid=(len(lanes), 2),
                scalars=1,
                in_specs=[pl.BlockSpec((brows, bcols), lambda h, k, s: (0, 0))] * (2 * len(lanes)),
                out_specs=[pl.BlockSpec((brows, bcols), lambda h, k, s: (k ^ s[h], h))],
                out_shape=[jax.ShapeDtypeStruct((p.rows, p.cols), BF)],
            )(
                order,
                self.scalars(*[self.bit(self.orders[l][self.step]) for l in lanes]),
                *[v for l in lanes for v in (self.kept[l], self.gots[l])],
            )
            p.other = self.swap(p.half, 0)

    def finish(self, order, at=0):
        outs = self.fill(order, at, 0)
        return self.fill(order, at, 1, outs)

    def fill(self, order, at, other, ahead=()):
        p = self.products[at]
        rows, cols = p.half.shape
        crows = min(256, rows)
        nblk = rows // crows
        turned = bool(p.pair)
        specs = [pl.BlockSpec((crows, w), lambda b, s: (s[0] * nblk + b, 0)) for w in p.widths]
        shapes = [jax.ShapeDtypeStruct((2 * rows, w), F32) for w in p.widths]
        if turned:
            w = p.widths[-1]
            specs[-1] = pl.BlockSpec((w, crows), lambda b, s: (0, s[0] * nblk + b))
            shapes[-1] = jax.ShapeDtypeStruct((w, 2 * rows), F32)
        return call(
            functools.partial(finish_body, turned=turned, count=len(specs)),
            name="finish",
            grid=(nblk,),
            scalars=1,
            in_specs=[pl.BlockSpec((crows, cols), lambda b, s: (b, 0))] + [ANY] * len(ahead),
            out_specs=specs,
            out_shape=shapes,
            aliases={2 + k: k for k in range(len(ahead))},
        )(order, self.scalars(self.bit(0) ^ other), p.other if other else p.half, *ahead)


class GainTotals:
    def __init__(self, parts, dp, tensor):
        self.size = parts[0].size
        self.value = jnp.concatenate([p.reshape(-1, 128) for p in parts], axis=0)
        self.left = [
            (name, size, [1 << k])
            for name, size in (("tensor", tensor), ("dp", dp))
            for k in range(size.bit_length() - 1)
        ]
        self.next()

    def next(self):
        name, size, masks = self.left.pop(0)
        self.got = [lax.ppermute(self.value, name, xor_pairs(size, m)) for m in masks]

    def step(self, order):
        self.value, *got = order.after(self.value, *self.got)
        self.value = self.value + got[0]
        if self.left:
            self.next()

    def split(self, order):
        while self.left:
            self.step(order)
        self.step(order)
        value = self.value.reshape(-1)
        return [value[k : k + self.size] for k in range(0, value.size, self.size)]


def qkv_body(*refs):
    chunk, rows, wq, wk, wv, cos, sin = refs[:7]
    q_out, k_out, v_out, rows_out = refs[-4:]
    x = rows[...]
    cosine, sine = cos[...], sin[...]

    def turned(pre):
        out = []
        for h in range(pre.shape[1] // HD):
            one = pre[:, h * HD : (h + 1) * HD]
            out.append(one * cosine + pltpu.roll(one, HD // 2, 1) * sine)
        return jnp.concatenate(out, axis=1)

    q_out[...] = turned(dot(x, wq[...])).astype(BF)
    k_out[...] = turned(dot(x, wk[...])).astype(BF)
    v_out[...] = dot(x, wv[...]).astype(BF)
    part = rows_out.shape[0]
    rows_out[...] = rows[:, pl.ds(pl.multiple_of(pl.program_id(0) * part, part), part)].T


def qkv_slot(order, chunk, rows, w_query, w_key, w_value, cos, sin, held, count):
    t, d = rows.shape
    width = w_query.shape[1]
    bn = min(256, width)
    wspec = pl.BlockSpec((d, bn), lambda i, s: (0, i))
    tspec = pl.BlockSpec((t, HD), lambda i, s: (s[0], 0))
    return call(
        qkv_body,
        name="qkv",
        grid=(width // bn,),
        scalars=1,
        in_specs=[pl.BlockSpec((t, d), lambda i, s: (0, 0)), wspec, wspec, wspec, tspec, tspec]
        + [ANY] * len(held),
        out_specs=[pl.BlockSpec((t, bn), lambda i, s: (s[0], i))] * 3
        + [pl.BlockSpec((d // (width // bn), t), lambda i, s: (i, s[0]))],
        out_shape=[jax.ShapeDtypeStruct((count * t, width), BF)] * 3
        + [jax.ShapeDtypeStruct((d, count * t), BF)],
        aliases={7 + i: i for i in range(len(held))},
    )(order, chunk, rows, w_query, w_key, w_value, cos, sin, *held)


def attend_consts(seq_len):
    to_log2 = math.log2(math.e)
    return (to_log2 / math.sqrt(HD), math.log2(seq_len))


def attend_body(docs, q_ref, k_ref, v_ref, ids_col, ids_row, mix, acc, *, block):
    seq_len = q_ref.shape[0]
    scale, shift = attend_consts(seq_len)
    causal = lax.broadcasted_iota(jnp.int32, (block, block), 0) >= lax.broadcasted_iota(
        jnp.int32, (block, block), 1
    )

    def term(i, j):
        q = q_ref[i * block : (i + 1) * block, :]
        k = k_ref[j * block : (j + 1) * block, :]
        sig = 1.0 / (1.0 + jnp.exp2(shift - dot_nt(q, k) * scale))
        same = ids_col[i * block : (i + 1) * block, :] == ids_row[:, j * block : (j + 1) * block]
        allowed = same & causal if i == j else same
        probs = jnp.where(allowed, sig, 0.0).astype(BF)
        return dot(probs, v_ref[j * block : (j + 1) * block, :])

    for i in range(seq_len // block):
        acc[...] = term(i, i)
        for j in range(i):

            @pl.when(docs[(j + 1) * block - 1] == docs[i * block])
            def _():
                acc[...] += term(i, j)

        mix[i * block : (i + 1) * block, :] = acc[...].astype(BF)


def attend(order, docs, q, k, v):
    seq_len, width = q.shape
    block = 256
    head = pl.BlockSpec((seq_len, HD), lambda h, s: (0, h))
    return call(
        functools.partial(attend_body, block=block),
        name="attend",
        grid=(width // HD,),
        scalars=1,
        in_specs=[
            head,
            head,
            head,
            pl.BlockSpec((seq_len, 1), lambda h, s: (0, 0)),
            pl.BlockSpec((1, seq_len), lambda h, s: (0, 0)),
        ],
        out_specs=[head],
        out_shape=[jax.ShapeDtypeStruct((seq_len, width), BF)],
        scratch=[pltpu.VMEM((block, HD), F32)],
    )(order, docs, q, k, v, docs.reshape(-1, 1), docs.reshape(1, -1))


def attend_back_body(
    docs, q_ref, k_ref, v_ref, dmix, ids_col, ids_row, cos, sin, out, dq, dk, dv, *, block
):
    seq_len = q_ref.shape[0]
    scale, shift = attend_consts(seq_len)
    causal = lax.broadcasted_iota(jnp.int32, (block, block), 0) <= lax.broadcasted_iota(
        jnp.int32, (block, block), 1
    )

    def at(i):
        return slice(i * block, (i + 1) * block)

    def term(i, j):
        q, k, v, d = q_ref[at(i), :], k_ref[at(j), :], v_ref[at(j), :], dmix[at(i), :]
        sig = 1.0 / (1.0 + jnp.exp2(shift - dot_nt(k, q) * scale))
        same = ids_col[at(j), :] == ids_row[:, at(i)]
        allowed = same & causal if i == j else same
        probs = jnp.where(allowed, sig, 0.0)
        d_scores = (dot_nt(v, d) * probs * (1.0 - probs)).astype(BF)
        return dot_tn(d_scores, k), dot(d_scores, q), dot(probs.astype(BF), d)

    for i in range(seq_len // block):
        dq[at(i), :], dk[at(i), :], dv[at(i), :] = term(i, i)
    for i in range(seq_len // block):
        for j in range(i):

            @pl.when(docs[(j + 1) * block - 1] == docs[i * block])
            def _():
                a, b, c = term(i, j)
                dq[at(i), :] += a
                dk[at(j), :] += b
                dv[at(j), :] += c

    cosine, sine = cos[...], sin[...]

    def turned_back(v):
        v = v * (1.0 / math.sqrt(HD))
        return (v * cosine - pltpu.roll(v, HD // 2, 1) * sine).astype(BF)

    width = out.shape[1] // 3
    at_head = pl.program_id(0) * HD
    for part, value in enumerate((turned_back(dq[...]), turned_back(dk[...]), dv[...].astype(BF))):
        out[:, pl.ds(pl.multiple_of(at_head + part * width, HD), HD)] = value


def attend_back(order, docs, q, k, v, d_mix, cos, sin):
    seq_len, width = q.shape
    head = pl.BlockSpec((seq_len, HD), lambda h, s: (0, h))
    whole = lambda r, c: pl.BlockSpec((r, c), lambda h, s: (0, 0))
    return call(
        functools.partial(attend_back_body, block=256),
        name="attend_back",
        grid=(width // HD,),
        scalars=1,
        in_specs=[head] * 4
        + [whole(seq_len, 1), whole(1, seq_len), whole(seq_len, HD), whole(seq_len, HD)],
        out_specs=[whole(seq_len, 3 * width)],
        out_shape=[jax.ShapeDtypeStruct((seq_len, 3 * width), BF)],
        scratch=[pltpu.VMEM((seq_len, HD), F32)] * 3,
    )(order, docs, q, k, v, d_mix, docs.reshape(-1, 1), docs.reshape(1, -1), cos, sin)


def project_body(mix, w_ref, x_ref, gain, resid, normed, acc):
    parts, _, cols = w_ref.shape
    step = pl.program_id(0)

    @pl.when(step == 0)
    def _():
        acc[...] = x_ref[...].astype(F32)

    for p in range(parts):
        acc[:, p * cols : (p + 1) * cols] += dot(mix[...], w_ref[p])

    @pl.when(step == pl.num_programs(0) - 1)
    def _():
        resid[...] = acc[...]
        normed[...] = rms_scale(acc[...], gain[...]).astype(BF)


def project(order, mix, w_out, x, gain):
    t, d = x.shape
    width = mix.shape[1]
    parts, _, cols = w_out.shape
    whole = lambda r, c: pl.BlockSpec((r, c), lambda i: (0, 0))
    return call(
        project_body,
        name="project",
        grid=(mix.shape[0] // t,),
        scalars=0,
        in_specs=[
            pl.BlockSpec((t, width), lambda i: (i, 0)),
            pl.BlockSpec((parts, width, cols), lambda i: (0, i, 0)),
            whole(t, d),
            whole(1, d),
        ],
        out_specs=[whole(t, d)] * 2,
        out_shape=[jax.ShapeDtypeStruct((t, d), F32), jax.ShapeDtypeStruct((t, d), BF)],
        scratch=[pltpu.VMEM((t, d), F32)],
    )(order, mix, w_out, x, gain.reshape(1, -1))


def norm_back(d_normed, rows, gain):
    r = lax.rsqrt(jnp.mean(rows * rows, axis=-1, keepdims=True) + EPS)
    u = rows * r
    scaled = d_normed * gain
    d_rows = r * (scaled - u * jnp.mean(scaled * u, axis=-1, keepdims=True))
    return d_rows, jnp.sum(d_normed * u, axis=0, keepdims=True)


def middle_body(d_ref, resid, cot, gain, w_ref, out, d_resid, low_t, part, low):
    parts, _, cols = w_ref.shape

    @pl.when(pl.program_id(0) == 0)
    def _():
        d_rows, part[...] = norm_back(d_ref[...].astype(F32), resid[...], gain[...])
        total = cot[...].astype(F32) + d_rows
        d_resid[...] = total
        low[...] = total.astype(BF)
        low_t[...] = low[...].T

    total = None
    for p in range(parts):
        term = dot_nt(low[:, p * cols : (p + 1) * cols], w_ref[p])
        total = term if total is None else total + term
    out[...] = total.astype(BF)


def middle(order, d_normed2, resid, cot, gain, w_out, width):
    t, d = resid.shape
    parts, rows, cols = w_out.shape
    count = rows // width
    whole = lambda r, c: pl.BlockSpec((r, c), lambda i: (0, 0))
    return call(
        middle_body,
        name="middle",
        grid=(count,),
        scalars=0,
        in_specs=[whole(t, d)] * 3
        + [whole(1, d), pl.BlockSpec((parts, width, cols), lambda i: (0, i, 0))],
        out_specs=[
            pl.BlockSpec((t, width), lambda i: (i, 0)),
            whole(t, d),
            whole(d, t),
            whole(1, d),
        ],
        out_shape=[
            jax.ShapeDtypeStruct((count * t, width), BF),
            jax.ShapeDtypeStruct((t, d), F32),
            jax.ShapeDtypeStruct((d, t), BF),
            jax.ShapeDtypeStruct((1, d), F32),
        ],
        scratch=[pltpu.VMEM((t, d), BF)],
    )(order, d_normed2, resid, cot, gain.reshape(1, -1), w_out)


def last_body(d_ref, x_ref, d_resid, gain, out, part):
    d_rows, part[...] = norm_back(d_ref[...].astype(F32), x_ref[...].astype(F32), gain[...])
    out[...] = (d_resid[...] + d_rows).astype(BF)


def last(order, d_normed, x, d_resid, gain):
    t, d = x.shape
    whole = lambda r, c: pl.BlockSpec((r, c), lambda i: (0, 0))
    return call(
        last_body,
        name="last",
        grid=(1,),
        scalars=0,
        in_specs=[whole(t, d)] * 3 + [whole(1, d)],
        out_specs=[whole(t, d), whole(1, d)],
        out_shape=[jax.ShapeDtypeStruct((t, d), BF), jax.ShapeDtypeStruct((1, d), F32)],
    )(order, d_normed, x, d_resid, gain.reshape(1, -1))


def back_project_body(d_ref, wq, wk, wv, out):
    total = None
    width = wq.shape[1]
    for k, w in enumerate((wq, wk, wv)):
        term = dot_nt(d_ref[:, k * width : (k + 1) * width], w[...])
        total = term if total is None else total + term
    out[...] = total.astype(BF)


def back_project(order, d_qkv, w_query, w_key, w_value):
    seq_len, wide = d_qkv.shape
    d, width = w_query.shape
    bn = 512
    wspec = pl.BlockSpec((bn, width), lambda i: (i, 0))
    return call(
        back_project_body,
        name="back_project",
        grid=(d // bn,),
        scalars=0,
        in_specs=[pl.BlockSpec((seq_len, wide), lambda i: (0, 0)), wspec, wspec, wspec],
        out_specs=[pl.BlockSpec((seq_len, bn), lambda i: (0, i))],
        out_shape=[jax.ShapeDtypeStruct((seq_len, d), BF)],
    )(order, d_qkv, w_query, w_key, w_value)[0]


def ffn_body(*refs):
    chunk, rows, cot, wg, wu, wd = refs[:6]
    inner, d_gate, d_up, rows_out, cot_out, d_rows, down, acc_d, acc_o = refs[-9:]
    step, last = pl.program_id(0), pl.num_programs(0) - 1
    x = rows[...]
    gate = dot(x, wg[...])
    up = dot(x, wu[...])
    sig = sigmoid(gate)
    silu = gate * sig
    inner_b = (silu * up).astype(BF)
    inner[...] = inner_b.T
    part = rows_out.shape[0]
    rows_out[...] = rows[:, pl.ds(pl.multiple_of(step * part, part), part)].T
    d_inner = dot_nt(cot[...], wd[...])
    dg = (d_inner * up * (sig * (1.0 + gate * (1.0 - sig)))).astype(BF)
    du = (d_inner * silu).astype(BF)
    d_gate[...] = dg
    d_up[...] = du
    term_o = dot(inner_b, wd[...])
    term_d = dot_nt(dg, wg[...]) + dot_nt(du, wu[...])

    @pl.when(step == 0)
    def _():
        acc_o[...] = term_o
        acc_d[...] = term_d
        cot_out[...] = cot[...]

    @pl.when(step > 0)
    def _():
        acc_o[...] += term_o
        acc_d[...] += term_d

    @pl.when(step == last)
    def _():
        d_rows[...] = acc_d[...].astype(BF)
        down[...] = acc_o[...].astype(BF)


def ffn_slot(order, chunk, rows, cot, w_gate, w_up, w_down, held, count):
    t, d = rows.shape
    hidden = w_gate.shape[1]
    bh = min(512, hidden)
    steps = hidden // bh
    wcol = pl.BlockSpec((d, bh), lambda i, s: (0, i))
    part = pl.BlockSpec((t, bh), lambda i, s: (s[0], i))
    line = pl.BlockSpec((t, d), lambda i, s: (s[0], 0))
    return call(
        ffn_body,
        name="ffn",
        grid=(hidden // bh,),
        scalars=1,
        in_specs=[
            pl.BlockSpec((t, d), lambda i, s: (0, 0)),
            pl.BlockSpec((t, d), lambda i, s: (0, 0)),
            wcol,
            wcol,
            pl.BlockSpec((bh, d), lambda i, s: (i, 0)),
        ]
        + [ANY] * len(held),
        out_specs=[pl.BlockSpec((bh, t), lambda i, s: (i, s[0])), part, part]
        + [pl.BlockSpec((d // steps, t), lambda i, s: (i, s[0])), line, line, line],
        out_shape=[jax.ShapeDtypeStruct((hidden, count * t), BF)]
        + [jax.ShapeDtypeStruct((count * t, hidden), BF)] * 2
        + [jax.ShapeDtypeStruct((d, count * t), BF)]
        + [jax.ShapeDtypeStruct((count * t, d), BF)] * 3,
        scratch=[pltpu.VMEM((t, d), F32)] * 2,
        aliases={6 + i: i for i in range(len(held))},
    )(order, chunk, rows, cot, w_gate, w_up, w_down, *held)


def ffn_forward_body(*refs):
    chunk, rows, cot, wg, wu = refs[:5]
    inner, rows_out, cot_out, gate_out, up_out = refs[-5:]
    step = pl.program_id(0)
    x = rows[...]
    gate = dot(x, wg[...])
    up = dot(x, wu[...])
    gate_out[...] = gate
    up_out[...] = up
    inner[...] = (gate * sigmoid(gate) * up).astype(BF).T
    part = rows_out.shape[0]
    rows_out[...] = rows[:, pl.ds(pl.multiple_of(step * part, part), part)].T

    @pl.when(step == 0)
    def _():
        cot_out[...] = cot[...]


def ffn_back_body(*refs):
    chunk, cot, gate_ref, up_ref, wg, wu, wd = refs[:7]
    d_gate, d_up, d_rows, down, acc_d, acc_o = refs[-6:]
    step, last = pl.program_id(0), pl.num_programs(0) - 1
    gate, up = gate_ref[...], up_ref[...]
    sig = sigmoid(gate)
    silu = gate * sig
    d_inner = dot_nt(cot[...], wd[...])
    dg = (d_inner * up * (sig * (1.0 + gate * (1.0 - sig)))).astype(BF)
    du = (d_inner * silu).astype(BF)
    d_gate[...] = dg
    d_up[...] = du
    term_o = dot((silu * up).astype(BF), wd[...])
    term_d = dot_nt(dg, wg[...]) + dot_nt(du, wu[...])

    @pl.when(step == 0)
    def _():
        acc_o[...] = term_o
        acc_d[...] = term_d

    @pl.when(step > 0)
    def _():
        acc_o[...] += term_o
        acc_d[...] += term_d

    @pl.when(step == last)
    def _():
        d_rows[...] = acc_d[...].astype(BF)
        down[...] = acc_o[...].astype(BF)


def ffn_forward(order, chunk, rows, cot, w_gate, w_up, held):
    t, d = rows.shape
    hidden = w_gate.shape[1]
    bh = min(512, hidden)
    steps = hidden // bh
    whole = pl.BlockSpec((t, d), lambda i, s: (0, 0))
    wcol = pl.BlockSpec((d, bh), lambda i, s: (0, i))
    own = pl.BlockSpec((t, bh), lambda i, s: (0, i))
    return call(
        ffn_forward_body,
        name="ffn_forward",
        grid=(steps,),
        scalars=1,
        in_specs=[whole, whole, wcol, wcol] + [ANY] * 3,
        out_specs=[
            pl.BlockSpec((bh, t), lambda i, s: (i, s[0])),
            pl.BlockSpec((d // steps, t), lambda i, s: (i, s[0])),
            pl.BlockSpec((t, d), lambda i, s: (s[0], 0)),
            own,
            own,
        ],
        out_shape=[jax.ShapeDtypeStruct(v.shape, v.dtype) for v in held]
        + [jax.ShapeDtypeStruct((t, hidden), F32)] * 2,
        aliases={5 + i: i for i in range(3)},
    )(order, chunk, rows, cot, w_gate, w_up, *held)


def ffn_back(order, chunk, cot, gate, up, w_gate, w_up, w_down, held):
    t, d = cot.shape
    hidden = w_gate.shape[1]
    bh = min(512, hidden)
    wcol = pl.BlockSpec((d, bh), lambda i, s: (0, i))
    own = pl.BlockSpec((t, bh), lambda i, s: (0, i))
    part = pl.BlockSpec((t, bh), lambda i, s: (s[0], i))
    line = pl.BlockSpec((t, d), lambda i, s: (s[0], 0))
    return call(
        ffn_back_body,
        name="ffn_back",
        grid=(hidden // bh,),
        scalars=1,
        in_specs=[
            pl.BlockSpec((t, d), lambda i, s: (0, 0)),
            own,
            own,
            wcol,
            wcol,
            pl.BlockSpec((bh, d), lambda i, s: (i, 0)),
        ]
        + [ANY] * 4,
        out_specs=[part, part, line, line],
        out_shape=[jax.ShapeDtypeStruct(v.shape, v.dtype) for v in held],
        scratch=[pltpu.VMEM((t, d), F32)] * 2,
        aliases={7 + i: i for i in range(4)},
    )(order, chunk, cot, gate, up, w_gate, w_up, w_down, *held)


def local(
    layer_in,
    cotangent,
    doc_ids,
    positions,
    attn_gain,
    w_query,
    w_key,
    w_value,
    w_out,
    ffn_gain,
    w_gate,
    w_up,
    w_down,
    *,
    dp,
    tensor,
):
    t, d = layer_in.shape
    width = w_query.shape[1]
    hidden = w_gate.shape[1]
    place = lax.axis_index("tensor")
    chunks = jnp.stack([place ^ j for j in range(tensor)]).astype(jnp.int32)
    chunk = [chunks[j : j + 1] for j in range(tensor)]
    order = Order()

    share = w_out.shape[1] // dp
    w_cols = lax.all_gather(
        cols_at(w_out, lax.axis_index("dp"), share), "tensor", axis=0, tiled=True
    )
    half = HD // 2
    freqs = ROPE_BASE ** (-(jnp.arange(half).astype(F32) * 2.0) / HD)
    angles = positions.astype(F32)[:, None] * freqs[None, :]
    cosine, sine = jnp.cos(angles), jnp.sin(angles)
    cos = jnp.concatenate([cosine, cosine], axis=1)
    sin = jnp.concatenate([-sine, sine], axis=1)

    normed_own = rms_scale(layer_in.astype(F32), attn_gain).astype(BF)
    line = LineGather(normed_own, tensor, place)
    line.step()
    held = []
    for j in range(tensor):
        if 0 < j < tensor - 1:
            line.step(order)
        if j == tensor - 1:
            cots = LineGather(cotangent, tensor, place)
            cots.step(order)
        usual, order.worth = order.worth, 20 if j == tensor - 1 else order.worth
        held = qkv_slot(order, chunk[j], line.slot(j), w_query, w_key, w_value, cos, sin, held, tensor)
        order.worth = usual
        if j == min(2, tensor - 1):
            (w_cols,) = order.after(w_cols)
            w_out_all = lax.all_gather(w_cols, "dp", axis=0)
    query, key, value, normed_t = held
    (mixed,) = attend(order, doc_ids, query, key, value)
    mix = exchange(mixed)
    cots.step(order)
    (cot_first,) = order.after(cots.slot(1))
    resid, normed2_own = project(order, mix, w_out_all, layer_in, ffn_gain)

    weights = (w_gate, w_up, w_down)
    line = LineGather(normed2_own, tensor, place)
    line.step()
    held = ffn_slot(order, chunk[0], line.slot(0), cotangent, *weights, [], tensor)
    for j in range(1, tensor):
        if j < tensor - 1:
            line.step(order)
            if len(cots.ups) < tensor:
                cots.step(order)
        else:
            cots.hold(order)
            line.hold(order)
        cot = cot_first if j == 1 else cots.slot(j)
        if j < tensor - 1:
            held = ffn_slot(order, chunk[j], line.slot(j), cot, *weights, held, tensor)
    inner_t, d_gate, d_up, normed2_t, cot_all, d_normed2_part, down_part = held
    inner_t, normed2_t, cot_all, gate_last, up_last = ffn_forward(
        order, chunk[j], line.slot(j), cot, w_gate, w_up, [inner_t, normed2_t, cot_all]
    )
    first = Gradients([(inner_t, cot_all, [d])], dp)
    first.give(order)
    d_gate, d_up, d_normed2_part, down_part = ffn_back(
        order, chunk[j], cot, gate_last, up_last, *weights,
        [d_gate, d_up, d_normed2_part, down_part],
    )
    d_normed2 = lax.psum_scatter(d_normed2_part, "tensor", scatter_dimension=0, tiled=True)

    wide = Gradients([(normed2_t, d_gate, [hidden]), (normed2_t, d_up, [hidden])], dp)
    more = range(first.bits - 2)
    usual = order.worth

    first.keep(order)
    wide.give(order, 0)
    wide.give(order, 1)
    order.worth = 25
    first.fold(order)
    order.worth = usual
    wide.keep(order, 0)
    wide.keep(order, 1)
    for _ in more:
        first.fold(order)
    d_mix, d_resid, d_resid_t, ffn_gain_part = middle(
        order, d_normed2, resid, cotangent, ffn_gain, w_out_all, width
    )
    d_mix = exchange(d_mix)
    d_resid_all = lax.all_gather(d_resid_t, "tensor", axis=0)
    for _ in more:
        first.spread(order)
    wide.fold(order)
    (d_qkv,) = attend_back(order, doc_ids, query, key, value, d_mix, cos, sin)
    attn = Gradients([(normed_t, d_qkv, [width] * 4, d_resid_all, mixed)], dp)
    attn.give(order)
    first.join(order)
    d_normed = lax.psum_scatter(
        back_project(order, d_qkv, w_query, w_key, w_value),
        "tensor",
        scatter_dimension=0,
        tiled=True,
    )
    for _ in more:
        wide.fold(order)
    attn.give(order, second=True)
    attn.keep(order)
    wide.hold(order)
    usual, order.worth = order.worth, 10
    attn.fold(order)
    order.worth = usual
    down_sum = lax.psum_scatter(
        order.after(down_part)[0], "tensor", scatter_dimension=0, tiled=True
    )
    for _ in more:
        wide.spread(order)
    for _ in more:
        attn.fold(order)
    (down_grad,) = first.finish(order)
    in_grad, attn_gain_part = last(order, d_normed, layer_in, d_resid, attn_gain)
    totals = GainTotals([attn_gain_part, ffn_gain_part], dp, tensor)
    totals.step(order)
    totals.step(order)
    totals.step(order)
    wide.hold(order)
    order.worth = 0.3
    wide.join(order)
    attn.hold(order)
    order.worth = 0.3
    for _ in more:
        attn.spread(order)
    order.worth = 0.3
    order.worth = 5
    gate_grad = wide.fill(order, 0, 0)
    up_grad = wide.fill(order, 1, 0)
    order.worth = 0.02
    (gate_grad,) = wide.fill(order, 0, 1, gate_grad)
    (up_grad,) = wide.fill(order, 1, 1, up_grad)
    (down_sum,) = order.after(down_sum)
    attn.join(order)
    attn_grads = attn.fill(order, 0, 0)
    totals.step(order)
    query_grad, key_grad, value_grad, out_grad = attn.fill(order, 0, 1, attn_grads)
    attn_gain_grad, ffn_gain_grad = totals.split(order)
    layer_out = (resid + down_sum.astype(F32)).astype(BF)
    return (
        layer_out,
        in_grad,
        attn_gain_grad,
        query_grad,
        key_grad,
        value_grad,
        out_grad,
        ffn_gain_grad,
        gate_grad,
        up_grad,
        down_grad,
    )


def solution(mesh):
    rows, cols, lines = P(("dp", "tensor"), None), P(None, "tensor"), P("tensor", None)
    return jax.shard_map(
        functools.partial(local, dp=mesh.shape["dp"], tensor=mesh.shape["tensor"]),
        mesh=mesh,
        in_specs=(
            rows, rows, P("dp"), P("dp"), P(), cols, cols, cols, lines, P(), cols, cols, lines
        ),
        out_specs=(rows, rows, P(), cols, cols, cols, lines, P(), cols, cols, lines),
        check_vma=False,
    )
```

```python
import functools
import math

import jax
import jax.numpy as jnp
from jax import lax
from jax.experimental import pallas as pl
from jax.experimental.pallas import tpu as pltpu
from jax.sharding import PartitionSpec as P

HD = 128
EPS = 1e-05
ROPE_BASE = 500000.0
BF = jnp.bfloat16
F32 = jnp.float32
VMEM = 56 << 20
COST = {
    "give": 8, "give_second": 2.5, "keep": 10, "fold": 4, "spread": 4, "join": 4.5, "finish": 5.5, "middle": 9.5, "attend": 11,
    "attend_back": 17, "back_project": 11, "qkv": 5.6, "project": 8.6, "ffn": 22, "last": 5, "tie": 0.5,
}


def dot(left, right):
    return lax.dot_general(left, right, (((1,), (0,)), ((), ())), preferred_element_type=F32)


def dot_nt(left, right):
    return lax.dot_general(left, right, (((1,), (1,)), ((), ())), preferred_element_type=F32)


def dot_tn(left, right):
    return lax.dot_general(left, right, (((0,), (0,)), ((), ())), preferred_element_type=F32)


def sigmoid(v):
    return 1.0 / (1.0 + jnp.exp(-v))


def rms_scale(values, gain):
    return values * lax.rsqrt(jnp.mean(values * values, axis=-1, keepdims=True) + EPS) * gain


ANY = pl.BlockSpec(memory_space=pl.ANY)
TOKEN = jax.ShapeDtypeStruct((8, 128), F32)


def call(body, *, name, grid, scalars, in_specs, out_specs, out_shape, scratch=(), aliases=None):
    def run(order, *operands):
        tokens = order.take()
        ahead = scalars + len(in_specs)

        def whole(*refs):
            outs = refs[ahead + len(tokens) :]
            body(*refs[:ahead], *outs[: len(out_shape)], *outs[len(out_shape) + 1 :])
            outs[len(out_shape)][...] = jnp.zeros((8, 128), F32)

        *values, token = pl.pallas_call(
            whole,
            grid_spec=pltpu.PrefetchScalarGridSpec(
                num_scalar_prefetch=scalars,
                grid=grid,
                in_specs=list(in_specs) + [ANY] * len(tokens),
                out_specs=list(out_specs) + [pl.BlockSpec((8, 128), lambda *_: (0, 0))],
                scratch_shapes=list(scratch),
            ),
            out_shape=list(out_shape) + [TOKEN],
            input_output_aliases=aliases or {},
            compiler_params=pltpu.CompilerParams(vmem_limit_bytes=VMEM),
            cost_estimate=pl.CostEstimate(flops=int(COST[name] * order.worth * 1e9), bytes_accessed=int(COST[name] * 1e6), transcendentals=0),
            name=name,
        )(*operands, *tokens)
        order.give(token)
        return values

    return run


class Order:
    def __init__(self):
        self.tokens, self.worth = [], 1.3

    def take(self):
        return self.tokens

    def give(self, token):
        self.tokens = [token]

    def after(self, *values):
        return call(
            lambda *refs: None,
            name="tie",
            grid=(1,),
            scalars=0,
            in_specs=[ANY] * len(values),
            out_specs=[ANY] * len(values),
            out_shape=[jax.ShapeDtypeStruct(v.shape, v.dtype) for v in values],
            aliases={i: i for i in range(len(values))},
            )(self, *values)


def xor_pairs(size, mask):
    return [(i, i ^ mask) for i in range(size)]


class LineGather:
    def __init__(self, own, size, place):
        self.size, self.place = size, place
        self.ups, self.downs = [own], [own]

    def step(self, order=None):
        k, size = len(self.ups), self.size
        if order is not None:
            if k == 1:
                self.ups = self.downs = order.after(self.ups[0])
                self.downs = list(self.downs)
            else:
                self.ups[-1], self.downs[-1] = order.after(self.ups[-1], self.downs[-1])
        up, down = self.ups[-1], self.downs[-1]
        self.ups.append(lax.ppermute(up, "tensor", [(i, i + 1) for i in range(k - 1, size - 1)]))
        self.downs.append(lax.ppermute(down, "tensor", [(i + 1, i) for i in range(0, size - k)]))

    def hold(self, order):
        self.ups[-1], self.downs[-1] = order.after(self.ups[-1], self.downs[-1])

    def slot(self, j):
        groups = {}
        for at in range(self.size):
            groups.setdefault((at ^ j) - at, []).append(at)
        value = None
        for off, places in groups.items():
            arr = self.downs[off] if off >= 0 else self.ups[-off]
            if value is None:
                value = arr
            else:
                here = functools.reduce(jnp.logical_or, [self.place == at for at in places])
                value = jnp.where(here, arr, value)
        return value


def exchange(values):
    return lax.all_to_all(values, "tensor", 0, 0, tiled=True)


def rows_at(values, block, rows):
    return lax.dynamic_slice_in_dim(values, block * rows, rows, axis=0)


def cols_at(values, block, cols):
    return lax.dynamic_slice_in_dim(values, block * cols, cols, axis=1)


def give_body(places, left, right, out):
    out[...] = dot(left[...], right[...]).astype(BF)


def give_second_body(places, left, right, out):
    out[...] = second((left, right), None).astype(BF)


def second(refs, rows):
    left, right = refs
    total, t = None, left.shape[2]
    for k in range(left.shape[0]):
        part = left[k] if rows is None else left[k, rows, :]
        term = dot(part, right[k * t : (k + 1) * t, :])
        total = term if total is None else total + term
    return total


def keep_body(places, *refs, two, last, lanes, chunks):
    ins = 4 if two else 2
    gots, outs = refs[ins : ins + (2 if two else 1)], refs[ins + (2 if two else 1) :]
    step = pl.program_id(0)
    rows = outs[0].shape[0]
    for lane in range(lanes):
        for rel in (1, 0):
            at = pl.multiple_of((places[1 + lane] ^ rel) * rows, rows)
            place = pl.ds(at, rows)
            out = outs[2 * lane + rel]
            inside = (step >= lane * chunks) & (step < (lane + 1) * chunks)

            @pl.when((inside & (step < last)) if two else inside)
            def _():
                total = dot(refs[0][place, :], refs[1][...])
                out[...] = (total + gots[0][place, :].astype(F32)).astype(BF)

            if two and lane == lanes - 1:

                @pl.when(step == last)
                def _():
                    total = second(refs[2:4], place)
                    out[...] = (total + gots[1][place, :].astype(F32)).astype(BF)


def fold_body(places, *refs):
    ins, outs = refs[:4], refs[4:]
    for h in (0, 1):
        total = (ins[2 * h][...].astype(F32) + ins[2 * h + 1][...].astype(F32)).astype(BF)
        if len(outs) == 2:
            outs[h][...] = total
        else:
            for rel in (0, 1):

                @pl.when(pl.program_id(0) == rel)
                def _():
                    outs[2 * h + rel][...] = total


def spread_body(places, *refs):
    ins, outs = refs[:4], refs[4:]
    for k in (0, 1):

        @pl.when(pl.program_id(0) == k)
        def _():
            for h in (0, 1):
                outs[h][...] = ins[2 * h + k][...]


def join_body(places, *refs):
    pieces, out = refs[:-1], refs[-1]
    step = pl.program_id(0) * 2 + pl.program_id(1)
    for k, piece in enumerate(pieces):

        @pl.when(step == k)
        def _():
            out[...] = piece[...]


def finish_body(place, source, *refs, turned, count):
    at, outs = 0, refs[-count:]
    for k, out in enumerate(outs):
        flip = turned and k == count - 1
        width = out.shape[0] if flip else out.shape[1]
        value = source[:, at : at + width].astype(F32)
        out[...] = value.T if flip else value
        at += width


class Product:
    def __init__(self, left, right, widths, firsts, pair=()):
        self.left, self.right, self.widths, self.firsts, self.pair = left, right, widths, firsts, pair
        self.rows = left.shape[0] // 2
        self.cols = right.shape[1] + (pair[1].shape[1] if pair else 0)
        self.bn = min(512, widths[-1])
        self.gots = []


class Gradients:
    def __init__(self, products, count):
        self.count = count
        self.bits = count.bit_length() - 1
        self.index = lax.axis_index("dp")
        self.orders = [list(range(1, self.bits)), list(range(self.bits - 1, 0, -1))]
        self.step = 0
        self.kept, self.gots = [], []
        per = 2 // len(products)
        self.products = [
            Product(*p[:3], [o[0] for o in self.orders[i * per : (i + 1) * per]], p[3:])
            for i, p in enumerate(products)
        ]

    def bit(self, b):
        return (self.index >> b) & 1

    def scalars(self, *values):
        return jnp.stack([jnp.asarray(v, jnp.int32) for v in values])

    def swap(self, value, b):
        return lax.ppermute(value, "dp", xor_pairs(self.count, 1 << b))

    def operands(self, p, core):
        tokens, last = p.right.shape[0], p.right.shape[1] // p.bn
        specs = [
            pl.BlockSpec((p.rows, tokens), lambda n, s: (s[0], 0)),
            pl.BlockSpec((tokens, p.bn), lambda n, s: (0, jnp.minimum(n, last - 1))),
        ]
        if p.pair:
            count, _, t = p.pair[0].shape
            specs += [
                pl.BlockSpec((count, p.rows, t), lambda n, s: (0, s[0], 0)),
                pl.BlockSpec((tokens, p.bn), lambda n, s: (0, 0)),
            ]
        return specs, [p.left, p.right, *p.pair], dict(two=bool(p.pair), last=last)

    def give(self, order, at=0, second=False):
        p = self.products[at]
        specs, values, facts = self.operands(p, 1 - self.bit(0))
        some = slice(2, 4) if second else slice(0, 2)
        cols = values[some][1].shape[1]
        (out,) = call(
            give_second_body if second else give_body,
            name="give_second" if second else "give",
            grid=(cols // p.bn,),
            scalars=1,
            in_specs=specs[some],
            out_specs=[pl.BlockSpec((p.rows, p.bn), lambda n, s: (0, n))],
            out_shape=[jax.ShapeDtypeStruct((p.rows, cols), BF)],
        )(order, self.scalars(1 - self.bit(0)), *values[some])
        p.gots.append(self.swap(out, 0))

    def keep(self, order, at=0):
        p = self.products[at]
        lanes = len(p.firsts)
        rows, cols = p.rows // 2, p.cols // lanes
        chunks = cols // p.bn
        specs, values, facts = self.operands(p, self.bit(0))

        def out_spec(lane):
            return pl.BlockSpec(
                (rows, p.bn), lambda n, s: (0, jnp.clip(n - lane * chunks, 0, chunks - 1))
            )

        outs = call(
            functools.partial(keep_body, lanes=lanes, chunks=chunks, **facts),
            name="keep",
            grid=(lanes * chunks,),
            scalars=1,
            in_specs=specs
            + [
                pl.BlockSpec((p.rows, p.bn), lambda n, s: (0, jnp.minimum(n, facts["last"] - 1))),
                pl.BlockSpec((p.rows, p.bn), lambda n, s: (0, 0)),
            ][: len(p.gots)],
            out_specs=[out_spec(k // 2) for k in range(2 * lanes)],
            out_shape=[jax.ShapeDtypeStruct((rows, cols), BF)] * (2 * lanes),
        )(order, self.scalars(self.bit(0), *[self.bit(b) for b in p.firsts]), *values, *p.gots)
        for h in range(lanes):
            self.kept.append(outs[2 * h])
            self.gots.append(self.swap(outs[2 * h + 1], p.firsts[h]))

    def fold(self, order):
        rows, cols = self.kept[0].shape
        self.step += 1
        more = self.step < self.bits - 1
        nexts = [self.bit(o[self.step]) for o in self.orders] if more else [0, 0]
        orows = rows // 2 if more else rows
        spec = lambda h: pl.BlockSpec((orows, cols), lambda r, s: (s[h] ^ r, 0))
        outs = call(
            fold_body,
            name="fold",
            grid=(2 if more else 1,),
            scalars=1,
            in_specs=[spec(0), spec(0), spec(1), spec(1)],
            out_specs=[pl.BlockSpec((orows, cols), lambda r, s: (0, 0))] * (4 if more else 2),
            out_shape=[jax.ShapeDtypeStruct((orows, cols), BF)] * (4 if more else 2),
        )(order, self.scalars(*nexts), self.kept[0], self.gots[0], self.kept[1], self.gots[1])
        self.kept = outs[:: 2 if more else 1]
        if more:
            self.gots = [self.swap(outs[1 + 2 * h], self.orders[h][self.step]) for h in (0, 1)]
        else:
            self.ask()

    def hold(self, order):
        self.gots = order.after(*self.gots)

    def ask(self):
        self.step -= 1
        self.gots = [self.swap(k, o[self.step]) for k, o in zip(self.kept, self.orders)]

    def spread(self, order):
        rows, cols = self.kept[0].shape
        spec = pl.BlockSpec((rows, cols), lambda k, s: (0, 0))
        self.kept = call(
            spread_body,
            name="spread",
            grid=(2,),
            scalars=1,
            in_specs=[spec] * 4,
            out_specs=[
                pl.BlockSpec((rows, cols), lambda k, s: (k ^ s[0], 0)),
                pl.BlockSpec((rows, cols), lambda k, s: (k ^ s[1], 0)),
            ],
            out_shape=[jax.ShapeDtypeStruct((2 * rows, cols), BF)] * 2,
        )(
            order,
            self.scalars(*[self.bit(o[self.step]) for o in self.orders]),
            self.kept[0],
            self.gots[0],
            self.kept[1],
            self.gots[1],
        )
        self.ask()

    def join(self, order):
        brows, bcols = self.kept[0].shape
        lane = 0
        for p in self.products:
            lanes = range(lane, lane + len(p.firsts))
            lane += len(p.firsts)
            (p.half,) = call(
                join_body,
                name="join",
                grid=(len(lanes), 2),
                scalars=1,
                in_specs=[pl.BlockSpec((brows, bcols), lambda h, k, s: (0, 0))] * (2 * len(lanes)),
                out_specs=[pl.BlockSpec((brows, bcols), lambda h, k, s: (k ^ s[h], h))],
                out_shape=[jax.ShapeDtypeStruct((p.rows, p.cols), BF)],
            )(
                order,
                self.scalars(*[self.bit(self.orders[l][self.step]) for l in lanes]),
                *[v for l in lanes for v in (self.kept[l], self.gots[l])],
            )
            p.other = self.swap(p.half, 0)

    def finish(self, order, at=0):
        outs = self.fill(order, at, 0)
        return self.fill(order, at, 1, outs)

    def fill(self, order, at, other, ahead=()):
        p = self.products[at]
        rows, cols = p.half.shape
        crows = min(256, rows)
        nblk = rows // crows
        turned = bool(p.pair)
        specs = [pl.BlockSpec((crows, w), lambda b, s: (s[0] * nblk + b, 0)) for w in p.widths]
        shapes = [jax.ShapeDtypeStruct((2 * rows, w), F32) for w in p.widths]
        if turned:
            w = p.widths[-1]
            specs[-1] = pl.BlockSpec((w, crows), lambda b, s: (0, s[0] * nblk + b))
            shapes[-1] = jax.ShapeDtypeStruct((w, 2 * rows), F32)
        return call(
            functools.partial(finish_body, turned=turned, count=len(specs)),
            name="finish",
            grid=(nblk,),
            scalars=1,
            in_specs=[pl.BlockSpec((crows, cols), lambda b, s: (b, 0))] + [ANY] * len(ahead),
            out_specs=specs,
            out_shape=shapes,
            aliases={2 + k: k for k in range(len(ahead))},
        )(order, self.scalars(self.bit(0) ^ other), p.other if other else p.half, *ahead)


class GainTotals:
    def __init__(self, parts, dp, tensor):
        self.size = parts[0].size
        self.value = jnp.concatenate([p.reshape(-1, 128) for p in parts], axis=0)
        self.left = [
            (name, size, [1 << k])
            for name, size in (("tensor", tensor), ("dp", dp))
            for k in range(size.bit_length() - 1)
        ]
        self.next()

    def next(self):
        name, size, masks = self.left.pop(0)
        self.got = [lax.ppermute(self.value, name, xor_pairs(size, m)) for m in masks]

    def step(self, order):
        self.value, *got = order.after(self.value, *self.got)
        self.value = self.value + got[0]
        if self.left:
            self.next()

    def split(self, order):
        while self.left:
            self.step(order)
        self.step(order)
        value = self.value.reshape(-1)
        return [value[k : k + self.size] for k in range(0, value.size, self.size)]


def qkv_body(*refs):
    chunk, rows, wq, wk, wv, cos, sin = refs[:7]
    q_out, k_out, v_out, rows_out = refs[-4:]
    x = rows[...]
    cosine, sine = cos[...], sin[...]

    def turned(pre):
        out = []
        for h in range(pre.shape[1] // HD):
            one = pre[:, h * HD : (h + 1) * HD]
            out.append(one * cosine + pltpu.roll(one, HD // 2, 1) * sine)
        return jnp.concatenate(out, axis=1)

    q_out[...] = turned(dot(x, wq[...])).astype(BF)
    k_out[...] = turned(dot(x, wk[...])).astype(BF)
    v_out[...] = dot(x, wv[...]).astype(BF)
    part = rows_out.shape[0]
    rows_out[...] = rows[:, pl.ds(pl.multiple_of(pl.program_id(0) * part, part), part)].T


def qkv_slot(order, chunk, rows, w_query, w_key, w_value, cos, sin, held, count):
    t, d = rows.shape
    width = w_query.shape[1]
    bn = min(256, width)
    wspec = pl.BlockSpec((d, bn), lambda i, s: (0, i))
    tspec = pl.BlockSpec((t, HD), lambda i, s: (s[0], 0))
    return call(
        qkv_body,
        name="qkv",
        grid=(width // bn,),
        scalars=1,
        in_specs=[pl.BlockSpec((t, d), lambda i, s: (0, 0)), wspec, wspec, wspec, tspec, tspec]
        + [ANY] * len(held),
        out_specs=[pl.BlockSpec((t, bn), lambda i, s: (s[0], i))] * 3
        + [pl.BlockSpec((d // (width // bn), t), lambda i, s: (i, s[0]))],
        out_shape=[jax.ShapeDtypeStruct((count * t, width), BF)] * 3
        + [jax.ShapeDtypeStruct((d, count * t), BF)],
        aliases={7 + i: i for i in range(len(held))},
    )(order, chunk, rows, w_query, w_key, w_value, cos, sin, *held)


def attend_consts(seq_len):
    to_log2 = math.log2(math.e)
    return (to_log2 / math.sqrt(HD), math.log2(seq_len))


def attend_body(docs, q_ref, k_ref, v_ref, ids_col, ids_row, mix, acc, *, block):
    seq_len = q_ref.shape[0]
    scale, shift = attend_consts(seq_len)
    causal = lax.broadcasted_iota(jnp.int32, (block, block), 0) >= lax.broadcasted_iota(
        jnp.int32, (block, block), 1
    )

    def term(i, j):
        q = q_ref[i * block : (i + 1) * block, :]
        k = k_ref[j * block : (j + 1) * block, :]
        sig = 1.0 / (1.0 + jnp.exp2(shift - dot_nt(q, k) * scale))
        same = ids_col[i * block : (i + 1) * block, :] == ids_row[:, j * block : (j + 1) * block]
        allowed = same & causal if i == j else same
        probs = jnp.where(allowed, sig, 0.0).astype(BF)
        return dot(probs, v_ref[j * block : (j + 1) * block, :])

    for i in range(seq_len // block):
        acc[...] = term(i, i)
        for j in range(i):

            @pl.when(docs[(j + 1) * block - 1] == docs[i * block])
            def _():
                acc[...] += term(i, j)

        mix[i * block : (i + 1) * block, :] = acc[...].astype(BF)


def attend(order, docs, q, k, v):
    seq_len, width = q.shape
    block = 256
    head = pl.BlockSpec((seq_len, HD), lambda h, s: (0, h))
    return call(
        functools.partial(attend_body, block=block),
        name="attend",
        grid=(width // HD,),
        scalars=1,
        in_specs=[
            head,
            head,
            head,
            pl.BlockSpec((seq_len, 1), lambda h, s: (0, 0)),
            pl.BlockSpec((1, seq_len), lambda h, s: (0, 0)),
        ],
        out_specs=[head],
        out_shape=[jax.ShapeDtypeStruct((seq_len, width), BF)],
        scratch=[pltpu.VMEM((block, HD), F32)],
    )(order, docs, q, k, v, docs.reshape(-1, 1), docs.reshape(1, -1))


def attend_back_body(
    docs, q_ref, k_ref, v_ref, dmix, ids_col, ids_row, cos, sin, out, dq, dk, dv, *, block
):
    seq_len = q_ref.shape[0]
    scale, shift = attend_consts(seq_len)
    causal = lax.broadcasted_iota(jnp.int32, (block, block), 0) <= lax.broadcasted_iota(
        jnp.int32, (block, block), 1
    )

    def at(i):
        return slice(i * block, (i + 1) * block)

    def term(i, j):
        q, k, v, d = q_ref[at(i), :], k_ref[at(j), :], v_ref[at(j), :], dmix[at(i), :]
        sig = 1.0 / (1.0 + jnp.exp2(shift - dot_nt(k, q) * scale))
        same = ids_col[at(j), :] == ids_row[:, at(i)]
        allowed = same & causal if i == j else same
        probs = jnp.where(allowed, sig, 0.0)
        d_scores = (dot_nt(v, d) * probs * (1.0 - probs)).astype(BF)
        return dot_tn(d_scores, k), dot(d_scores, q), dot(probs.astype(BF), d)

    for i in range(seq_len // block):
        dq[at(i), :], dk[at(i), :], dv[at(i), :] = term(i, i)
    for i in range(seq_len // block):
        for j in range(i):

            @pl.when(docs[(j + 1) * block - 1] == docs[i * block])
            def _():
                a, b, c = term(i, j)
                dq[at(i), :] += a
                dk[at(j), :] += b
                dv[at(j), :] += c

    cosine, sine = cos[...], sin[...]

    def turned_back(v):
        v = v * (1.0 / math.sqrt(HD))
        return (v * cosine - pltpu.roll(v, HD // 2, 1) * sine).astype(BF)

    width = out.shape[1] // 3
    at_head = pl.program_id(0) * HD
    for part, value in enumerate((turned_back(dq[...]), turned_back(dk[...]), dv[...].astype(BF))):
        out[:, pl.ds(pl.multiple_of(at_head + part * width, HD), HD)] = value


def attend_back(order, docs, q, k, v, d_mix, cos, sin):
    seq_len, width = q.shape
    head = pl.BlockSpec((seq_len, HD), lambda h, s: (0, h))
    whole = lambda r, c: pl.BlockSpec((r, c), lambda h, s: (0, 0))
    return call(
        functools.partial(attend_back_body, block=256),
        name="attend_back",
        grid=(width // HD,),
        scalars=1,
        in_specs=[head] * 4
        + [whole(seq_len, 1), whole(1, seq_len), whole(seq_len, HD), whole(seq_len, HD)],
        out_specs=[whole(seq_len, 3 * width)],
        out_shape=[jax.ShapeDtypeStruct((seq_len, 3 * width), BF)],
        scratch=[pltpu.VMEM((seq_len, HD), F32)] * 3,
    )(order, docs, q, k, v, d_mix, docs.reshape(-1, 1), docs.reshape(1, -1), cos, sin)


def project_body(mix, w_ref, x_ref, gain, resid, normed, acc):
    parts, _, cols = w_ref.shape
    step = pl.program_id(0)

    @pl.when(step == 0)
    def _():
        acc[...] = x_ref[...].astype(F32)

    for p in range(parts):
        acc[:, p * cols : (p + 1) * cols] += dot(mix[...], w_ref[p])

    @pl.when(step == pl.num_programs(0) - 1)
    def _():
        resid[...] = acc[...]
        normed[...] = rms_scale(acc[...], gain[...]).astype(BF)


def project(order, mix, w_out, x, gain):
    t, d = x.shape
    width = mix.shape[1]
    parts, _, cols = w_out.shape
    whole = lambda r, c: pl.BlockSpec((r, c), lambda i: (0, 0))
    return call(
        project_body,
        name="project",
        grid=(mix.shape[0] // t,),
        scalars=0,
        in_specs=[
            pl.BlockSpec((t, width), lambda i: (i, 0)),
            pl.BlockSpec((parts, width, cols), lambda i: (0, i, 0)),
            whole(t, d),
            whole(1, d),
        ],
        out_specs=[whole(t, d)] * 2,
        out_shape=[jax.ShapeDtypeStruct((t, d), F32), jax.ShapeDtypeStruct((t, d), BF)],
        scratch=[pltpu.VMEM((t, d), F32)],
    )(order, mix, w_out, x, gain.reshape(1, -1))


def norm_back(d_normed, rows, gain):
    r = lax.rsqrt(jnp.mean(rows * rows, axis=-1, keepdims=True) + EPS)
    u = rows * r
    scaled = d_normed * gain
    d_rows = r * (scaled - u * jnp.mean(scaled * u, axis=-1, keepdims=True))
    return d_rows, jnp.sum(d_normed * u, axis=0, keepdims=True)


def middle_body(d_ref, resid, cot, gain, w_ref, out, d_resid, low_t, part, low):
    parts, _, cols = w_ref.shape

    @pl.when(pl.program_id(0) == 0)
    def _():
        d_rows, part[...] = norm_back(d_ref[...].astype(F32), resid[...], gain[...])
        total = cot[...].astype(F32) + d_rows
        d_resid[...] = total
        low[...] = total.astype(BF)
        low_t[...] = low[...].T

    total = None
    for p in range(parts):
        term = dot_nt(low[:, p * cols : (p + 1) * cols], w_ref[p])
        total = term if total is None else total + term
    out[...] = total.astype(BF)


def middle(order, d_normed2, resid, cot, gain, w_out, width):
    t, d = resid.shape
    parts, rows, cols = w_out.shape
    count = rows // width
    whole = lambda r, c: pl.BlockSpec((r, c), lambda i: (0, 0))
    return call(
        middle_body,
        name="middle",
        grid=(count,),
        scalars=0,
        in_specs=[whole(t, d)] * 3
        + [whole(1, d), pl.BlockSpec((parts, width, cols), lambda i: (0, i, 0))],
        out_specs=[
            pl.BlockSpec((t, width), lambda i: (i, 0)),
            whole(t, d),
            whole(d, t),
            whole(1, d),
        ],
        out_shape=[
            jax.ShapeDtypeStruct((count * t, width), BF),
            jax.ShapeDtypeStruct((t, d), F32),
            jax.ShapeDtypeStruct((d, t), BF),
            jax.ShapeDtypeStruct((1, d), F32),
        ],
        scratch=[pltpu.VMEM((t, d), BF)],
    )(order, d_normed2, resid, cot, gain.reshape(1, -1), w_out)


def last_body(d_ref, x_ref, d_resid, gain, out, part):
    d_rows, part[...] = norm_back(d_ref[...].astype(F32), x_ref[...].astype(F32), gain[...])
    out[...] = (d_resid[...] + d_rows).astype(BF)


def last(order, d_normed, x, d_resid, gain):
    t, d = x.shape
    whole = lambda r, c: pl.BlockSpec((r, c), lambda i: (0, 0))
    return call(
        last_body,
        name="last",
        grid=(1,),
        scalars=0,
        in_specs=[whole(t, d)] * 3 + [whole(1, d)],
        out_specs=[whole(t, d), whole(1, d)],
        out_shape=[jax.ShapeDtypeStruct((t, d), BF), jax.ShapeDtypeStruct((1, d), F32)],
    )(order, d_normed, x, d_resid, gain.reshape(1, -1))


def back_project_body(d_ref, wq, wk, wv, out):
    total = None
    width = wq.shape[1]
    for k, w in enumerate((wq, wk, wv)):
        term = dot_nt(d_ref[:, k * width : (k + 1) * width], w[...])
        total = term if total is None else total + term
    out[...] = total.astype(BF)


def back_project(order, d_qkv, w_query, w_key, w_value):
    seq_len, wide = d_qkv.shape
    d, width = w_query.shape
    bn = 512
    wspec = pl.BlockSpec((bn, width), lambda i: (i, 0))
    return call(
        back_project_body,
        name="back_project",
        grid=(d // bn,),
        scalars=0,
        in_specs=[pl.BlockSpec((seq_len, wide), lambda i: (0, 0)), wspec, wspec, wspec],
        out_specs=[pl.BlockSpec((seq_len, bn), lambda i: (0, i))],
        out_shape=[jax.ShapeDtypeStruct((seq_len, d), BF)],
    )(order, d_qkv, w_query, w_key, w_value)[0]


def ffn_body(*refs):
    chunk, rows, cot, wg, wu, wd = refs[:6]
    inner, d_gate, d_up, rows_out, cot_out, d_rows, down, acc_d, acc_o = refs[-9:]
    step, last = pl.program_id(0), pl.num_programs(0) - 1
    x = rows[...]
    gate = dot(x, wg[...])
    up = dot(x, wu[...])
    sig = sigmoid(gate)
    silu = gate * sig
    inner_b = (silu * up).astype(BF)
    inner[...] = inner_b.T
    part = rows_out.shape[0]
    rows_out[...] = rows[:, pl.ds(pl.multiple_of(step * part, part), part)].T
    d_inner = dot_nt(cot[...], wd[...])
    dg = (d_inner * up * (sig * (1.0 + gate * (1.0 - sig)))).astype(BF)
    du = (d_inner * silu).astype(BF)
    d_gate[...] = dg
    d_up[...] = du
    term_o = dot(inner_b, wd[...])
    term_d = dot_nt(dg, wg[...]) + dot_nt(du, wu[...])

    @pl.when(step == 0)
    def _():
        acc_o[...] = term_o
        acc_d[...] = term_d
        cot_out[...] = cot[...]

    @pl.when(step > 0)
    def _():
        acc_o[...] += term_o
        acc_d[...] += term_d

    @pl.when(step == last)
    def _():
        d_rows[...] = acc_d[...].astype(BF)
        down[...] = acc_o[...].astype(BF)


def ffn_slot(order, chunk, rows, cot, w_gate, w_up, w_down, held, count):
    t, d = rows.shape
    hidden = w_gate.shape[1]
    bh = min(512, hidden)
    steps = hidden // bh
    wcol = pl.BlockSpec((d, bh), lambda i, s: (0, i))
    part = pl.BlockSpec((t, bh), lambda i, s: (s[0], i))
    line = pl.BlockSpec((t, d), lambda i, s: (s[0], 0))
    return call(
        ffn_body,
        name="ffn",
        grid=(hidden // bh,),
        scalars=1,
        in_specs=[
            pl.BlockSpec((t, d), lambda i, s: (0, 0)),
            pl.BlockSpec((t, d), lambda i, s: (0, 0)),
            wcol,
            wcol,
            pl.BlockSpec((bh, d), lambda i, s: (i, 0)),
        ]
        + [ANY] * len(held),
        out_specs=[pl.BlockSpec((bh, t), lambda i, s: (i, s[0])), part, part]
        + [pl.BlockSpec((d // steps, t), lambda i, s: (i, s[0])), line, line, line],
        out_shape=[jax.ShapeDtypeStruct((hidden, count * t), BF)]
        + [jax.ShapeDtypeStruct((count * t, hidden), BF)] * 2
        + [jax.ShapeDtypeStruct((d, count * t), BF)]
        + [jax.ShapeDtypeStruct((count * t, d), BF)] * 3,
        scratch=[pltpu.VMEM((t, d), F32)] * 2,
        aliases={6 + i: i for i in range(len(held))},
    )(order, chunk, rows, cot, w_gate, w_up, w_down, *held)


def local(
    layer_in,
    cotangent,
    doc_ids,
    positions,
    attn_gain,
    w_query,
    w_key,
    w_value,
    w_out,
    ffn_gain,
    w_gate,
    w_up,
    w_down,
    *,
    dp,
    tensor,
):
    t, d = layer_in.shape
    width = w_query.shape[1]
    hidden = w_gate.shape[1]
    place = lax.axis_index("tensor")
    chunks = jnp.stack([place ^ j for j in range(tensor)]).astype(jnp.int32)
    chunk = [chunks[j : j + 1] for j in range(tensor)]
    order = Order()

    share = w_out.shape[1] // dp
    w_cols = lax.all_gather(
        cols_at(w_out, lax.axis_index("dp"), share), "tensor", axis=0, tiled=True
    )
    half = HD // 2
    freqs = ROPE_BASE ** (-(jnp.arange(half).astype(F32) * 2.0) / HD)
    angles = positions.astype(F32)[:, None] * freqs[None, :]
    cosine, sine = jnp.cos(angles), jnp.sin(angles)
    cos = jnp.concatenate([cosine, cosine], axis=1)
    sin = jnp.concatenate([-sine, sine], axis=1)

    normed_own = rms_scale(layer_in.astype(F32), attn_gain).astype(BF)
    line = LineGather(normed_own, tensor, place)
    line.step()
    held = []
    for j in range(tensor):
        if 0 < j < tensor - 1:
            line.step(order)
        if j == tensor - 1:
            cots = LineGather(cotangent, tensor, place)
            cots.step(order)
        usual, order.worth = order.worth, 20 if j == tensor - 1 else order.worth
        held = qkv_slot(order, chunk[j], line.slot(j), w_query, w_key, w_value, cos, sin, held, tensor)
        order.worth = usual
        if j == min(2, tensor - 1):
            (w_cols,) = order.after(w_cols)
            w_out_all = lax.all_gather(w_cols, "dp", axis=0)
    query, key, value, normed_t = held
    (mixed,) = attend(order, doc_ids, query, key, value)
    mix = exchange(mixed)
    cots.step(order)
    (cot_first,) = order.after(cots.slot(1))
    resid, normed2_own = project(order, mix, w_out_all, layer_in, ffn_gain)

    weights = (w_gate, w_up, w_down)
    line = LineGather(normed2_own, tensor, place)
    line.step()
    held = ffn_slot(order, chunk[0], line.slot(0), cotangent, *weights, [], tensor)
    for j in range(1, tensor):
        if j < tensor - 1:
            line.step(order)
            if len(cots.ups) < tensor:
                cots.step(order)
        else:
            cots.hold(order)
            line.hold(order)
        cot = cot_first if j == 1 else cots.slot(j)
        held = ffn_slot(order, chunk[j], line.slot(j), cot, *weights, held, tensor)
    inner_t, d_gate, d_up, normed2_t, cot_all, d_normed2_part, down_part = held
    d_normed2 = lax.psum_scatter(d_normed2_part, "tensor", scatter_dimension=0, tiled=True)

    first = Gradients([(inner_t, cot_all, [d])], dp)
    wide = Gradients([(normed2_t, d_gate, [hidden]), (normed2_t, d_up, [hidden])], dp)
    more = range(first.bits - 2)

    usual = order.worth
    first.give(order)
    wide.give(order, 0)
    first.keep(order)
    wide.give(order, 1)
    order.worth = 10
    first.fold(order)
    order.worth = usual
    wide.keep(order, 0)
    wide.keep(order, 1)
    d_mix, d_resid, d_resid_t, ffn_gain_part = middle(
        order, d_normed2, resid, cotangent, ffn_gain, w_out_all, width
    )
    d_mix = exchange(d_mix)
    d_resid_all = lax.all_gather(d_resid_t, "tensor", axis=0)
    for _ in more:
        first.fold(order)
    wide.fold(order)
    for _ in more:
        first.spread(order)
    (d_qkv,) = attend_back(order, doc_ids, query, key, value, d_mix, cos, sin)
    attn = Gradients([(normed_t, d_qkv, [width] * 4, d_resid_all, mixed)], dp)
    attn.give(order)
    for _ in more:
        wide.fold(order)
    first.join(order)
    attn.give(order, second=True)
    d_normed = lax.psum_scatter(
        back_project(order, d_qkv, w_query, w_key, w_value),
        "tensor",
        scatter_dimension=0,
        tiled=True,
    )
    wide.hold(order)
    for _ in more:
        wide.spread(order)
    attn.keep(order)
    down_grad = first.fill(order, 0, 0)
    (down_grad,) = first.fill(order, 0, 1, down_grad)
    wide.hold(order)
    order.worth = 0.3
    wide.join(order)
    attn.hold(order)
    order.worth = 10
    attn.fold(order)
    down_sum = lax.psum_scatter(
        order.after(down_part)[0], "tensor", scatter_dimension=0, tiled=True
    )
    gate_grad = wide.fill(order, 0, 0)
    order.worth = 1.3
    for _ in more:
        attn.fold(order)
    up_grad = wide.fill(order, 1, 0)
    in_grad, attn_gain_part = last(order, d_normed, layer_in, d_resid, attn_gain)
    totals = GainTotals([attn_gain_part, ffn_gain_part], dp, tensor)
    attn.hold(order)
    for _ in more:
        attn.spread(order)
    totals.step(order)
    (gate_grad,) = wide.fill(order, 0, 1, gate_grad)
    totals.step(order)
    (up_grad,) = wide.fill(order, 1, 1, up_grad)
    order.worth = 0.02
    totals.step(order)
    attn.join(order)
    attn_grads = attn.fill(order, 0, 0)
    totals.step(order)
    (down_sum,) = order.after(down_sum)
    query_grad, key_grad, value_grad, out_grad = attn.fill(order, 0, 1, attn_grads)
    attn_gain_grad, ffn_gain_grad = totals.split(order)
    layer_out = (resid + down_sum.astype(F32)).astype(BF)
    return (
        layer_out,
        in_grad,
        attn_gain_grad,
        query_grad,
        key_grad,
        value_grad,
        out_grad,
        ffn_gain_grad,
        gate_grad,
        up_grad,
        down_grad,
    )


def solution(mesh):
    rows, cols, lines = P(("dp", "tensor"), None), P(None, "tensor"), P("tensor", None)
    return jax.shard_map(
        functools.partial(local, dp=mesh.shape["dp"], tensor=mesh.shape["tensor"]),
        mesh=mesh,
        in_specs=(
            rows, rows, P("dp"), P("dp"), P(), cols, cols, cols, lines, P(), cols, cols, lines
        ),
        out_specs=(rows, rows, P(), cols, cols, cols, lines, P(), cols, cols, lines),
        check_vma=False,
    )
```

```python
import functools
import math

import jax
import jax.numpy as jnp
from jax import lax
from jax.experimental import pallas as pl
from jax.experimental.pallas import tpu as pltpu
from jax.sharding import PartitionSpec as P

HD = 128
EPS = 1e-05
ROPE_BASE = 500000.0
BF = jnp.bfloat16
F32 = jnp.float32
VMEM = 56 << 20
COST = {
    "give": 8, "give_second": 2.5, "keep": 10, "fold": 4, "spread": 4, "join": 4.5, "finish": 5.5, "middle": 9.5, "attend": 11,
    "attend_back": 17, "back_project": 11, "qkv": 5.6, "project": 8.6, "ffn": 22, "last": 5, "tie": 0.5,
}


def dot(left, right):
    return lax.dot_general(left, right, (((1,), (0,)), ((), ())), preferred_element_type=F32)


def dot_nt(left, right):
    return lax.dot_general(left, right, (((1,), (1,)), ((), ())), preferred_element_type=F32)


def dot_tn(left, right):
    return lax.dot_general(left, right, (((0,), (0,)), ((), ())), preferred_element_type=F32)


def sigmoid(v):
    return 1.0 / (1.0 + jnp.exp(-v))


def rms_scale(values, gain):
    return values * lax.rsqrt(jnp.mean(values * values, axis=-1, keepdims=True) + EPS) * gain


ANY = pl.BlockSpec(memory_space=pl.ANY)
TOKEN = jax.ShapeDtypeStruct((8, 128), F32)


def call(body, *, name, grid, scalars, in_specs, out_specs, out_shape, scratch=(), aliases=None):
    def run(order, *operands):
        tokens = order.take()
        ahead = scalars + len(in_specs)

        def whole(*refs):
            outs = refs[ahead + len(tokens) :]
            body(*refs[:ahead], *outs[: len(out_shape)], *outs[len(out_shape) + 1 :])
            outs[len(out_shape)][...] = jnp.zeros((8, 128), F32)

        *values, token = pl.pallas_call(
            whole,
            grid_spec=pltpu.PrefetchScalarGridSpec(
                num_scalar_prefetch=scalars,
                grid=grid,
                in_specs=list(in_specs) + [ANY] * len(tokens),
                out_specs=list(out_specs) + [pl.BlockSpec((8, 128), lambda *_: (0, 0))],
                scratch_shapes=list(scratch),
            ),
            out_shape=list(out_shape) + [TOKEN],
            input_output_aliases=aliases or {},
            compiler_params=pltpu.CompilerParams(vmem_limit_bytes=VMEM),
            cost_estimate=pl.CostEstimate(flops=int(COST[name] * order.worth * 1e9), bytes_accessed=int(COST[name] * 1e6), transcendentals=0),
            name=name,
        )(*operands, *tokens)
        order.give(token)
        return values

    return run


class Order:
    def __init__(self):
        self.tokens, self.worth = [], 1.3

    def take(self):
        return self.tokens

    def give(self, token):
        self.tokens = [token]

    def after(self, *values):
        return call(
            lambda *refs: None,
            name="tie",
            grid=(1,),
            scalars=0,
            in_specs=[ANY] * len(values),
            out_specs=[ANY] * len(values),
            out_shape=[jax.ShapeDtypeStruct(v.shape, v.dtype) for v in values],
            aliases={i: i for i in range(len(values))},
            )(self, *values)


def xor_pairs(size, mask):
    return [(i, i ^ mask) for i in range(size)]


class LineGather:
    def __init__(self, own, size, place):
        self.size, self.place = size, place
        self.ups, self.downs = [own], [own]

    def step(self, order=None):
        k, size = len(self.ups), self.size
        if order is not None:
            if k == 1:
                self.ups = self.downs = order.after(self.ups[0])
                self.downs = list(self.downs)
            else:
                self.ups[-1], self.downs[-1] = order.after(self.ups[-1], self.downs[-1])
        up, down = self.ups[-1], self.downs[-1]
        self.ups.append(lax.ppermute(up, "tensor", [(i, i + 1) for i in range(k - 1, size - 1)]))
        self.downs.append(lax.ppermute(down, "tensor", [(i + 1, i) for i in range(0, size - k)]))

    def hold(self, order):
        self.ups[-1], self.downs[-1] = order.after(self.ups[-1], self.downs[-1])

    def slot(self, j):
        groups = {}
        for at in range(self.size):
            groups.setdefault((at ^ j) - at, []).append(at)
        value = None
        for off, places in groups.items():
            arr = self.downs[off] if off >= 0 else self.ups[-off]
            if value is None:
                value = arr
            else:
                here = functools.reduce(jnp.logical_or, [self.place == at for at in places])
                value = jnp.where(here, arr, value)
        return value


def exchange(values):
    return lax.all_to_all(values, "tensor", 0, 0, tiled=True)


def rows_at(values, block, rows):
    return lax.dynamic_slice_in_dim(values, block * rows, rows, axis=0)


def cols_at(values, block, cols):
    return lax.dynamic_slice_in_dim(values, block * cols, cols, axis=1)


def give_body(places, left, right, out):
    out[...] = dot(left[...], right[...]).astype(BF)


def give_second_body(places, left, right, out):
    out[...] = second((left, right), None).astype(BF)


def second(refs, rows):
    left, right = refs
    total, t = None, left.shape[2]
    for k in range(left.shape[0]):
        part = left[k] if rows is None else left[k, rows, :]
        term = dot(part, right[k * t : (k + 1) * t, :])
        total = term if total is None else total + term
    return total


def keep_body(places, *refs, two, last, lanes, chunks):
    ins = 4 if two else 2
    gots, outs = refs[ins : ins + (2 if two else 1)], refs[ins + (2 if two else 1) :]
    step = pl.program_id(0)
    rows = outs[0].shape[0]
    for lane in range(lanes):
        for rel in (1, 0):
            at = pl.multiple_of((places[1 + lane] ^ rel) * rows, rows)
            place = pl.ds(at, rows)
            out = outs[2 * lane + rel]
            inside = (step >= lane * chunks) & (step < (lane + 1) * chunks)

            @pl.when((inside & (step < last)) if two else inside)
            def _():
                total = dot(refs[0][place, :], refs[1][...])
                out[...] = (total + gots[0][place, :].astype(F32)).astype(BF)

            if two and lane == lanes - 1:

                @pl.when(step == last)
                def _():
                    total = second(refs[2:4], place)
                    out[...] = (total + gots[1][place, :].astype(F32)).astype(BF)


def fold_body(places, *refs):
    ins, outs = refs[:4], refs[4:]
    for h in (0, 1):
        total = (ins[2 * h][...].astype(F32) + ins[2 * h + 1][...].astype(F32)).astype(BF)
        if len(outs) == 2:
            outs[h][...] = total
        else:
            for rel in (0, 1):

                @pl.when(pl.program_id(0) == rel)
                def _():
                    outs[2 * h + rel][...] = total


def spread_body(places, *refs):
    ins, outs = refs[:4], refs[4:]
    for k in (0, 1):

        @pl.when(pl.program_id(0) == k)
        def _():
            for h in (0, 1):
                outs[h][...] = ins[2 * h + k][...]


def join_body(places, *refs):
    pieces, out = refs[:-1], refs[-1]
    step = pl.program_id(0) * 2 + pl.program_id(1)
    for k, piece in enumerate(pieces):

        @pl.when(step == k)
        def _():
            out[...] = piece[...]


def finish_body(place, source, *refs, turned, count):
    at, outs = 0, refs[-count:]
    for k, out in enumerate(outs):
        flip = turned and k == count - 1
        width = out.shape[0] if flip else out.shape[1]
        value = source[:, at : at + width].astype(F32)
        out[...] = value.T if flip else value
        at += width


class Product:
    def __init__(self, left, right, widths, firsts, pair=()):
        self.left, self.right, self.widths, self.firsts, self.pair = left, right, widths, firsts, pair
        self.rows = left.shape[0] // 2
        self.cols = right.shape[1] + (pair[1].shape[1] if pair else 0)
        self.bn = min(512, widths[-1])
        self.gots = []


class Gradients:
    def __init__(self, products, count):
        self.count = count
        self.bits = count.bit_length() - 1
        self.index = lax.axis_index("dp")
        self.orders = [list(range(1, self.bits)), list(range(self.bits - 1, 0, -1))]
        self.step = 0
        self.kept, self.gots = [], []
        per = 2 // len(products)
        self.products = [
            Product(*p[:3], [o[0] for o in self.orders[i * per : (i + 1) * per]], p[3:])
            for i, p in enumerate(products)
        ]

    def bit(self, b):
        return (self.index >> b) & 1

    def scalars(self, *values):
        return jnp.stack([jnp.asarray(v, jnp.int32) for v in values])

    def swap(self, value, b):
        return lax.ppermute(value, "dp", xor_pairs(self.count, 1 << b))

    def operands(self, p, core):
        tokens, last = p.right.shape[0], p.right.shape[1] // p.bn
        specs = [
            pl.BlockSpec((p.rows, tokens), lambda n, s: (s[0], 0)),
            pl.BlockSpec((tokens, p.bn), lambda n, s: (0, jnp.minimum(n, last - 1))),
        ]
        if p.pair:
            count, _, t = p.pair[0].shape
            specs += [
                pl.BlockSpec((count, p.rows, t), lambda n, s: (0, s[0], 0)),
                pl.BlockSpec((tokens, p.bn), lambda n, s: (0, 0)),
            ]
        return specs, [p.left, p.right, *p.pair], dict(two=bool(p.pair), last=last)

    def give(self, order, at=0, second=False):
        p = self.products[at]
        specs, values, facts = self.operands(p, 1 - self.bit(0))
        some = slice(2, 4) if second else slice(0, 2)
        cols = values[some][1].shape[1]
        (out,) = call(
            give_second_body if second else give_body,
            name="give_second" if second else "give",
            grid=(cols // p.bn,),
            scalars=1,
            in_specs=specs[some],
            out_specs=[pl.BlockSpec((p.rows, p.bn), lambda n, s: (0, n))],
            out_shape=[jax.ShapeDtypeStruct((p.rows, cols), BF)],
        )(order, self.scalars(1 - self.bit(0)), *values[some])
        p.gots.append(self.swap(out, 0))

    def keep(self, order, at=0):
        p = self.products[at]
        lanes = len(p.firsts)
        rows, cols = p.rows // 2, p.cols // lanes
        chunks = cols // p.bn
        specs, values, facts = self.operands(p, self.bit(0))

        def out_spec(lane):
            return pl.BlockSpec(
                (rows, p.bn), lambda n, s: (0, jnp.clip(n - lane * chunks, 0, chunks - 1))
            )

        outs = call(
            functools.partial(keep_body, lanes=lanes, chunks=chunks, **facts),
            name="keep",
            grid=(lanes * chunks,),
            scalars=1,
            in_specs=specs
            + [
                pl.BlockSpec((p.rows, p.bn), lambda n, s: (0, jnp.minimum(n, facts["last"] - 1))),
                pl.BlockSpec((p.rows, p.bn), lambda n, s: (0, 0)),
            ][: len(p.gots)],
            out_specs=[out_spec(k // 2) for k in range(2 * lanes)],
            out_shape=[jax.ShapeDtypeStruct((rows, cols), BF)] * (2 * lanes),
        )(order, self.scalars(self.bit(0), *[self.bit(b) for b in p.firsts]), *values, *p.gots)
        for h in range(lanes):
            self.kept.append(outs[2 * h])
            self.gots.append(self.swap(outs[2 * h + 1], p.firsts[h]))

    def fold(self, order):
        rows, cols = self.kept[0].shape
        self.step += 1
        more = self.step < self.bits - 1
        nexts = [self.bit(o[self.step]) for o in self.orders] if more else [0, 0]
        orows = rows // 2 if more else rows
        spec = lambda h: pl.BlockSpec((orows, cols), lambda r, s: (s[h] ^ r, 0))
        outs = call(
            fold_body,
            name="fold",
            grid=(2 if more else 1,),
            scalars=1,
            in_specs=[spec(0), spec(0), spec(1), spec(1)],
            out_specs=[pl.BlockSpec((orows, cols), lambda r, s: (0, 0))] * (4 if more else 2),
            out_shape=[jax.ShapeDtypeStruct((orows, cols), BF)] * (4 if more else 2),
        )(order, self.scalars(*nexts), self.kept[0], self.gots[0], self.kept[1], self.gots[1])
        self.kept = outs[:: 2 if more else 1]
        if more:
            self.gots = [self.swap(outs[1 + 2 * h], self.orders[h][self.step]) for h in (0, 1)]
        else:
            self.ask()

    def hold(self, order):
        self.gots = order.after(*self.gots)

    def ask(self):
        self.step -= 1
        self.gots = [self.swap(k, o[self.step]) for k, o in zip(self.kept, self.orders)]

    def spread(self, order):
        rows, cols = self.kept[0].shape
        spec = pl.BlockSpec((rows, cols), lambda k, s: (0, 0))
        self.kept = call(
            spread_body,
            name="spread",
            grid=(2,),
            scalars=1,
            in_specs=[spec] * 4,
            out_specs=[
                pl.BlockSpec((rows, cols), lambda k, s: (k ^ s[0], 0)),
                pl.BlockSpec((rows, cols), lambda k, s: (k ^ s[1], 0)),
            ],
            out_shape=[jax.ShapeDtypeStruct((2 * rows, cols), BF)] * 2,
        )(
            order,
            self.scalars(*[self.bit(o[self.step]) for o in self.orders]),
            self.kept[0],
            self.gots[0],
            self.kept[1],
            self.gots[1],
        )
        self.ask()

    def join(self, order):
        brows, bcols = self.kept[0].shape
        lane = 0
        for p in self.products:
            lanes = range(lane, lane + len(p.firsts))
            lane += len(p.firsts)
            (p.half,) = call(
                join_body,
                name="join",
                grid=(len(lanes), 2),
                scalars=1,
                in_specs=[pl.BlockSpec((brows, bcols), lambda h, k, s: (0, 0))] * (2 * len(lanes)),
                out_specs=[pl.BlockSpec((brows, bcols), lambda h, k, s: (k ^ s[h], h))],
                out_shape=[jax.ShapeDtypeStruct((p.rows, p.cols), BF)],
            )(
                order,
                self.scalars(*[self.bit(self.orders[l][self.step]) for l in lanes]),
                *[v for l in lanes for v in (self.kept[l], self.gots[l])],
            )
            p.other = self.swap(p.half, 0)

    def finish(self, order, at=0):
        outs = self.fill(order, at, 0)
        return self.fill(order, at, 1, outs)

    def fill(self, order, at, other, ahead=()):
        p = self.products[at]
        rows, cols = p.half.shape
        crows = min(256, rows)
        nblk = rows // crows
        turned = bool(p.pair)
        specs = [pl.BlockSpec((crows, w), lambda b, s: (s[0] * nblk + b, 0)) for w in p.widths]
        shapes = [jax.ShapeDtypeStruct((2 * rows, w), F32) for w in p.widths]
        if turned:
            w = p.widths[-1]
            specs[-1] = pl.BlockSpec((w, crows), lambda b, s: (0, s[0] * nblk + b))
            shapes[-1] = jax.ShapeDtypeStruct((w, 2 * rows), F32)
        return call(
            functools.partial(finish_body, turned=turned, count=len(specs)),
            name="finish",
            grid=(nblk,),
            scalars=1,
            in_specs=[pl.BlockSpec((crows, cols), lambda b, s: (b, 0))] + [ANY] * len(ahead),
            out_specs=specs,
            out_shape=shapes,
            aliases={2 + k: k for k in range(len(ahead))},
        )(order, self.scalars(self.bit(0) ^ other), p.other if other else p.half, *ahead)


class GainTotals:
    def __init__(self, parts, dp, tensor):
        self.size = parts[0].size
        self.value = jnp.concatenate([p.reshape(-1, 128) for p in parts], axis=0)
        self.left = [
            (name, size, [1 << k])
            for name, size in (("tensor", tensor), ("dp", dp))
            for k in range(size.bit_length() - 1)
        ]
        self.next()

    def next(self):
        name, size, masks = self.left.pop(0)
        self.got = [lax.ppermute(self.value, name, xor_pairs(size, m)) for m in masks]

    def step(self, order):
        self.value, *got = order.after(self.value, *self.got)
        self.value = self.value + got[0]
        if self.left:
            self.next()

    def split(self, order):
        while self.left:
            self.step(order)
        self.step(order)
        value = self.value.reshape(-1)
        return [value[k : k + self.size] for k in range(0, value.size, self.size)]


def qkv_body(*refs):
    chunk, rows, wq, wk, wv, cos, sin = refs[:7]
    q_out, k_out, v_out, rows_out = refs[-4:]
    x = rows[...]
    cosine, sine = cos[...], sin[...]

    def turned(pre):
        out = []
        for h in range(pre.shape[1] // HD):
            one = pre[:, h * HD : (h + 1) * HD]
            out.append(one * cosine + pltpu.roll(one, HD // 2, 1) * sine)
        return jnp.concatenate(out, axis=1)

    q_out[...] = turned(dot(x, wq[...])).astype(BF)
    k_out[...] = turned(dot(x, wk[...])).astype(BF)
    v_out[...] = dot(x, wv[...]).astype(BF)
    part = rows_out.shape[0]
    rows_out[...] = rows[:, pl.ds(pl.multiple_of(pl.program_id(0) * part, part), part)].T


def qkv_slot(order, chunk, rows, w_query, w_key, w_value, cos, sin, held, count):
    t, d = rows.shape
    width = w_query.shape[1]
    bn = min(256, width)
    wspec = pl.BlockSpec((d, bn), lambda i, s: (0, i))
    tspec = pl.BlockSpec((t, HD), lambda i, s: (s[0], 0))
    return call(
        qkv_body,
        name="qkv",
        grid=(width // bn,),
        scalars=1,
        in_specs=[pl.BlockSpec((t, d), lambda i, s: (0, 0)), wspec, wspec, wspec, tspec, tspec]
        + [ANY] * len(held),
        out_specs=[pl.BlockSpec((t, bn), lambda i, s: (s[0], i))] * 3
        + [pl.BlockSpec((d // (width // bn), t), lambda i, s: (i, s[0]))],
        out_shape=[jax.ShapeDtypeStruct((count * t, width), BF)] * 3
        + [jax.ShapeDtypeStruct((d, count * t), BF)],
        aliases={7 + i: i for i in range(len(held))},
    )(order, chunk, rows, w_query, w_key, w_value, cos, sin, *held)


def attend_consts(seq_len):
    to_log2 = math.log2(math.e)
    return (to_log2 / math.sqrt(HD), math.log2(seq_len))


def attend_body(docs, q_ref, k_ref, v_ref, ids_col, ids_row, mix, acc, *, block):
    seq_len = q_ref.shape[0]
    scale, shift = attend_consts(seq_len)
    causal = lax.broadcasted_iota(jnp.int32, (block, block), 0) >= lax.broadcasted_iota(
        jnp.int32, (block, block), 1
    )

    def term(i, j):
        q = q_ref[i * block : (i + 1) * block, :]
        k = k_ref[j * block : (j + 1) * block, :]
        sig = 1.0 / (1.0 + jnp.exp2(shift - dot_nt(q, k) * scale))
        same = ids_col[i * block : (i + 1) * block, :] == ids_row[:, j * block : (j + 1) * block]
        allowed = same & causal if i == j else same
        probs = jnp.where(allowed, sig, 0.0).astype(BF)
        return dot(probs, v_ref[j * block : (j + 1) * block, :])

    for i in range(seq_len // block):
        acc[...] = term(i, i)
        for j in range(i):

            @pl.when(docs[(j + 1) * block - 1] == docs[i * block])
            def _():
                acc[...] += term(i, j)

        mix[i * block : (i + 1) * block, :] = acc[...].astype(BF)


def attend(order, docs, q, k, v):
    seq_len, width = q.shape
    block = 256
    head = pl.BlockSpec((seq_len, HD), lambda h, s: (0, h))
    return call(
        functools.partial(attend_body, block=block),
        name="attend",
        grid=(width // HD,),
        scalars=1,
        in_specs=[
            head,
            head,
            head,
            pl.BlockSpec((seq_len, 1), lambda h, s: (0, 0)),
            pl.BlockSpec((1, seq_len), lambda h, s: (0, 0)),
        ],
        out_specs=[head],
        out_shape=[jax.ShapeDtypeStruct((seq_len, width), BF)],
        scratch=[pltpu.VMEM((block, HD), F32)],
    )(order, docs, q, k, v, docs.reshape(-1, 1), docs.reshape(1, -1))


def attend_back_body(
    docs, q_ref, k_ref, v_ref, dmix, ids_col, ids_row, cos, sin, out, dq, dk, dv, *, block
):
    seq_len = q_ref.shape[0]
    scale, shift = attend_consts(seq_len)
    causal = lax.broadcasted_iota(jnp.int32, (block, block), 0) <= lax.broadcasted_iota(
        jnp.int32, (block, block), 1
    )

    def at(i):
        return slice(i * block, (i + 1) * block)

    def term(i, j):
        q, k, v, d = q_ref[at(i), :], k_ref[at(j), :], v_ref[at(j), :], dmix[at(i), :]
        sig = 1.0 / (1.0 + jnp.exp2(shift - dot_nt(k, q) * scale))
        same = ids_col[at(j), :] == ids_row[:, at(i)]
        allowed = same & causal if i == j else same
        probs = jnp.where(allowed, sig, 0.0)
        d_scores = (dot_nt(v, d) * probs * (1.0 - probs)).astype(BF)
        return dot_tn(d_scores, k), dot(d_scores, q), dot(probs.astype(BF), d)

    for i in range(seq_len // block):
        dq[at(i), :], dk[at(i), :], dv[at(i), :] = term(i, i)
    for i in range(seq_len // block):
        for j in range(i):

            @pl.when(docs[(j + 1) * block - 1] == docs[i * block])
            def _():
                a, b, c = term(i, j)
                dq[at(i), :] += a
                dk[at(j), :] += b
                dv[at(j), :] += c

    cosine, sine = cos[...], sin[...]

    def turned_back(v):
        v = v * (1.0 / math.sqrt(HD))
        return (v * cosine - pltpu.roll(v, HD // 2, 1) * sine).astype(BF)

    width = out.shape[1] // 3
    at_head = pl.program_id(0) * HD
    for part, value in enumerate((turned_back(dq[...]), turned_back(dk[...]), dv[...].astype(BF))):
        out[:, pl.ds(pl.multiple_of(at_head + part * width, HD), HD)] = value


def attend_back(order, docs, q, k, v, d_mix, cos, sin):
    seq_len, width = q.shape
    head = pl.BlockSpec((seq_len, HD), lambda h, s: (0, h))
    whole = lambda r, c: pl.BlockSpec((r, c), lambda h, s: (0, 0))
    return call(
        functools.partial(attend_back_body, block=256),
        name="attend_back",
        grid=(width // HD,),
        scalars=1,
        in_specs=[head] * 4
        + [whole(seq_len, 1), whole(1, seq_len), whole(seq_len, HD), whole(seq_len, HD)],
        out_specs=[whole(seq_len, 3 * width)],
        out_shape=[jax.ShapeDtypeStruct((seq_len, 3 * width), BF)],
        scratch=[pltpu.VMEM((seq_len, HD), F32)] * 3,
    )(order, docs, q, k, v, d_mix, docs.reshape(-1, 1), docs.reshape(1, -1), cos, sin)


def project_body(mix, w_ref, x_ref, gain, resid, normed, acc):
    parts, _, cols = w_ref.shape
    step = pl.program_id(0)

    @pl.when(step == 0)
    def _():
        acc[...] = x_ref[...].astype(F32)

    for p in range(parts):
        acc[:, p * cols : (p + 1) * cols] += dot(mix[...], w_ref[p])

    @pl.when(step == pl.num_programs(0) - 1)
    def _():
        resid[...] = acc[...]
        normed[...] = rms_scale(acc[...], gain[...]).astype(BF)


def project(order, mix, w_out, x, gain):
    t, d = x.shape
    width = mix.shape[1]
    parts, _, cols = w_out.shape
    whole = lambda r, c: pl.BlockSpec((r, c), lambda i: (0, 0))
    return call(
        project_body,
        name="project",
        grid=(mix.shape[0] // t,),
        scalars=0,
        in_specs=[
            pl.BlockSpec((t, width), lambda i: (i, 0)),
            pl.BlockSpec((parts, width, cols), lambda i: (0, i, 0)),
            whole(t, d),
            whole(1, d),
        ],
        out_specs=[whole(t, d)] * 2,
        out_shape=[jax.ShapeDtypeStruct((t, d), F32), jax.ShapeDtypeStruct((t, d), BF)],
        scratch=[pltpu.VMEM((t, d), F32)],
    )(order, mix, w_out, x, gain.reshape(1, -1))


def norm_back(d_normed, rows, gain):
    r = lax.rsqrt(jnp.mean(rows * rows, axis=-1, keepdims=True) + EPS)
    u = rows * r
    scaled = d_normed * gain
    d_rows = r * (scaled - u * jnp.mean(scaled * u, axis=-1, keepdims=True))
    return d_rows, jnp.sum(d_normed * u, axis=0, keepdims=True)


def middle_body(d_ref, resid, cot, gain, w_ref, out, d_resid, low_t, part, low):
    parts, _, cols = w_ref.shape

    @pl.when(pl.program_id(0) == 0)
    def _():
        d_rows, part[...] = norm_back(d_ref[...].astype(F32), resid[...], gain[...])
        total = cot[...].astype(F32) + d_rows
        d_resid[...] = total
        low[...] = total.astype(BF)
        low_t[...] = low[...].T

    total = None
    for p in range(parts):
        term = dot_nt(low[:, p * cols : (p + 1) * cols], w_ref[p])
        total = term if total is None else total + term
    out[...] = total.astype(BF)


def middle(order, d_normed2, resid, cot, gain, w_out, width):
    t, d = resid.shape
    parts, rows, cols = w_out.shape
    count = rows // width
    whole = lambda r, c: pl.BlockSpec((r, c), lambda i: (0, 0))
    return call(
        middle_body,
        name="middle",
        grid=(count,),
        scalars=0,
        in_specs=[whole(t, d)] * 3
        + [whole(1, d), pl.BlockSpec((parts, width, cols), lambda i: (0, i, 0))],
        out_specs=[
            pl.BlockSpec((t, width), lambda i: (i, 0)),
            whole(t, d),
            whole(d, t),
            whole(1, d),
        ],
        out_shape=[
            jax.ShapeDtypeStruct((count * t, width), BF),
            jax.ShapeDtypeStruct((t, d), F32),
            jax.ShapeDtypeStruct((d, t), BF),
            jax.ShapeDtypeStruct((1, d), F32),
        ],
        scratch=[pltpu.VMEM((t, d), BF)],
    )(order, d_normed2, resid, cot, gain.reshape(1, -1), w_out)


def last_body(d_ref, x_ref, d_resid, gain, out, part):
    d_rows, part[...] = norm_back(d_ref[...].astype(F32), x_ref[...].astype(F32), gain[...])
    out[...] = (d_resid[...] + d_rows).astype(BF)


def last(order, d_normed, x, d_resid, gain):
    t, d = x.shape
    whole = lambda r, c: pl.BlockSpec((r, c), lambda i: (0, 0))
    return call(
        last_body,
        name="last",
        grid=(1,),
        scalars=0,
        in_specs=[whole(t, d)] * 3 + [whole(1, d)],
        out_specs=[whole(t, d), whole(1, d)],
        out_shape=[jax.ShapeDtypeStruct((t, d), BF), jax.ShapeDtypeStruct((1, d), F32)],
    )(order, d_normed, x, d_resid, gain.reshape(1, -1))


def back_project_body(d_ref, wq, wk, wv, out):
    total = None
    width = wq.shape[1]
    for k, w in enumerate((wq, wk, wv)):
        term = dot_nt(d_ref[:, k * width : (k + 1) * width], w[...])
        total = term if total is None else total + term
    out[...] = total.astype(BF)


def back_project(order, d_qkv, w_query, w_key, w_value):
    seq_len, wide = d_qkv.shape
    d, width = w_query.shape
    bn = 512
    wspec = pl.BlockSpec((bn, width), lambda i: (i, 0))
    return call(
        back_project_body,
        name="back_project",
        grid=(d // bn,),
        scalars=0,
        in_specs=[pl.BlockSpec((seq_len, wide), lambda i: (0, 0)), wspec, wspec, wspec],
        out_specs=[pl.BlockSpec((seq_len, bn), lambda i: (0, i))],
        out_shape=[jax.ShapeDtypeStruct((seq_len, d), BF)],
    )(order, d_qkv, w_query, w_key, w_value)[0]


def ffn_body(*refs):
    chunk, rows, cot, wg, wu, wd = refs[:6]
    inner, d_gate, d_up, rows_out, cot_out, d_rows, down, acc_d, acc_o = refs[-9:]
    step, last = pl.program_id(0), pl.num_programs(0) - 1
    x = rows[...]
    gate = dot(x, wg[...])
    up = dot(x, wu[...])
    sig = sigmoid(gate)
    silu = gate * sig
    inner_b = (silu * up).astype(BF)
    inner[...] = inner_b.T
    part = rows_out.shape[0]
    rows_out[...] = rows[:, pl.ds(pl.multiple_of(step * part, part), part)].T
    d_inner = dot_nt(cot[...], wd[...])
    dg = (d_inner * up * (sig * (1.0 + gate * (1.0 - sig)))).astype(BF)
    du = (d_inner * silu).astype(BF)
    d_gate[...] = dg
    d_up[...] = du
    term_o = dot(inner_b, wd[...])
    term_d = dot_nt(dg, wg[...]) + dot_nt(du, wu[...])

    @pl.when(step == 0)
    def _():
        acc_o[...] = term_o
        acc_d[...] = term_d
        cot_out[...] = cot[...]

    @pl.when(step > 0)
    def _():
        acc_o[...] += term_o
        acc_d[...] += term_d

    @pl.when(step == last)
    def _():
        d_rows[...] = acc_d[...].astype(BF)
        down[...] = acc_o[...].astype(BF)


def ffn_slot(order, chunk, rows, cot, w_gate, w_up, w_down, held, count):
    t, d = rows.shape
    hidden = w_gate.shape[1]
    bh = min(512, hidden)
    steps = hidden // bh
    wcol = pl.BlockSpec((d, bh), lambda i, s: (0, i))
    part = pl.BlockSpec((t, bh), lambda i, s: (s[0], i))
    line = pl.BlockSpec((t, d), lambda i, s: (s[0], 0))
    return call(
        ffn_body,
        name="ffn",
        grid=(hidden // bh,),
        scalars=1,
        in_specs=[
            pl.BlockSpec((t, d), lambda i, s: (0, 0)),
            pl.BlockSpec((t, d), lambda i, s: (0, 0)),
            wcol,
            wcol,
            pl.BlockSpec((bh, d), lambda i, s: (i, 0)),
        ]
        + [ANY] * len(held),
        out_specs=[pl.BlockSpec((bh, t), lambda i, s: (i, s[0])), part, part]
        + [pl.BlockSpec((d // steps, t), lambda i, s: (i, s[0])), line, line, line],
        out_shape=[jax.ShapeDtypeStruct((hidden, count * t), BF)]
        + [jax.ShapeDtypeStruct((count * t, hidden), BF)] * 2
        + [jax.ShapeDtypeStruct((d, count * t), BF)]
        + [jax.ShapeDtypeStruct((count * t, d), BF)] * 3,
        scratch=[pltpu.VMEM((t, d), F32)] * 2,
        aliases={6 + i: i for i in range(len(held))},
    )(order, chunk, rows, cot, w_gate, w_up, w_down, *held)


def local(
    layer_in,
    cotangent,
    doc_ids,
    positions,
    attn_gain,
    w_query,
    w_key,
    w_value,
    w_out,
    ffn_gain,
    w_gate,
    w_up,
    w_down,
    *,
    dp,
    tensor,
):
    t, d = layer_in.shape
    width = w_query.shape[1]
    hidden = w_gate.shape[1]
    place = lax.axis_index("tensor")
    chunks = jnp.stack([place ^ j for j in range(tensor)]).astype(jnp.int32)
    chunk = [chunks[j : j + 1] for j in range(tensor)]
    order = Order()

    share = w_out.shape[1] // dp
    w_cols = lax.all_gather(
        cols_at(w_out, lax.axis_index("dp"), share), "tensor", axis=0, tiled=True
    )
    half = HD // 2
    freqs = ROPE_BASE ** (-(jnp.arange(half).astype(F32) * 2.0) / HD)
    angles = positions.astype(F32)[:, None] * freqs[None, :]
    cosine, sine = jnp.cos(angles), jnp.sin(angles)
    cos = jnp.concatenate([cosine, cosine], axis=1)
    sin = jnp.concatenate([-sine, sine], axis=1)

    normed_own = rms_scale(layer_in.astype(F32), attn_gain).astype(BF)
    line = LineGather(normed_own, tensor, place)
    line.step()
    held = []
    for j in range(tensor):
        if 0 < j < tensor - 1:
            line.step(order)
        if j == tensor - 1:
            cots = LineGather(cotangent, tensor, place)
            cots.step(order)
        usual, order.worth = order.worth, 20 if j == tensor - 1 else order.worth
        held = qkv_slot(order, chunk[j], line.slot(j), w_query, w_key, w_value, cos, sin, held, tensor)
        order.worth = usual
        if j == min(2, tensor - 1):
            (w_cols,) = order.after(w_cols)
            w_out_all = lax.all_gather(w_cols, "dp", axis=0)
    query, key, value, normed_t = held
    (mixed,) = attend(order, doc_ids, query, key, value)
    mix = exchange(mixed)
    cots.step(order)
    (cot_first,) = order.after(cots.slot(1))
    resid, normed2_own = project(order, mix, w_out_all, layer_in, ffn_gain)

    weights = (w_gate, w_up, w_down)
    line = LineGather(normed2_own, tensor, place)
    line.step()
    held = ffn_slot(order, chunk[0], line.slot(0), cotangent, *weights, [], tensor)
    for j in range(1, tensor):
        if j < tensor - 1:
            line.step(order)
            if len(cots.ups) < tensor:
                cots.step(order)
        else:
            cots.hold(order)
            line.hold(order)
        cot = cot_first if j == 1 else cots.slot(j)
        held = ffn_slot(order, chunk[j], line.slot(j), cot, *weights, held, tensor)
    inner_t, d_gate, d_up, normed2_t, cot_all, d_normed2_part, down_part = held
    d_normed2 = lax.psum_scatter(d_normed2_part, "tensor", scatter_dimension=0, tiled=True)

    first = Gradients([(inner_t, cot_all, [d])], dp)
    wide = Gradients([(normed2_t, d_gate, [hidden]), (normed2_t, d_up, [hidden])], dp)
    more = range(first.bits - 2)

    first.give(order)
    wide.give(order, 0)
    wide.give(order, 1)
    first.keep(order)
    wide.keep(order, 0)
    wide.keep(order, 1)
    usual = order.worth
    first.fold(order)
    d_mix, d_resid, d_resid_t, ffn_gain_part = middle(
        order, d_normed2, resid, cotangent, ffn_gain, w_out_all, width
    )
    d_mix = exchange(d_mix)
    d_resid_all = lax.all_gather(d_resid_t, "tensor", axis=0)
    for _ in more:
        first.fold(order)
    wide.fold(order)
    for _ in more:
        first.spread(order)
    order.worth = 1.3
    (d_qkv,) = attend_back(order, doc_ids, query, key, value, d_mix, cos, sin)
    order.worth = usual
    attn = Gradients([(normed_t, d_qkv, [width] * 4, d_resid_all, mixed)], dp)
    attn.give(order)
    for _ in more:
        wide.fold(order)
    first.join(order)
    attn.give(order, second=True)
    d_normed = lax.psum_scatter(
        back_project(order, d_qkv, w_query, w_key, w_value),
        "tensor",
        scatter_dimension=0,
        tiled=True,
    )
    attn.keep(order)
    wide.hold(order)
    usual, order.worth = order.worth, 10
    attn.fold(order)
    order.worth = usual
    down_sum = lax.psum_scatter(
        order.after(down_part)[0], "tensor", scatter_dimension=0, tiled=True
    )
    for _ in more:
        wide.spread(order)
    for _ in more:
        attn.fold(order)
    (down_grad,) = first.finish(order)
    in_grad, attn_gain_part = last(order, d_normed, layer_in, d_resid, attn_gain)
    totals = GainTotals([attn_gain_part, ffn_gain_part], dp, tensor)
    totals.step(order)
    totals.step(order)
    totals.step(order)
    wide.hold(order)
    order.worth = 0.3
    wide.join(order)
    attn.hold(order)
    order.worth = 0.3
    for _ in more:
        attn.spread(order)
    order.worth = 0.3
    order.worth = 5
    gate_grad = wide.fill(order, 0, 0)
    up_grad = wide.fill(order, 1, 0)
    order.worth = 0.02
    (gate_grad,) = wide.fill(order, 0, 1, gate_grad)
    attn.join(order)
    (up_grad,) = wide.fill(order, 1, 1, up_grad)
    attn_grads = attn.fill(order, 0, 0)
    totals.step(order)
    (down_sum,) = order.after(down_sum)
    query_grad, key_grad, value_grad, out_grad = attn.fill(order, 0, 1, attn_grads)
    attn_gain_grad, ffn_gain_grad = totals.split(order)
    layer_out = (resid + down_sum.astype(F32)).astype(BF)
    return (
        layer_out,
        in_grad,
        attn_gain_grad,
        query_grad,
        key_grad,
        value_grad,
        out_grad,
        ffn_gain_grad,
        gate_grad,
        up_grad,
        down_grad,
    )


def solution(mesh):
    rows, cols, lines = P(("dp", "tensor"), None), P(None, "tensor"), P("tensor", None)
    return jax.shard_map(
        functools.partial(local, dp=mesh.shape["dp"], tensor=mesh.shape["tensor"]),
        mesh=mesh,
        in_specs=(
            rows, rows, P("dp"), P("dp"), P(), cols, cols, cols, lines, P(), cols, cols, lines
        ),
        out_specs=(rows, rows, P(), cols, cols, cols, lines, P(), cols, cols, lines),
        check_vma=False,
    )
```

```python
import functools
import math

import jax
import jax.numpy as jnp
from jax import lax
from jax.experimental import pallas as pl
from jax.experimental.pallas import tpu as pltpu
from jax.sharding import PartitionSpec as P

HD = 128
EPS = 1e-05
ROPE_BASE = 500000.0
BF = jnp.bfloat16
F32 = jnp.float32
VMEM = 56 << 20
COST = {
    "give": 8, "give_second": 2.5, "keep": 10, "fold": 4, "spread": 4, "join": 4.5, "finish": 5.5, "middle": 9.5, "attend": 11,
    "attend_back": 17, "back_project": 11, "qkv": 5.6, "project": 8.6, "ffn": 22, "last": 5, "tie": 0.5,
}


def dot(left, right):
    return lax.dot_general(left, right, (((1,), (0,)), ((), ())), preferred_element_type=F32)


def dot_nt(left, right):
    return lax.dot_general(left, right, (((1,), (1,)), ((), ())), preferred_element_type=F32)


def dot_tn(left, right):
    return lax.dot_general(left, right, (((0,), (0,)), ((), ())), preferred_element_type=F32)


def sigmoid(v):
    return 1.0 / (1.0 + jnp.exp(-v))


def rms_scale(values, gain):
    return values * lax.rsqrt(jnp.mean(values * values, axis=-1, keepdims=True) + EPS) * gain


ANY = pl.BlockSpec(memory_space=pl.ANY)
TOKEN = jax.ShapeDtypeStruct((8, 128), F32)


def call(body, *, name, grid, scalars, in_specs, out_specs, out_shape, scratch=(), aliases=None):
    def run(order, *operands):
        tokens = order.take()
        ahead = scalars + len(in_specs)

        def whole(*refs):
            outs = refs[ahead + len(tokens) :]
            body(*refs[:ahead], *outs[: len(out_shape)], *outs[len(out_shape) + 1 :])
            outs[len(out_shape)][...] = jnp.zeros((8, 128), F32)

        *values, token = pl.pallas_call(
            whole,
            grid_spec=pltpu.PrefetchScalarGridSpec(
                num_scalar_prefetch=scalars,
                grid=grid,
                in_specs=list(in_specs) + [ANY] * len(tokens),
                out_specs=list(out_specs) + [pl.BlockSpec((8, 128), lambda *_: (0, 0))],
                scratch_shapes=list(scratch),
            ),
            out_shape=list(out_shape) + [TOKEN],
            input_output_aliases=aliases or {},
            compiler_params=pltpu.CompilerParams(vmem_limit_bytes=VMEM),
            cost_estimate=pl.CostEstimate(flops=int(COST[name] * order.worth * 1e9), bytes_accessed=int(COST[name] * 1e6), transcendentals=0),
            name=name,
        )(*operands, *tokens)
        order.give(token)
        return values

    return run


class Order:
    def __init__(self):
        self.tokens, self.worth = [], 1.3

    def take(self):
        return self.tokens

    def give(self, token):
        self.tokens = [token]

    def after(self, *values):
        return call(
            lambda *refs: None,
            name="tie",
            grid=(1,),
            scalars=0,
            in_specs=[ANY] * len(values),
            out_specs=[ANY] * len(values),
            out_shape=[jax.ShapeDtypeStruct(v.shape, v.dtype) for v in values],
            aliases={i: i for i in range(len(values))},
            )(self, *values)


def xor_pairs(size, mask):
    return [(i, i ^ mask) for i in range(size)]


class LineGather:
    def __init__(self, own, size, place):
        self.size, self.place = size, place
        self.ups, self.downs = [own], [own]

    def step(self, order=None):
        k, size = len(self.ups), self.size
        if order is not None:
            if k == 1:
                self.ups = self.downs = order.after(self.ups[0])
                self.downs = list(self.downs)
            else:
                self.ups[-1], self.downs[-1] = order.after(self.ups[-1], self.downs[-1])
        up, down = self.ups[-1], self.downs[-1]
        self.ups.append(lax.ppermute(up, "tensor", [(i, i + 1) for i in range(k - 1, size - 1)]))
        self.downs.append(lax.ppermute(down, "tensor", [(i + 1, i) for i in range(0, size - k)]))

    def hold(self, order):
        self.ups[-1], self.downs[-1] = order.after(self.ups[-1], self.downs[-1])

    def slot(self, j):
        groups = {}
        for at in range(self.size):
            groups.setdefault((at ^ j) - at, []).append(at)
        value = None
        for off, places in groups.items():
            arr = self.downs[off] if off >= 0 else self.ups[-off]
            if value is None:
                value = arr
            else:
                here = functools.reduce(jnp.logical_or, [self.place == at for at in places])
                value = jnp.where(here, arr, value)
        return value


def exchange(values):
    return lax.all_to_all(values, "tensor", 0, 0, tiled=True)


def rows_at(values, block, rows):
    return lax.dynamic_slice_in_dim(values, block * rows, rows, axis=0)


def cols_at(values, block, cols):
    return lax.dynamic_slice_in_dim(values, block * cols, cols, axis=1)


def give_body(places, left, right, out):
    out[...] = dot(left[...], right[...]).astype(BF)


def give_second_body(places, left, right, out):
    out[...] = second((left, right), None).astype(BF)


def second(refs, rows):
    left, right = refs
    total, t = None, left.shape[2]
    for k in range(left.shape[0]):
        part = left[k] if rows is None else left[k, rows, :]
        term = dot(part, right[k * t : (k + 1) * t, :])
        total = term if total is None else total + term
    return total


def keep_body(places, *refs, two, last, lanes, chunks):
    ins = 4 if two else 2
    gots, outs = refs[ins : ins + (2 if two else 1)], refs[ins + (2 if two else 1) :]
    step = pl.program_id(0)
    rows = outs[0].shape[0]
    for lane in range(lanes):
        for rel in (1, 0):
            at = pl.multiple_of((places[1 + lane] ^ rel) * rows, rows)
            place = pl.ds(at, rows)
            out = outs[2 * lane + rel]
            inside = (step >= lane * chunks) & (step < (lane + 1) * chunks)

            @pl.when((inside & (step < last)) if two else inside)
            def _():
                total = dot(refs[0][place, :], refs[1][...])
                out[...] = (total + gots[0][place, :].astype(F32)).astype(BF)

            if two and lane == lanes - 1:

                @pl.when(step == last)
                def _():
                    total = second(refs[2:4], place)
                    out[...] = (total + gots[1][place, :].astype(F32)).astype(BF)


def fold_body(places, *refs):
    ins, outs = refs[:4], refs[4:]
    for h in (0, 1):
        total = (ins[2 * h][...].astype(F32) + ins[2 * h + 1][...].astype(F32)).astype(BF)
        if len(outs) == 2:
            outs[h][...] = total
        else:
            for rel in (0, 1):

                @pl.when(pl.program_id(0) == rel)
                def _():
                    outs[2 * h + rel][...] = total


def spread_body(places, *refs):
    ins, outs = refs[:4], refs[4:]
    for k in (0, 1):

        @pl.when(pl.program_id(0) == k)
        def _():
            for h in (0, 1):
                outs[h][...] = ins[2 * h + k][...]


def join_body(places, *refs):
    pieces, out = refs[:-1], refs[-1]
    step = pl.program_id(0) * 2 + pl.program_id(1)
    for k, piece in enumerate(pieces):

        @pl.when(step == k)
        def _():
            out[...] = piece[...]


def finish_body(place, source, *refs, turned, count):
    at, outs = 0, refs[-count:]
    for k, out in enumerate(outs):
        flip = turned and k == count - 1
        width = out.shape[0] if flip else out.shape[1]
        value = source[:, at : at + width].astype(F32)
        out[...] = value.T if flip else value
        at += width


class Product:
    def __init__(self, left, right, widths, firsts, pair=()):
        self.left, self.right, self.widths, self.firsts, self.pair = left, right, widths, firsts, pair
        self.rows = left.shape[0] // 2
        self.cols = right.shape[1] + (pair[1].shape[1] if pair else 0)
        self.bn = min(512, widths[-1])
        self.gots = []


class Gradients:
    def __init__(self, products, count):
        self.count = count
        self.bits = count.bit_length() - 1
        self.index = lax.axis_index("dp")
        self.orders = [list(range(1, self.bits)), list(range(self.bits - 1, 0, -1))]
        self.step = 0
        self.kept, self.gots = [], []
        per = 2 // len(products)
        self.products = [
            Product(*p[:3], [o[0] for o in self.orders[i * per : (i + 1) * per]], p[3:])
            for i, p in enumerate(products)
        ]

    def bit(self, b):
        return (self.index >> b) & 1

    def scalars(self, *values):
        return jnp.stack([jnp.asarray(v, jnp.int32) for v in values])

    def swap(self, value, b):
        return lax.ppermute(value, "dp", xor_pairs(self.count, 1 << b))

    def operands(self, p, core):
        tokens, last = p.right.shape[0], p.right.shape[1] // p.bn
        specs = [
            pl.BlockSpec((p.rows, tokens), lambda n, s: (s[0], 0)),
            pl.BlockSpec((tokens, p.bn), lambda n, s: (0, jnp.minimum(n, last - 1))),
        ]
        if p.pair:
            count, _, t = p.pair[0].shape
            specs += [
                pl.BlockSpec((count, p.rows, t), lambda n, s: (0, s[0], 0)),
                pl.BlockSpec((tokens, p.bn), lambda n, s: (0, 0)),
            ]
        return specs, [p.left, p.right, *p.pair], dict(two=bool(p.pair), last=last)

    def give(self, order, at=0, second=False):
        p = self.products[at]
        specs, values, facts = self.operands(p, 1 - self.bit(0))
        some = slice(2, 4) if second else slice(0, 2)
        cols = values[some][1].shape[1]
        (out,) = call(
            give_second_body if second else give_body,
            name="give_second" if second else "give",
            grid=(cols // p.bn,),
            scalars=1,
            in_specs=specs[some],
            out_specs=[pl.BlockSpec((p.rows, p.bn), lambda n, s: (0, n))],
            out_shape=[jax.ShapeDtypeStruct((p.rows, cols), BF)],
        )(order, self.scalars(1 - self.bit(0)), *values[some])
        p.gots.append(self.swap(out, 0))

    def keep(self, order, at=0):
        p = self.products[at]
        lanes = len(p.firsts)
        rows, cols = p.rows // 2, p.cols // lanes
        chunks = cols // p.bn
        specs, values, facts = self.operands(p, self.bit(0))

        def out_spec(lane):
            return pl.BlockSpec(
                (rows, p.bn), lambda n, s: (0, jnp.clip(n - lane * chunks, 0, chunks - 1))
            )

        outs = call(
            functools.partial(keep_body, lanes=lanes, chunks=chunks, **facts),
            name="keep",
            grid=(lanes * chunks,),
            scalars=1,
            in_specs=specs
            + [
                pl.BlockSpec((p.rows, p.bn), lambda n, s: (0, jnp.minimum(n, facts["last"] - 1))),
                pl.BlockSpec((p.rows, p.bn), lambda n, s: (0, 0)),
            ][: len(p.gots)],
            out_specs=[out_spec(k // 2) for k in range(2 * lanes)],
            out_shape=[jax.ShapeDtypeStruct((rows, cols), BF)] * (2 * lanes),
        )(order, self.scalars(self.bit(0), *[self.bit(b) for b in p.firsts]), *values, *p.gots)
        for h in range(lanes):
            self.kept.append(outs[2 * h])
            self.gots.append(self.swap(outs[2 * h + 1], p.firsts[h]))

    def fold(self, order):
        rows, cols = self.kept[0].shape
        self.step += 1
        more = self.step < self.bits - 1
        nexts = [self.bit(o[self.step]) for o in self.orders] if more else [0, 0]
        orows = rows // 2 if more else rows
        spec = lambda h: pl.BlockSpec((orows, cols), lambda r, s: (s[h] ^ r, 0))
        outs = call(
            fold_body,
            name="fold",
            grid=(2 if more else 1,),
            scalars=1,
            in_specs=[spec(0), spec(0), spec(1), spec(1)],
            out_specs=[pl.BlockSpec((orows, cols), lambda r, s: (0, 0))] * (4 if more else 2),
            out_shape=[jax.ShapeDtypeStruct((orows, cols), BF)] * (4 if more else 2),
        )(order, self.scalars(*nexts), self.kept[0], self.gots[0], self.kept[1], self.gots[1])
        self.kept = outs[:: 2 if more else 1]
        if more:
            self.gots = [self.swap(outs[1 + 2 * h], self.orders[h][self.step]) for h in (0, 1)]
        else:
            self.ask()

    def hold(self, order):
        self.gots = order.after(*self.gots)

    def ask(self):
        self.step -= 1
        self.gots = [self.swap(k, o[self.step]) for k, o in zip(self.kept, self.orders)]

    def spread(self, order):
        rows, cols = self.kept[0].shape
        spec = pl.BlockSpec((rows, cols), lambda k, s: (0, 0))
        self.kept = call(
            spread_body,
            name="spread",
            grid=(2,),
            scalars=1,
            in_specs=[spec] * 4,
            out_specs=[
                pl.BlockSpec((rows, cols), lambda k, s: (k ^ s[0], 0)),
                pl.BlockSpec((rows, cols), lambda k, s: (k ^ s[1], 0)),
            ],
            out_shape=[jax.ShapeDtypeStruct((2 * rows, cols), BF)] * 2,
        )(
            order,
            self.scalars(*[self.bit(o[self.step]) for o in self.orders]),
            self.kept[0],
            self.gots[0],
            self.kept[1],
            self.gots[1],
        )
        self.ask()

    def join(self, order):
        brows, bcols = self.kept[0].shape
        lane = 0
        for p in self.products:
            lanes = range(lane, lane + len(p.firsts))
            lane += len(p.firsts)
            (p.half,) = call(
                join_body,
                name="join",
                grid=(len(lanes), 2),
                scalars=1,
                in_specs=[pl.BlockSpec((brows, bcols), lambda h, k, s: (0, 0))] * (2 * len(lanes)),
                out_specs=[pl.BlockSpec((brows, bcols), lambda h, k, s: (k ^ s[h], h))],
                out_shape=[jax.ShapeDtypeStruct((p.rows, p.cols), BF)],
            )(
                order,
                self.scalars(*[self.bit(self.orders[l][self.step]) for l in lanes]),
                *[v for l in lanes for v in (self.kept[l], self.gots[l])],
            )
            p.other = self.swap(p.half, 0)

    def finish(self, order, at=0):
        outs = self.fill(order, at, 0)
        return self.fill(order, at, 1, outs)

    def fill(self, order, at, other, ahead=()):
        p = self.products[at]
        rows, cols = p.half.shape
        crows = min(256, rows)
        nblk = rows // crows
        turned = bool(p.pair)
        specs = [pl.BlockSpec((crows, w), lambda b, s: (s[0] * nblk + b, 0)) for w in p.widths]
        shapes = [jax.ShapeDtypeStruct((2 * rows, w), F32) for w in p.widths]
        if turned:
            w = p.widths[-1]
            specs[-1] = pl.BlockSpec((w, crows), lambda b, s: (0, s[0] * nblk + b))
            shapes[-1] = jax.ShapeDtypeStruct((w, 2 * rows), F32)
        return call(
            functools.partial(finish_body, turned=turned, count=len(specs)),
            name="finish",
            grid=(nblk,),
            scalars=1,
            in_specs=[pl.BlockSpec((crows, cols), lambda b, s: (b, 0))] + [ANY] * len(ahead),
            out_specs=specs,
            out_shape=shapes,
            aliases={2 + k: k for k in range(len(ahead))},
        )(order, self.scalars(self.bit(0) ^ other), p.other if other else p.half, *ahead)


class GainTotals:
    def __init__(self, parts, dp, tensor):
        self.size = parts[0].size
        self.value = jnp.concatenate([p.reshape(-1, 128) for p in parts], axis=0)
        self.left = [
            (name, size, [1 << k])
            for name, size in (("tensor", tensor), ("dp", dp))
            for k in range(size.bit_length() - 1)
        ]
        self.next()

    def next(self):
        name, size, masks = self.left.pop(0)
        self.got = [lax.ppermute(self.value, name, xor_pairs(size, m)) for m in masks]

    def step(self, order):
        self.value, *got = order.after(self.value, *self.got)
        self.value = self.value + got[0]
        if self.left:
            self.next()

    def split(self, order):
        while self.left:
            self.step(order)
        self.step(order)
        value = self.value.reshape(-1)
        return [value[k : k + self.size] for k in range(0, value.size, self.size)]


def qkv_body(*refs):
    chunk, rows, wq, wk, wv, cos, sin = refs[:7]
    q_out, k_out, v_out, rows_out = refs[-4:]
    x = rows[...]
    cosine, sine = cos[...], sin[...]

    def turned(pre):
        out = []
        for h in range(pre.shape[1] // HD):
            one = pre[:, h * HD : (h + 1) * HD]
            out.append(one * cosine + pltpu.roll(one, HD // 2, 1) * sine)
        return jnp.concatenate(out, axis=1)

    q_out[...] = turned(dot(x, wq[...])).astype(BF)
    k_out[...] = turned(dot(x, wk[...])).astype(BF)
    v_out[...] = dot(x, wv[...]).astype(BF)
    part = rows_out.shape[0]
    rows_out[...] = rows[:, pl.ds(pl.multiple_of(pl.program_id(0) * part, part), part)].T


def qkv_slot(order, chunk, rows, w_query, w_key, w_value, cos, sin, held, count):
    t, d = rows.shape
    width = w_query.shape[1]
    bn = min(256, width)
    wspec = pl.BlockSpec((d, bn), lambda i, s: (0, i))
    tspec = pl.BlockSpec((t, HD), lambda i, s: (s[0], 0))
    return call(
        qkv_body,
        name="qkv",
        grid=(width // bn,),
        scalars=1,
        in_specs=[pl.BlockSpec((t, d), lambda i, s: (0, 0)), wspec, wspec, wspec, tspec, tspec]
        + [ANY] * len(held),
        out_specs=[pl.BlockSpec((t, bn), lambda i, s: (s[0], i))] * 3
        + [pl.BlockSpec((d // (width // bn), t), lambda i, s: (i, s[0]))],
        out_shape=[jax.ShapeDtypeStruct((count * t, width), BF)] * 3
        + [jax.ShapeDtypeStruct((d, count * t), BF)],
        aliases={7 + i: i for i in range(len(held))},
    )(order, chunk, rows, w_query, w_key, w_value, cos, sin, *held)


def attend_consts(seq_len):
    to_log2 = math.log2(math.e)
    return (to_log2 / math.sqrt(HD), math.log2(seq_len))


def attend_body(docs, q_ref, k_ref, v_ref, ids_col, ids_row, mix, acc, *, block):
    seq_len = q_ref.shape[0]
    scale, shift = attend_consts(seq_len)
    causal = lax.broadcasted_iota(jnp.int32, (block, block), 0) >= lax.broadcasted_iota(
        jnp.int32, (block, block), 1
    )

    def term(i, j):
        q = q_ref[i * block : (i + 1) * block, :]
        k = k_ref[j * block : (j + 1) * block, :]
        sig = 1.0 / (1.0 + jnp.exp2(shift - dot_nt(q, k) * scale))
        same = ids_col[i * block : (i + 1) * block, :] == ids_row[:, j * block : (j + 1) * block]
        allowed = same & causal if i == j else same
        probs = jnp.where(allowed, sig, 0.0).astype(BF)
        return dot(probs, v_ref[j * block : (j + 1) * block, :])

    for i in range(seq_len // block):
        acc[...] = term(i, i)
        for j in range(i):

            @pl.when(docs[(j + 1) * block - 1] == docs[i * block])
            def _():
                acc[...] += term(i, j)

        mix[i * block : (i + 1) * block, :] = acc[...].astype(BF)


def attend(order, docs, q, k, v):
    seq_len, width = q.shape
    block = 256
    head = pl.BlockSpec((seq_len, HD), lambda h, s: (0, h))
    return call(
        functools.partial(attend_body, block=block),
        name="attend",
        grid=(width // HD,),
        scalars=1,
        in_specs=[
            head,
            head,
            head,
            pl.BlockSpec((seq_len, 1), lambda h, s: (0, 0)),
            pl.BlockSpec((1, seq_len), lambda h, s: (0, 0)),
        ],
        out_specs=[head],
        out_shape=[jax.ShapeDtypeStruct((seq_len, width), BF)],
        scratch=[pltpu.VMEM((block, HD), F32)],
    )(order, docs, q, k, v, docs.reshape(-1, 1), docs.reshape(1, -1))


def attend_back_body(
    docs, q_ref, k_ref, v_ref, dmix, ids_col, ids_row, cos, sin, out, dq, dk, dv, *, block
):
    seq_len = q_ref.shape[0]
    scale, shift = attend_consts(seq_len)
    causal = lax.broadcasted_iota(jnp.int32, (block, block), 0) <= lax.broadcasted_iota(
        jnp.int32, (block, block), 1
    )

    def at(i):
        return slice(i * block, (i + 1) * block)

    def term(i, j):
        q, k, v, d = q_ref[at(i), :], k_ref[at(j), :], v_ref[at(j), :], dmix[at(i), :]
        sig = 1.0 / (1.0 + jnp.exp2(shift - dot_nt(k, q) * scale))
        same = ids_col[at(j), :] == ids_row[:, at(i)]
        allowed = same & causal if i == j else same
        probs = jnp.where(allowed, sig, 0.0)
        d_scores = (dot_nt(v, d) * probs * (1.0 - probs)).astype(BF)
        return dot_tn(d_scores, k), dot(d_scores, q), dot(probs.astype(BF), d)

    for i in range(seq_len // block):
        dq[at(i), :], dk[at(i), :], dv[at(i), :] = term(i, i)
    for i in range(seq_len // block):
        for j in range(i):

            @pl.when(docs[(j + 1) * block - 1] == docs[i * block])
            def _():
                a, b, c = term(i, j)
                dq[at(i), :] += a
                dk[at(j), :] += b
                dv[at(j), :] += c

    cosine, sine = cos[...], sin[...]

    def turned_back(v):
        v = v * (1.0 / math.sqrt(HD))
        return (v * cosine - pltpu.roll(v, HD // 2, 1) * sine).astype(BF)

    width = out.shape[1] // 3
    at_head = pl.program_id(0) * HD
    for part, value in enumerate((turned_back(dq[...]), turned_back(dk[...]), dv[...].astype(BF))):
        out[:, pl.ds(pl.multiple_of(at_head + part * width, HD), HD)] = value


def attend_back(order, docs, q, k, v, d_mix, cos, sin):
    seq_len, width = q.shape
    head = pl.BlockSpec((seq_len, HD), lambda h, s: (0, h))
    whole = lambda r, c: pl.BlockSpec((r, c), lambda h, s: (0, 0))
    return call(
        functools.partial(attend_back_body, block=256),
        name="attend_back",
        grid=(width // HD,),
        scalars=1,
        in_specs=[head] * 4
        + [whole(seq_len, 1), whole(1, seq_len), whole(seq_len, HD), whole(seq_len, HD)],
        out_specs=[whole(seq_len, 3 * width)],
        out_shape=[jax.ShapeDtypeStruct((seq_len, 3 * width), BF)],
        scratch=[pltpu.VMEM((seq_len, HD), F32)] * 3,
    )(order, docs, q, k, v, d_mix, docs.reshape(-1, 1), docs.reshape(1, -1), cos, sin)


def project_body(mix, w_ref, x_ref, gain, resid, normed, acc):
    parts, _, cols = w_ref.shape
    step = pl.program_id(0)

    @pl.when(step == 0)
    def _():
        acc[...] = x_ref[...].astype(F32)

    for p in range(parts):
        acc[:, p * cols : (p + 1) * cols] += dot(mix[...], w_ref[p])

    @pl.when(step == pl.num_programs(0) - 1)
    def _():
        resid[...] = acc[...]
        normed[...] = rms_scale(acc[...], gain[...]).astype(BF)


def project(order, mix, w_out, x, gain):
    t, d = x.shape
    width = mix.shape[1]
    parts, _, cols = w_out.shape
    whole = lambda r, c: pl.BlockSpec((r, c), lambda i: (0, 0))
    return call(
        project_body,
        name="project",
        grid=(mix.shape[0] // t,),
        scalars=0,
        in_specs=[
            pl.BlockSpec((t, width), lambda i: (i, 0)),
            pl.BlockSpec((parts, width, cols), lambda i: (0, i, 0)),
            whole(t, d),
            whole(1, d),
        ],
        out_specs=[whole(t, d)] * 2,
        out_shape=[jax.ShapeDtypeStruct((t, d), F32), jax.ShapeDtypeStruct((t, d), BF)],
        scratch=[pltpu.VMEM((t, d), F32)],
    )(order, mix, w_out, x, gain.reshape(1, -1))


def norm_back(d_normed, rows, gain):
    r = lax.rsqrt(jnp.mean(rows * rows, axis=-1, keepdims=True) + EPS)
    u = rows * r
    scaled = d_normed * gain
    d_rows = r * (scaled - u * jnp.mean(scaled * u, axis=-1, keepdims=True))
    return d_rows, jnp.sum(d_normed * u, axis=0, keepdims=True)


def middle_body(d_ref, resid, cot, gain, w_ref, out, d_resid, low_t, part, low):
    parts, _, cols = w_ref.shape

    @pl.when(pl.program_id(0) == 0)
    def _():
        d_rows, part[...] = norm_back(d_ref[...].astype(F32), resid[...], gain[...])
        total = cot[...].astype(F32) + d_rows
        d_resid[...] = total
        low[...] = total.astype(BF)
        low_t[...] = low[...].T

    total = None
    for p in range(parts):
        term = dot_nt(low[:, p * cols : (p + 1) * cols], w_ref[p])
        total = term if total is None else total + term
    out[...] = total.astype(BF)


def middle(order, d_normed2, resid, cot, gain, w_out, width):
    t, d = resid.shape
    parts, rows, cols = w_out.shape
    count = rows // width
    whole = lambda r, c: pl.BlockSpec((r, c), lambda i: (0, 0))
    return call(
        middle_body,
        name="middle",
        grid=(count,),
        scalars=0,
        in_specs=[whole(t, d)] * 3
        + [whole(1, d), pl.BlockSpec((parts, width, cols), lambda i: (0, i, 0))],
        out_specs=[
            pl.BlockSpec((t, width), lambda i: (i, 0)),
            whole(t, d),
            whole(d, t),
            whole(1, d),
        ],
        out_shape=[
            jax.ShapeDtypeStruct((count * t, width), BF),
            jax.ShapeDtypeStruct((t, d), F32),
            jax.ShapeDtypeStruct((d, t), BF),
            jax.ShapeDtypeStruct((1, d), F32),
        ],
        scratch=[pltpu.VMEM((t, d), BF)],
    )(order, d_normed2, resid, cot, gain.reshape(1, -1), w_out)


def last_body(d_ref, x_ref, d_resid, gain, out, part):
    d_rows, part[...] = norm_back(d_ref[...].astype(F32), x_ref[...].astype(F32), gain[...])
    out[...] = (d_resid[...] + d_rows).astype(BF)


def last(order, d_normed, x, d_resid, gain):
    t, d = x.shape
    whole = lambda r, c: pl.BlockSpec((r, c), lambda i: (0, 0))
    return call(
        last_body,
        name="last",
        grid=(1,),
        scalars=0,
        in_specs=[whole(t, d)] * 3 + [whole(1, d)],
        out_specs=[whole(t, d), whole(1, d)],
        out_shape=[jax.ShapeDtypeStruct((t, d), BF), jax.ShapeDtypeStruct((1, d), F32)],
    )(order, d_normed, x, d_resid, gain.reshape(1, -1))


def back_project_body(d_ref, wq, wk, wv, out):
    total = None
    width = wq.shape[1]
    for k, w in enumerate((wq, wk, wv)):
        term = dot_nt(d_ref[:, k * width : (k + 1) * width], w[...])
        total = term if total is None else total + term
    out[...] = total.astype(BF)


def back_project(order, d_qkv, w_query, w_key, w_value):
    seq_len, wide = d_qkv.shape
    d, width = w_query.shape
    bn = 512
    wspec = pl.BlockSpec((bn, width), lambda i: (i, 0))
    return call(
        back_project_body,
        name="back_project",
        grid=(d // bn,),
        scalars=0,
        in_specs=[pl.BlockSpec((seq_len, wide), lambda i: (0, 0)), wspec, wspec, wspec],
        out_specs=[pl.BlockSpec((seq_len, bn), lambda i: (0, i))],
        out_shape=[jax.ShapeDtypeStruct((seq_len, d), BF)],
    )(order, d_qkv, w_query, w_key, w_value)[0]


def ffn_body(*refs):
    chunk, rows, cot, wg, wu, wd = refs[:6]
    inner, d_gate, d_up, rows_out, cot_out, d_rows, down, acc_d, acc_o = refs[-9:]
    step, last = pl.program_id(0), pl.num_programs(0) - 1
    x = rows[...]
    gate = dot(x, wg[...])
    up = dot(x, wu[...])
    sig = sigmoid(gate)
    silu = gate * sig
    inner_b = (silu * up).astype(BF)
    inner[...] = inner_b.T
    part = rows_out.shape[0]
    rows_out[...] = rows[:, pl.ds(pl.multiple_of(step * part, part), part)].T
    d_inner = dot_nt(cot[...], wd[...])
    dg = (d_inner * up * (sig * (1.0 + gate * (1.0 - sig)))).astype(BF)
    du = (d_inner * silu).astype(BF)
    d_gate[...] = dg
    d_up[...] = du
    term_o = dot(inner_b, wd[...])
    term_d = dot_nt(dg, wg[...]) + dot_nt(du, wu[...])

    @pl.when(step == 0)
    def _():
        acc_o[...] = term_o
        acc_d[...] = term_d
        cot_out[...] = cot[...]

    @pl.when(step > 0)
    def _():
        acc_o[...] += term_o
        acc_d[...] += term_d

    @pl.when(step == last)
    def _():
        d_rows[...] = acc_d[...].astype(BF)
        down[...] = acc_o[...].astype(BF)


def ffn_slot(order, chunk, rows, cot, w_gate, w_up, w_down, held, count):
    t, d = rows.shape
    hidden = w_gate.shape[1]
    bh = min(512, hidden)
    steps = hidden // bh
    wcol = pl.BlockSpec((d, bh), lambda i, s: (0, i))
    part = pl.BlockSpec((t, bh), lambda i, s: (s[0], i))
    line = pl.BlockSpec((t, d), lambda i, s: (s[0], 0))
    return call(
        ffn_body,
        name="ffn",
        grid=(hidden // bh,),
        scalars=1,
        in_specs=[
            pl.BlockSpec((t, d), lambda i, s: (0, 0)),
            pl.BlockSpec((t, d), lambda i, s: (0, 0)),
            wcol,
            wcol,
            pl.BlockSpec((bh, d), lambda i, s: (i, 0)),
        ]
        + [ANY] * len(held),
        out_specs=[pl.BlockSpec((bh, t), lambda i, s: (i, s[0])), part, part]
        + [pl.BlockSpec((d // steps, t), lambda i, s: (i, s[0])), line, line, line],
        out_shape=[jax.ShapeDtypeStruct((hidden, count * t), BF)]
        + [jax.ShapeDtypeStruct((count * t, hidden), BF)] * 2
        + [jax.ShapeDtypeStruct((d, count * t), BF)]
        + [jax.ShapeDtypeStruct((count * t, d), BF)] * 3,
        scratch=[pltpu.VMEM((t, d), F32)] * 2,
        aliases={6 + i: i for i in range(len(held))},
    )(order, chunk, rows, cot, w_gate, w_up, w_down, *held)


def local(
    layer_in,
    cotangent,
    doc_ids,
    positions,
    attn_gain,
    w_query,
    w_key,
    w_value,
    w_out,
    ffn_gain,
    w_gate,
    w_up,
    w_down,
    *,
    dp,
    tensor,
):
    t, d = layer_in.shape
    width = w_query.shape[1]
    hidden = w_gate.shape[1]
    place = lax.axis_index("tensor")
    chunks = jnp.stack([place ^ j for j in range(tensor)]).astype(jnp.int32)
    chunk = [chunks[j : j + 1] for j in range(tensor)]
    order = Order()

    share = w_out.shape[1] // dp
    w_cols = lax.all_gather(
        cols_at(w_out, lax.axis_index("dp"), share), "tensor", axis=0, tiled=True
    )
    half = HD // 2
    freqs = ROPE_BASE ** (-(jnp.arange(half).astype(F32) * 2.0) / HD)
    angles = positions.astype(F32)[:, None] * freqs[None, :]
    cosine, sine = jnp.cos(angles), jnp.sin(angles)
    cos = jnp.concatenate([cosine, cosine], axis=1)
    sin = jnp.concatenate([-sine, sine], axis=1)

    normed_own = rms_scale(layer_in.astype(F32), attn_gain).astype(BF)
    line = LineGather(normed_own, tensor, place)
    line.step()
    held = []
    for j in range(tensor):
        if 0 < j < tensor - 1:
            line.step(order)
        if j == tensor - 1:
            cots = LineGather(cotangent, tensor, place)
            cots.step(order)
        usual, order.worth = order.worth, 20 if j == tensor - 1 else order.worth
        held = qkv_slot(order, chunk[j], line.slot(j), w_query, w_key, w_value, cos, sin, held, tensor)
        order.worth = usual
        if j == min(2, tensor - 1):
            (w_cols,) = order.after(w_cols)
            w_out_all = lax.all_gather(w_cols, "dp", axis=0)
    query, key, value, normed_t = held
    (mixed,) = attend(order, doc_ids, query, key, value)
    mix = exchange(mixed)
    cots.step(order)
    (cot_first,) = order.after(cots.slot(1))
    resid, normed2_own = project(order, mix, w_out_all, layer_in, ffn_gain)

    weights = (w_gate, w_up, w_down)
    line = LineGather(normed2_own, tensor, place)
    line.step()
    held = ffn_slot(order, chunk[0], line.slot(0), cotangent, *weights, [], tensor)
    for j in range(1, tensor):
        if j < tensor - 1:
            line.step(order)
            if len(cots.ups) < tensor:
                cots.step(order)
        else:
            cots.hold(order)
            line.hold(order)
        cot = cot_first if j == 1 else cots.slot(j)
        held = ffn_slot(order, chunk[j], line.slot(j), cot, *weights, held, tensor)
    inner_t, d_gate, d_up, normed2_t, cot_all, d_normed2_part, down_part = held
    d_normed2 = lax.psum_scatter(d_normed2_part, "tensor", scatter_dimension=0, tiled=True)

    first = Gradients([(inner_t, cot_all, [d])], dp)
    wide = Gradients([(normed2_t, d_gate, [hidden]), (normed2_t, d_up, [hidden])], dp)
    more = range(first.bits - 2)

    first.give(order)
    wide.give(order, 0)
    wide.give(order, 1)
    first.keep(order)
    wide.keep(order, 0)
    wide.keep(order, 1)
    usual = order.worth
    first.fold(order)
    d_mix, d_resid, d_resid_t, ffn_gain_part = middle(
        order, d_normed2, resid, cotangent, ffn_gain, w_out_all, width
    )
    d_mix = exchange(d_mix)
    d_resid_all = lax.all_gather(d_resid_t, "tensor", axis=0)
    wide.fold(order)
    for _ in more:
        first.fold(order)
    (d_qkv,) = attend_back(order, doc_ids, query, key, value, d_mix, cos, sin)
    attn = Gradients([(normed_t, d_qkv, [width] * 4, d_resid_all, mixed)], dp)
    for _ in more:
        first.spread(order)
    attn.give(order)
    for _ in more:
        wide.fold(order)
    first.join(order)
    attn.give(order, second=True)
    d_normed = lax.psum_scatter(
        back_project(order, d_qkv, w_query, w_key, w_value),
        "tensor",
        scatter_dimension=0,
        tiled=True,
    )
    attn.keep(order)
    wide.hold(order)
    usual, order.worth = order.worth, 10
    attn.fold(order)
    order.worth = usual
    down_sum = lax.psum_scatter(
        order.after(down_part)[0], "tensor", scatter_dimension=0, tiled=True
    )
    for _ in more:
        wide.spread(order)
    for _ in more:
        attn.fold(order)
    (down_grad,) = first.finish(order)
    in_grad, attn_gain_part = last(order, d_normed, layer_in, d_resid, attn_gain)
    totals = GainTotals([attn_gain_part, ffn_gain_part], dp, tensor)
    totals.step(order)
    totals.step(order)
    totals.step(order)
    wide.hold(order)
    order.worth = 0.3
    wide.join(order)
    attn.hold(order)
    order.worth = 0.3
    for _ in more:
        attn.spread(order)
    order.worth = 0.3
    order.worth = 5
    gate_grad = wide.fill(order, 0, 0)
    up_grad = wide.fill(order, 1, 0)
    order.worth = 0.02
    (gate_grad,) = wide.fill(order, 0, 1, gate_grad)
    attn.join(order)
    (up_grad,) = wide.fill(order, 1, 1, up_grad)
    attn_grads = attn.fill(order, 0, 0)
    totals.step(order)
    (down_sum,) = order.after(down_sum)
    query_grad, key_grad, value_grad, out_grad = attn.fill(order, 0, 1, attn_grads)
    attn_gain_grad, ffn_gain_grad = totals.split(order)
    layer_out = (resid + down_sum.astype(F32)).astype(BF)
    return (
        layer_out,
        in_grad,
        attn_gain_grad,
        query_grad,
        key_grad,
        value_grad,
        out_grad,
        ffn_gain_grad,
        gate_grad,
        up_grad,
        down_grad,
    )


def solution(mesh):
    rows, cols, lines = P(("dp", "tensor"), None), P(None, "tensor"), P("tensor", None)
    return jax.shard_map(
        functools.partial(local, dp=mesh.shape["dp"], tensor=mesh.shape["tensor"]),
        mesh=mesh,
        in_specs=(
            rows, rows, P("dp"), P("dp"), P(), cols, cols, cols, lines, P(), cols, cols, lines
        ),
        out_specs=(rows, rows, P(), cols, cols, cols, lines, P(), cols, cols, lines),
        check_vma=False,
    )
```

```python
import functools
import math

import jax
import jax.numpy as jnp
from jax import lax
from jax.experimental import pallas as pl
from jax.experimental.pallas import tpu as pltpu
from jax.sharding import PartitionSpec as P

HD = 128
EPS = 1e-05
ROPE_BASE = 500000.0
BF = jnp.bfloat16
F32 = jnp.float32
VMEM = 56 << 20
COST = {
    "give": 8, "give_second": 2.5, "keep": 10, "fold": 4, "spread": 4, "join": 4.5, "finish": 5.5, "middle": 9.5, "attend": 11,
    "attend_back": 17, "back_project": 11, "qkv": 5.6, "project": 8.6, "ffn": 22, "last": 5, "tie": 0.5,
}


def dot(left, right):
    return lax.dot_general(left, right, (((1,), (0,)), ((), ())), preferred_element_type=F32)


def dot_nt(left, right):
    return lax.dot_general(left, right, (((1,), (1,)), ((), ())), preferred_element_type=F32)


def dot_tn(left, right):
    return lax.dot_general(left, right, (((0,), (0,)), ((), ())), preferred_element_type=F32)


def sigmoid(v):
    return 1.0 / (1.0 + jnp.exp(-v))


def rms_scale(values, gain):
    return values * lax.rsqrt(jnp.mean(values * values, axis=-1, keepdims=True) + EPS) * gain


ANY = pl.BlockSpec(memory_space=pl.ANY)
TOKEN = jax.ShapeDtypeStruct((8, 128), F32)


def call(body, *, name, grid, scalars, in_specs, out_specs, out_shape, scratch=(), aliases=None):
    def run(order, *operands):
        tokens = order.take()
        ahead = scalars + len(in_specs)

        def whole(*refs):
            outs = refs[ahead + len(tokens) :]
            body(*refs[:ahead], *outs[: len(out_shape)], *outs[len(out_shape) + 1 :])
            outs[len(out_shape)][...] = jnp.zeros((8, 128), F32)

        *values, token = pl.pallas_call(
            whole,
            grid_spec=pltpu.PrefetchScalarGridSpec(
                num_scalar_prefetch=scalars,
                grid=grid,
                in_specs=list(in_specs) + [ANY] * len(tokens),
                out_specs=list(out_specs) + [pl.BlockSpec((8, 128), lambda *_: (0, 0))],
                scratch_shapes=list(scratch),
            ),
            out_shape=list(out_shape) + [TOKEN],
            input_output_aliases=aliases or {},
            compiler_params=pltpu.CompilerParams(vmem_limit_bytes=VMEM),
            cost_estimate=pl.CostEstimate(flops=int(COST[name] * order.worth * 1e9), bytes_accessed=int(COST[name] * 1e6), transcendentals=0),
            name=name,
        )(*operands, *tokens)
        order.give(token)
        return values

    return run


class Order:
    def __init__(self):
        self.tokens, self.worth = [], 1.3

    def take(self):
        return self.tokens

    def give(self, token):
        self.tokens = [token]

    def after(self, *values):
        return call(
            lambda *refs: None,
            name="tie",
            grid=(1,),
            scalars=0,
            in_specs=[ANY] * len(values),
            out_specs=[ANY] * len(values),
            out_shape=[jax.ShapeDtypeStruct(v.shape, v.dtype) for v in values],
            aliases={i: i for i in range(len(values))},
            )(self, *values)


def xor_pairs(size, mask):
    return [(i, i ^ mask) for i in range(size)]


class LineGather:
    def __init__(self, own, size, place):
        self.size, self.place = size, place
        self.ups, self.downs = [own], [own]

    def step(self, order=None):
        k, size = len(self.ups), self.size
        if order is not None:
            if k == 1:
                self.ups = self.downs = order.after(self.ups[0])
                self.downs = list(self.downs)
            else:
                self.ups[-1], self.downs[-1] = order.after(self.ups[-1], self.downs[-1])
        up, down = self.ups[-1], self.downs[-1]
        self.ups.append(lax.ppermute(up, "tensor", [(i, i + 1) for i in range(k - 1, size - 1)]))
        self.downs.append(lax.ppermute(down, "tensor", [(i + 1, i) for i in range(0, size - k)]))

    def hold(self, order):
        self.ups[-1], self.downs[-1] = order.after(self.ups[-1], self.downs[-1])

    def slot(self, j):
        groups = {}
        for at in range(self.size):
            groups.setdefault((at ^ j) - at, []).append(at)
        value = None
        for off, places in groups.items():
            arr = self.downs[off] if off >= 0 else self.ups[-off]
            if value is None:
                value = arr
            else:
                here = functools.reduce(jnp.logical_or, [self.place == at for at in places])
                value = jnp.where(here, arr, value)
        return value


def exchange(values):
    return lax.all_to_all(values, "tensor", 0, 0, tiled=True)


def rows_at(values, block, rows):
    return lax.dynamic_slice_in_dim(values, block * rows, rows, axis=0)


def cols_at(values, block, cols):
    return lax.dynamic_slice_in_dim(values, block * cols, cols, axis=1)


def give_body(places, left, right, out):
    out[...] = dot(left[...], right[...]).astype(BF)


def give_second_body(places, left, right, out):
    out[...] = second((left, right), None).astype(BF)


def second(refs, rows):
    left, right = refs
    total, t = None, left.shape[2]
    for k in range(left.shape[0]):
        part = left[k] if rows is None else left[k, rows, :]
        term = dot(part, right[k * t : (k + 1) * t, :])
        total = term if total is None else total + term
    return total


def keep_body(places, *refs, two, last, lanes, chunks):
    ins = 4 if two else 2
    gots, outs = refs[ins : ins + (2 if two else 1)], refs[ins + (2 if two else 1) :]
    step = pl.program_id(0)
    rows = outs[0].shape[0]
    for lane in range(lanes):
        for rel in (1, 0):
            at = pl.multiple_of((places[1 + lane] ^ rel) * rows, rows)
            place = pl.ds(at, rows)
            out = outs[2 * lane + rel]
            inside = (step >= lane * chunks) & (step < (lane + 1) * chunks)

            @pl.when((inside & (step < last)) if two else inside)
            def _():
                total = dot(refs[0][place, :], refs[1][...])
                out[...] = (total + gots[0][place, :].astype(F32)).astype(BF)

            if two and lane == lanes - 1:

                @pl.when(step == last)
                def _():
                    total = second(refs[2:4], place)
                    out[...] = (total + gots[1][place, :].astype(F32)).astype(BF)


def fold_body(places, *refs):
    ins, outs = refs[:4], refs[4:]
    for h in (0, 1):
        total = (ins[2 * h][...].astype(F32) + ins[2 * h + 1][...].astype(F32)).astype(BF)
        if len(outs) == 2:
            outs[h][...] = total
        else:
            for rel in (0, 1):

                @pl.when(pl.program_id(0) == rel)
                def _():
                    outs[2 * h + rel][...] = total


def spread_body(places, *refs):
    ins, outs = refs[:4], refs[4:]
    for k in (0, 1):

        @pl.when(pl.program_id(0) == k)
        def _():
            for h in (0, 1):
                outs[h][...] = ins[2 * h + k][...]


def join_body(places, *refs):
    pieces, out = refs[:-1], refs[-1]
    step = pl.program_id(0) * 2 + pl.program_id(1)
    for k, piece in enumerate(pieces):

        @pl.when(step == k)
        def _():
            out[...] = piece[...]


def finish_body(place, source, *refs, turned, count):
    at, outs = 0, refs[-count:]
    for k, out in enumerate(outs):
        flip = turned and k == count - 1
        width = out.shape[0] if flip else out.shape[1]
        value = source[:, at : at + width].astype(F32)
        out[...] = value.T if flip else value
        at += width


class Product:
    def __init__(self, left, right, widths, firsts, pair=()):
        self.left, self.right, self.widths, self.firsts, self.pair = left, right, widths, firsts, pair
        self.rows = left.shape[0] // 2
        self.cols = right.shape[1] + (pair[1].shape[1] if pair else 0)
        self.bn = min(512, widths[-1])
        self.gots = []


class Gradients:
    def __init__(self, products, count):
        self.count = count
        self.bits = count.bit_length() - 1
        self.index = lax.axis_index("dp")
        self.orders = [list(range(1, self.bits)), list(range(self.bits - 1, 0, -1))]
        self.step = 0
        self.kept, self.gots = [], []
        per = 2 // len(products)
        self.products = [
            Product(*p[:3], [o[0] for o in self.orders[i * per : (i + 1) * per]], p[3:])
            for i, p in enumerate(products)
        ]

    def bit(self, b):
        return (self.index >> b) & 1

    def scalars(self, *values):
        return jnp.stack([jnp.asarray(v, jnp.int32) for v in values])

    def swap(self, value, b):
        return lax.ppermute(value, "dp", xor_pairs(self.count, 1 << b))

    def operands(self, p, core):
        tokens, last = p.right.shape[0], p.right.shape[1] // p.bn
        specs = [
            pl.BlockSpec((p.rows, tokens), lambda n, s: (s[0], 0)),
            pl.BlockSpec((tokens, p.bn), lambda n, s: (0, jnp.minimum(n, last - 1))),
        ]
        if p.pair:
            count, _, t = p.pair[0].shape
            specs += [
                pl.BlockSpec((count, p.rows, t), lambda n, s: (0, s[0], 0)),
                pl.BlockSpec((tokens, p.bn), lambda n, s: (0, 0)),
            ]
        return specs, [p.left, p.right, *p.pair], dict(two=bool(p.pair), last=last)

    def give(self, order, at=0, second=False):
        p = self.products[at]
        specs, values, facts = self.operands(p, 1 - self.bit(0))
        some = slice(2, 4) if second else slice(0, 2)
        cols = values[some][1].shape[1]
        (out,) = call(
            give_second_body if second else give_body,
            name="give_second" if second else "give",
            grid=(cols // p.bn,),
            scalars=1,
            in_specs=specs[some],
            out_specs=[pl.BlockSpec((p.rows, p.bn), lambda n, s: (0, n))],
            out_shape=[jax.ShapeDtypeStruct((p.rows, cols), BF)],
        )(order, self.scalars(1 - self.bit(0)), *values[some])
        p.gots.append(self.swap(out, 0))

    def keep(self, order, at=0):
        p = self.products[at]
        lanes = len(p.firsts)
        rows, cols = p.rows // 2, p.cols // lanes
        chunks = cols // p.bn
        specs, values, facts = self.operands(p, self.bit(0))

        def out_spec(lane):
            return pl.BlockSpec(
                (rows, p.bn), lambda n, s: (0, jnp.clip(n - lane * chunks, 0, chunks - 1))
            )

        outs = call(
            functools.partial(keep_body, lanes=lanes, chunks=chunks, **facts),
            name="keep",
            grid=(lanes * chunks,),
            scalars=1,
            in_specs=specs
            + [
                pl.BlockSpec((p.rows, p.bn), lambda n, s: (0, jnp.minimum(n, facts["last"] - 1))),
                pl.BlockSpec((p.rows, p.bn), lambda n, s: (0, 0)),
            ][: len(p.gots)],
            out_specs=[out_spec(k // 2) for k in range(2 * lanes)],
            out_shape=[jax.ShapeDtypeStruct((rows, cols), BF)] * (2 * lanes),
        )(order, self.scalars(self.bit(0), *[self.bit(b) for b in p.firsts]), *values, *p.gots)
        for h in range(lanes):
            self.kept.append(outs[2 * h])
            self.gots.append(self.swap(outs[2 * h + 1], p.firsts[h]))

    def fold(self, order):
        rows, cols = self.kept[0].shape
        self.step += 1
        more = self.step < self.bits - 1
        nexts = [self.bit(o[self.step]) for o in self.orders] if more else [0, 0]
        orows = rows // 2 if more else rows
        spec = lambda h: pl.BlockSpec((orows, cols), lambda r, s: (s[h] ^ r, 0))
        outs = call(
            fold_body,
            name="fold",
            grid=(2 if more else 1,),
            scalars=1,
            in_specs=[spec(0), spec(0), spec(1), spec(1)],
            out_specs=[pl.BlockSpec((orows, cols), lambda r, s: (0, 0))] * (4 if more else 2),
            out_shape=[jax.ShapeDtypeStruct((orows, cols), BF)] * (4 if more else 2),
        )(order, self.scalars(*nexts), self.kept[0], self.gots[0], self.kept[1], self.gots[1])
        self.kept = outs[:: 2 if more else 1]
        if more:
            self.gots = [self.swap(outs[1 + 2 * h], self.orders[h][self.step]) for h in (0, 1)]
        else:
            self.ask()

    def hold(self, order):
        self.gots = order.after(*self.gots)

    def ask(self):
        self.step -= 1
        self.gots = [self.swap(k, o[self.step]) for k, o in zip(self.kept, self.orders)]

    def spread(self, order):
        rows, cols = self.kept[0].shape
        spec = pl.BlockSpec((rows, cols), lambda k, s: (0, 0))
        self.kept = call(
            spread_body,
            name="spread",
            grid=(2,),
            scalars=1,
            in_specs=[spec] * 4,
            out_specs=[
                pl.BlockSpec((rows, cols), lambda k, s: (k ^ s[0], 0)),
                pl.BlockSpec((rows, cols), lambda k, s: (k ^ s[1], 0)),
            ],
            out_shape=[jax.ShapeDtypeStruct((2 * rows, cols), BF)] * 2,
        )(
            order,
            self.scalars(*[self.bit(o[self.step]) for o in self.orders]),
            self.kept[0],
            self.gots[0],
            self.kept[1],
            self.gots[1],
        )
        self.ask()

    def join(self, order):
        brows, bcols = self.kept[0].shape
        lane = 0
        for p in self.products:
            lanes = range(lane, lane + len(p.firsts))
            lane += len(p.firsts)
            (p.half,) = call(
                join_body,
                name="join",
                grid=(len(lanes), 2),
                scalars=1,
                in_specs=[pl.BlockSpec((brows, bcols), lambda h, k, s: (0, 0))] * (2 * len(lanes)),
                out_specs=[pl.BlockSpec((brows, bcols), lambda h, k, s: (k ^ s[h], h))],
                out_shape=[jax.ShapeDtypeStruct((p.rows, p.cols), BF)],
            )(
                order,
                self.scalars(*[self.bit(self.orders[l][self.step]) for l in lanes]),
                *[v for l in lanes for v in (self.kept[l], self.gots[l])],
            )
            p.other = self.swap(p.half, 0)

    def finish(self, order, at=0):
        outs = self.fill(order, at, 0)
        return self.fill(order, at, 1, outs)

    def fill(self, order, at, other, ahead=()):
        p = self.products[at]
        rows, cols = p.half.shape
        crows = min(256, rows)
        nblk = rows // crows
        turned = bool(p.pair)
        specs = [pl.BlockSpec((crows, w), lambda b, s: (s[0] * nblk + b, 0)) for w in p.widths]
        shapes = [jax.ShapeDtypeStruct((2 * rows, w), F32) for w in p.widths]
        if turned:
            w = p.widths[-1]
            specs[-1] = pl.BlockSpec((w, crows), lambda b, s: (0, s[0] * nblk + b))
            shapes[-1] = jax.ShapeDtypeStruct((w, 2 * rows), F32)
        return call(
            functools.partial(finish_body, turned=turned, count=len(specs)),
            name="finish",
            grid=(nblk,),
            scalars=1,
            in_specs=[pl.BlockSpec((crows, cols), lambda b, s: (b, 0))] + [ANY] * len(ahead),
            out_specs=specs,
            out_shape=shapes,
            aliases={2 + k: k for k in range(len(ahead))},
        )(order, self.scalars(self.bit(0) ^ other), p.other if other else p.half, *ahead)


class GainTotals:
    def __init__(self, parts, dp, tensor):
        self.size = parts[0].size
        self.value = jnp.concatenate([p.reshape(-1, 128) for p in parts], axis=0)
        self.left = [
            (name, size, [1 << k])
            for name, size in (("tensor", tensor), ("dp", dp))
            for k in range(size.bit_length() - 1)
        ]
        self.next()

    def next(self):
        name, size, masks = self.left.pop(0)
        self.got = [lax.ppermute(self.value, name, xor_pairs(size, m)) for m in masks]

    def step(self, order):
        self.value, *got = order.after(self.value, *self.got)
        self.value = self.value + got[0]
        if self.left:
            self.next()

    def split(self, order):
        while self.left:
            self.step(order)
        self.step(order)
        value = self.value.reshape(-1)
        return [value[k : k + self.size] for k in range(0, value.size, self.size)]


def qkv_body(*refs):
    chunk, rows, wq, wk, wv, cos, sin = refs[:7]
    q_out, k_out, v_out, rows_out = refs[-4:]
    x = rows[...]
    cosine, sine = cos[...], sin[...]

    def turned(pre):
        out = []
        for h in range(pre.shape[1] // HD):
            one = pre[:, h * HD : (h + 1) * HD]
            out.append(one * cosine + pltpu.roll(one, HD // 2, 1) * sine)
        return jnp.concatenate(out, axis=1)

    q_out[...] = turned(dot(x, wq[...])).astype(BF)
    k_out[...] = turned(dot(x, wk[...])).astype(BF)
    v_out[...] = dot(x, wv[...]).astype(BF)
    part = rows_out.shape[0]
    rows_out[...] = rows[:, pl.ds(pl.multiple_of(pl.program_id(0) * part, part), part)].T


def qkv_slot(order, chunk, rows, w_query, w_key, w_value, cos, sin, held, count):
    t, d = rows.shape
    width = w_query.shape[1]
    bn = min(256, width)
    wspec = pl.BlockSpec((d, bn), lambda i, s: (0, i))
    tspec = pl.BlockSpec((t, HD), lambda i, s: (s[0], 0))
    return call(
        qkv_body,
        name="qkv",
        grid=(width // bn,),
        scalars=1,
        in_specs=[pl.BlockSpec((t, d), lambda i, s: (0, 0)), wspec, wspec, wspec, tspec, tspec]
        + [ANY] * len(held),
        out_specs=[pl.BlockSpec((t, bn), lambda i, s: (s[0], i))] * 3
        + [pl.BlockSpec((d // (width // bn), t), lambda i, s: (i, s[0]))],
        out_shape=[jax.ShapeDtypeStruct((count * t, width), BF)] * 3
        + [jax.ShapeDtypeStruct((d, count * t), BF)],
        aliases={7 + i: i for i in range(len(held))},
    )(order, chunk, rows, w_query, w_key, w_value, cos, sin, *held)


def attend_consts(seq_len):
    to_log2 = math.log2(math.e)
    return (to_log2 / math.sqrt(HD), math.log2(seq_len))


def attend_body(docs, q_ref, k_ref, v_ref, ids_col, ids_row, mix, acc, *, block):
    seq_len = q_ref.shape[0]
    scale, shift = attend_consts(seq_len)
    causal = lax.broadcasted_iota(jnp.int32, (block, block), 0) >= lax.broadcasted_iota(
        jnp.int32, (block, block), 1
    )

    def term(i, j):
        q = q_ref[i * block : (i + 1) * block, :]
        k = k_ref[j * block : (j + 1) * block, :]
        sig = 1.0 / (1.0 + jnp.exp2(shift - dot_nt(q, k) * scale))
        same = ids_col[i * block : (i + 1) * block, :] == ids_row[:, j * block : (j + 1) * block]
        allowed = same & causal if i == j else same
        probs = jnp.where(allowed, sig, 0.0).astype(BF)
        return dot(probs, v_ref[j * block : (j + 1) * block, :])

    for i in range(seq_len // block):
        acc[...] = term(i, i)
        for j in range(i):

            @pl.when(docs[(j + 1) * block - 1] == docs[i * block])
            def _():
                acc[...] += term(i, j)

        mix[i * block : (i + 1) * block, :] = acc[...].astype(BF)


def attend(order, docs, q, k, v):
    seq_len, width = q.shape
    block = 256
    head = pl.BlockSpec((seq_len, HD), lambda h, s: (0, h))
    return call(
        functools.partial(attend_body, block=block),
        name="attend",
        grid=(width // HD,),
        scalars=1,
        in_specs=[
            head,
            head,
            head,
            pl.BlockSpec((seq_len, 1), lambda h, s: (0, 0)),
            pl.BlockSpec((1, seq_len), lambda h, s: (0, 0)),
        ],
        out_specs=[head],
        out_shape=[jax.ShapeDtypeStruct((seq_len, width), BF)],
        scratch=[pltpu.VMEM((block, HD), F32)],
    )(order, docs, q, k, v, docs.reshape(-1, 1), docs.reshape(1, -1))


def attend_back_body(
    docs, q_ref, k_ref, v_ref, dmix, ids_col, ids_row, cos, sin, out, dq, dk, dv, *, block
):
    seq_len = q_ref.shape[0]
    scale, shift = attend_consts(seq_len)
    causal = lax.broadcasted_iota(jnp.int32, (block, block), 0) <= lax.broadcasted_iota(
        jnp.int32, (block, block), 1
    )

    def at(i):
        return slice(i * block, (i + 1) * block)

    def term(i, j):
        q, k, v, d = q_ref[at(i), :], k_ref[at(j), :], v_ref[at(j), :], dmix[at(i), :]
        sig = 1.0 / (1.0 + jnp.exp2(shift - dot_nt(k, q) * scale))
        same = ids_col[at(j), :] == ids_row[:, at(i)]
        allowed = same & causal if i == j else same
        probs = jnp.where(allowed, sig, 0.0)
        d_scores = (dot_nt(v, d) * probs * (1.0 - probs)).astype(BF)
        return dot_tn(d_scores, k), dot(d_scores, q), dot(probs.astype(BF), d)

    for i in range(seq_len // block):
        dq[at(i), :], dk[at(i), :], dv[at(i), :] = term(i, i)
    for i in range(seq_len // block):
        for j in range(i):

            @pl.when(docs[(j + 1) * block - 1] == docs[i * block])
            def _():
                a, b, c = term(i, j)
                dq[at(i), :] += a
                dk[at(j), :] += b
                dv[at(j), :] += c

    cosine, sine = cos[...], sin[...]

    def turned_back(v):
        v = v * (1.0 / math.sqrt(HD))
        return (v * cosine - pltpu.roll(v, HD // 2, 1) * sine).astype(BF)

    width = out.shape[1] // 3
    at_head = pl.program_id(0) * HD
    for part, value in enumerate((turned_back(dq[...]), turned_back(dk[...]), dv[...].astype(BF))):
        out[:, pl.ds(pl.multiple_of(at_head + part * width, HD), HD)] = value


def attend_back(order, docs, q, k, v, d_mix, cos, sin):
    seq_len, width = q.shape
    head = pl.BlockSpec((seq_len, HD), lambda h, s: (0, h))
    whole = lambda r, c: pl.BlockSpec((r, c), lambda h, s: (0, 0))
    return call(
        functools.partial(attend_back_body, block=256),
        name="attend_back",
        grid=(width // HD,),
        scalars=1,
        in_specs=[head] * 4
        + [whole(seq_len, 1), whole(1, seq_len), whole(seq_len, HD), whole(seq_len, HD)],
        out_specs=[whole(seq_len, 3 * width)],
        out_shape=[jax.ShapeDtypeStruct((seq_len, 3 * width), BF)],
        scratch=[pltpu.VMEM((seq_len, HD), F32)] * 3,
    )(order, docs, q, k, v, d_mix, docs.reshape(-1, 1), docs.reshape(1, -1), cos, sin)


def project_body(mix, w_ref, x_ref, gain, resid, normed, acc):
    parts, _, cols = w_ref.shape
    step = pl.program_id(0)

    @pl.when(step == 0)
    def _():
        acc[...] = x_ref[...].astype(F32)

    for p in range(parts):
        acc[:, p * cols : (p + 1) * cols] += dot(mix[...], w_ref[p])

    @pl.when(step == pl.num_programs(0) - 1)
    def _():
        resid[...] = acc[...]
        normed[...] = rms_scale(acc[...], gain[...]).astype(BF)


def project(order, mix, w_out, x, gain):
    t, d = x.shape
    width = mix.shape[1]
    parts, _, cols = w_out.shape
    whole = lambda r, c: pl.BlockSpec((r, c), lambda i: (0, 0))
    return call(
        project_body,
        name="project",
        grid=(mix.shape[0] // t,),
        scalars=0,
        in_specs=[
            pl.BlockSpec((t, width), lambda i: (i, 0)),
            pl.BlockSpec((parts, width, cols), lambda i: (0, i, 0)),
            whole(t, d),
            whole(1, d),
        ],
        out_specs=[whole(t, d)] * 2,
        out_shape=[jax.ShapeDtypeStruct((t, d), F32), jax.ShapeDtypeStruct((t, d), BF)],
        scratch=[pltpu.VMEM((t, d), F32)],
    )(order, mix, w_out, x, gain.reshape(1, -1))


def norm_back(d_normed, rows, gain):
    r = lax.rsqrt(jnp.mean(rows * rows, axis=-1, keepdims=True) + EPS)
    u = rows * r
    scaled = d_normed * gain
    d_rows = r * (scaled - u * jnp.mean(scaled * u, axis=-1, keepdims=True))
    return d_rows, jnp.sum(d_normed * u, axis=0, keepdims=True)


def middle_body(d_ref, resid, cot, gain, w_ref, out, d_resid, low_t, part, low):
    parts, _, cols = w_ref.shape

    @pl.when(pl.program_id(0) == 0)
    def _():
        d_rows, part[...] = norm_back(d_ref[...].astype(F32), resid[...], gain[...])
        total = cot[...].astype(F32) + d_rows
        d_resid[...] = total
        low[...] = total.astype(BF)
        low_t[...] = low[...].T

    total = None
    for p in range(parts):
        term = dot_nt(low[:, p * cols : (p + 1) * cols], w_ref[p])
        total = term if total is None else total + term
    out[...] = total.astype(BF)


def middle(order, d_normed2, resid, cot, gain, w_out, width):
    t, d = resid.shape
    parts, rows, cols = w_out.shape
    count = rows // width
    whole = lambda r, c: pl.BlockSpec((r, c), lambda i: (0, 0))
    return call(
        middle_body,
        name="middle",
        grid=(count,),
        scalars=0,
        in_specs=[whole(t, d)] * 3
        + [whole(1, d), pl.BlockSpec((parts, width, cols), lambda i: (0, i, 0))],
        out_specs=[
            pl.BlockSpec((t, width), lambda i: (i, 0)),
            whole(t, d),
            whole(d, t),
            whole(1, d),
        ],
        out_shape=[
            jax.ShapeDtypeStruct((count * t, width), BF),
            jax.ShapeDtypeStruct((t, d), F32),
            jax.ShapeDtypeStruct((d, t), BF),
            jax.ShapeDtypeStruct((1, d), F32),
        ],
        scratch=[pltpu.VMEM((t, d), BF)],
    )(order, d_normed2, resid, cot, gain.reshape(1, -1), w_out)


def last_body(d_ref, x_ref, d_resid, gain, out, part):
    d_rows, part[...] = norm_back(d_ref[...].astype(F32), x_ref[...].astype(F32), gain[...])
    out[...] = (d_resid[...] + d_rows).astype(BF)


def last(order, d_normed, x, d_resid, gain):
    t, d = x.shape
    whole = lambda r, c: pl.BlockSpec((r, c), lambda i: (0, 0))
    return call(
        last_body,
        name="last",
        grid=(1,),
        scalars=0,
        in_specs=[whole(t, d)] * 3 + [whole(1, d)],
        out_specs=[whole(t, d), whole(1, d)],
        out_shape=[jax.ShapeDtypeStruct((t, d), BF), jax.ShapeDtypeStruct((1, d), F32)],
    )(order, d_normed, x, d_resid, gain.reshape(1, -1))


def back_project_body(d_ref, wq, wk, wv, out):
    total = None
    width = wq.shape[1]
    for k, w in enumerate((wq, wk, wv)):
        term = dot_nt(d_ref[:, k * width : (k + 1) * width], w[...])
        total = term if total is None else total + term
    out[...] = total.astype(BF)


def back_project(order, d_qkv, w_query, w_key, w_value):
    seq_len, wide = d_qkv.shape
    d, width = w_query.shape
    bn = 512
    wspec = pl.BlockSpec((bn, width), lambda i: (i, 0))
    return call(
        back_project_body,
        name="back_project",
        grid=(d // bn,),
        scalars=0,
        in_specs=[pl.BlockSpec((seq_len, wide), lambda i: (0, 0)), wspec, wspec, wspec],
        out_specs=[pl.BlockSpec((seq_len, bn), lambda i: (0, i))],
        out_shape=[jax.ShapeDtypeStruct((seq_len, d), BF)],
    )(order, d_qkv, w_query, w_key, w_value)[0]


def ffn_body(*refs):
    chunk, rows, cot, wg, wu, wd = refs[:6]
    inner, d_gate, d_up, rows_out, cot_out, d_rows, down, acc_d, acc_o = refs[-9:]
    step, last = pl.program_id(0), pl.num_programs(0) - 1
    x = rows[...]
    gate = dot(x, wg[...])
    up = dot(x, wu[...])
    sig = sigmoid(gate)
    silu = gate * sig
    inner_b = (silu * up).astype(BF)
    inner[...] = inner_b.T
    part = rows_out.shape[0]
    rows_out[...] = rows[:, pl.ds(pl.multiple_of(step * part, part), part)].T
    d_inner = dot_nt(cot[...], wd[...])
    dg = (d_inner * up * (sig * (1.0 + gate * (1.0 - sig)))).astype(BF)
    du = (d_inner * silu).astype(BF)
    d_gate[...] = dg
    d_up[...] = du
    term_o = dot(inner_b, wd[...])
    term_d = dot_nt(dg, wg[...]) + dot_nt(du, wu[...])

    @pl.when(step == 0)
    def _():
        acc_o[...] = term_o
        acc_d[...] = term_d
        cot_out[...] = cot[...]

    @pl.when(step > 0)
    def _():
        acc_o[...] += term_o
        acc_d[...] += term_d

    @pl.when(step == last)
    def _():
        d_rows[...] = acc_d[...].astype(BF)
        down[...] = acc_o[...].astype(BF)


def ffn_slot(order, chunk, rows, cot, w_gate, w_up, w_down, held, count):
    t, d = rows.shape
    hidden = w_gate.shape[1]
    bh = min(512, hidden)
    steps = hidden // bh
    wcol = pl.BlockSpec((d, bh), lambda i, s: (0, i))
    part = pl.BlockSpec((t, bh), lambda i, s: (s[0], i))
    line = pl.BlockSpec((t, d), lambda i, s: (s[0], 0))
    return call(
        ffn_body,
        name="ffn",
        grid=(hidden // bh,),
        scalars=1,
        in_specs=[
            pl.BlockSpec((t, d), lambda i, s: (0, 0)),
            pl.BlockSpec((t, d), lambda i, s: (0, 0)),
            wcol,
            wcol,
            pl.BlockSpec((bh, d), lambda i, s: (i, 0)),
        ]
        + [ANY] * len(held),
        out_specs=[pl.BlockSpec((bh, t), lambda i, s: (i, s[0])), part, part]
        + [pl.BlockSpec((d // steps, t), lambda i, s: (i, s[0])), line, line, line],
        out_shape=[jax.ShapeDtypeStruct((hidden, count * t), BF)]
        + [jax.ShapeDtypeStruct((count * t, hidden), BF)] * 2
        + [jax.ShapeDtypeStruct((d, count * t), BF)]
        + [jax.ShapeDtypeStruct((count * t, d), BF)] * 3,
        scratch=[pltpu.VMEM((t, d), F32)] * 2,
        aliases={6 + i: i for i in range(len(held))},
    )(order, chunk, rows, cot, w_gate, w_up, w_down, *held)


def local(
    layer_in,
    cotangent,
    doc_ids,
    positions,
    attn_gain,
    w_query,
    w_key,
    w_value,
    w_out,
    ffn_gain,
    w_gate,
    w_up,
    w_down,
    *,
    dp,
    tensor,
):
    t, d = layer_in.shape
    width = w_query.shape[1]
    hidden = w_gate.shape[1]
    place = lax.axis_index("tensor")
    chunks = jnp.stack([place ^ j for j in range(tensor)]).astype(jnp.int32)
    chunk = [chunks[j : j + 1] for j in range(tensor)]
    order = Order()

    share = w_out.shape[1] // dp
    w_cols = lax.all_gather(
        cols_at(w_out, lax.axis_index("dp"), share), "tensor", axis=0, tiled=True
    )
    half = HD // 2
    freqs = ROPE_BASE ** (-(jnp.arange(half).astype(F32) * 2.0) / HD)
    angles = positions.astype(F32)[:, None] * freqs[None, :]
    cosine, sine = jnp.cos(angles), jnp.sin(angles)
    cos = jnp.concatenate([cosine, cosine], axis=1)
    sin = jnp.concatenate([-sine, sine], axis=1)

    normed_own = rms_scale(layer_in.astype(F32), attn_gain).astype(BF)
    line = LineGather(normed_own, tensor, place)
    line.step()
    held = []
    for j in range(tensor):
        if 0 < j < tensor - 1:
            line.step(order)
        if j == tensor - 1:
            cots = LineGather(cotangent, tensor, place)
            cots.step(order)
        usual, order.worth = order.worth, 20 if j == tensor - 1 else order.worth
        held = qkv_slot(order, chunk[j], line.slot(j), w_query, w_key, w_value, cos, sin, held, tensor)
        order.worth = usual
        if j == min(2, tensor - 1):
            (w_cols,) = order.after(w_cols)
            w_out_all = lax.all_gather(w_cols, "dp", axis=0)
    query, key, value, normed_t = held
    (mixed,) = attend(order, doc_ids, query, key, value)
    mix = exchange(mixed)
    cots.step(order)
    (cot_first,) = order.after(cots.slot(1))
    resid, normed2_own = project(order, mix, w_out_all, layer_in, ffn_gain)

    weights = (w_gate, w_up, w_down)
    line = LineGather(normed2_own, tensor, place)
    line.step()
    held = ffn_slot(order, chunk[0], line.slot(0), cotangent, *weights, [], tensor)
    for j in range(1, tensor):
        if j < tensor - 1:
            line.step(order)
            if len(cots.ups) < tensor:
                cots.step(order)
        else:
            cots.hold(order)
            line.hold(order)
        cot = cot_first if j == 1 else cots.slot(j)
        held = ffn_slot(order, chunk[j], line.slot(j), cot, *weights, held, tensor)
    inner_t, d_gate, d_up, normed2_t, cot_all, d_normed2_part, down_part = held
    d_normed2 = lax.psum_scatter(d_normed2_part, "tensor", scatter_dimension=0, tiled=True)

    first = Gradients([(inner_t, cot_all, [d])], dp)
    wide = Gradients([(normed2_t, d_gate, [hidden]), (normed2_t, d_up, [hidden])], dp)
    more = range(first.bits - 2)

    first.give(order)
    wide.give(order, 0)
    wide.give(order, 1)
    first.keep(order)
    wide.keep(order, 0)
    wide.keep(order, 1)
    usual = order.worth
    first.fold(order)
    d_mix, d_resid, d_resid_t, ffn_gain_part = middle(
        order, d_normed2, resid, cotangent, ffn_gain, w_out_all, width
    )
    d_mix = exchange(d_mix)
    d_resid_all = lax.all_gather(d_resid_t, "tensor", axis=0)
    for _ in more:
        first.fold(order)
    wide.fold(order)
    for _ in more:
        first.spread(order)
    order.worth = 1.3
    (d_qkv,) = attend_back(order, doc_ids, query, key, value, d_mix, cos, sin)
    order.worth = usual
    attn = Gradients([(normed_t, d_qkv, [width] * 4, d_resid_all, mixed)], dp)
    attn.give(order)
    for _ in more:
        wide.fold(order)
    first.join(order)
    attn.give(order, second=True)
    d_normed = lax.psum_scatter(
        back_project(order, d_qkv, w_query, w_key, w_value),
        "tensor",
        scatter_dimension=0,
        tiled=True,
    )
    attn.keep(order)
    wide.hold(order)
    usual, order.worth = order.worth, 10
    attn.fold(order)
    order.worth = usual
    down_sum = lax.psum_scatter(
        order.after(down_part)[0], "tensor", scatter_dimension=0, tiled=True
    )
    for _ in more:
        wide.spread(order)
    for _ in more:
        attn.fold(order)
    (down_grad,) = first.finish(order)
    in_grad, attn_gain_part = last(order, d_normed, layer_in, d_resid, attn_gain)
    totals = GainTotals([attn_gain_part, ffn_gain_part], dp, tensor)
    totals.step(order)
    totals.step(order)
    totals.step(order)
    wide.hold(order)
    order.worth = 0.3
    wide.join(order)
    attn.hold(order)
    order.worth = 0.3
    for _ in more:
        attn.spread(order)
    order.worth = 0.3
    order.worth = 4
    gate_grad = wide.fill(order, 0, 0)
    up_grad = wide.fill(order, 1, 0)
    order.worth = 0.02
    (gate_grad,) = wide.fill(order, 0, 1, gate_grad)
    attn.join(order)
    (up_grad,) = wide.fill(order, 1, 1, up_grad)
    attn_grads = attn.fill(order, 0, 0)
    totals.step(order)
    (down_sum,) = order.after(down_sum)
    query_grad, key_grad, value_grad, out_grad = attn.fill(order, 0, 1, attn_grads)
    attn_gain_grad, ffn_gain_grad = totals.split(order)
    layer_out = (resid + down_sum.astype(F32)).astype(BF)
    return (
        layer_out,
        in_grad,
        attn_gain_grad,
        query_grad,
        key_grad,
        value_grad,
        out_grad,
        ffn_gain_grad,
        gate_grad,
        up_grad,
        down_grad,
    )


def solution(mesh):
    rows, cols, lines = P(("dp", "tensor"), None), P(None, "tensor"), P("tensor", None)
    return jax.shard_map(
        functools.partial(local, dp=mesh.shape["dp"], tensor=mesh.shape["tensor"]),
        mesh=mesh,
        in_specs=(
            rows, rows, P("dp"), P("dp"), P(), cols, cols, cols, lines, P(), cols, cols, lines
        ),
        out_specs=(rows, rows, P(), cols, cols, cols, lines, P(), cols, cols, lines),
        check_vma=False,
    )
```
